32 devices in a mesh: groups: 2 (over y), tile: 4 (over z), image: 4 (over x, core).
Axes of the slice: x: 2, y: 2, z: 4, core: 2. Of those that a mesh axis runs over, the one named last changes fastest.
Arguments:
- images: bfloat16 [8, 16, 64, 256], P(('groups', 'image'), 'tile'), parts along dimension 0, may hold values from -12 to 12
- cotangent: bfloat16 [8, 16, 64, 256], P(('groups', 'image'), 'tile'), parts along dimension 0, may hold values from -12 to 12
- timesteps: int32 [8], P(('groups', 'image')), parts along dimension 0, may hold values from 0 to 999
- class_ids: int32 [8], P(('groups', 'image')), parts along dimension 0, may hold values from 0 to 999
- norm_gain: float32 [256], replicated, may hold values from 0.25 to 1.75
- norm_bias: float32 [256], replicated, may hold values from -3 to 3
- conv_first: bfloat16 [3, 3, 256, 256], replicated, may hold values from -0.125 to 0.125
- conv_second: bfloat16 [3, 3, 256, 256], replicated, may hold values from -0.125 to 0.125
- time_weight: bfloat16 [256, 1024], P(None, 'tile'), may hold values from -0.375 to 0.375
- time_bias: float32 [1024], P('tile'), may hold values from -3 to 3
- class_table: bfloat16 [1000, 1024], P(None, 'tile'), may hold values from -5 to 5
- adaptive_weight: bfloat16 [1024, 512], P('tile'), may hold values from -0.1875 to 0.1875
- adaptive_bias: float32 [512], replicated, may hold values from -2 to 2
Outputs:
- branch: bfloat16 [8, 16, 64, 256], P(('groups', 'image'), 'tile'), parts along dimension 0
- input_grad: bfloat16 [8, 16, 64, 256], P(('groups', 'image'), 'tile'), parts along dimension 0
- grad_adaptive_weight: float32 [2048, 512], P(('groups', 'tile')), parts along dimension 0
- grad_adaptive_bias: float32 [1024], P('groups'), parts along dimension 0
The draws below stay inside these ranges and needn't reach their ends.
There are 2 independent parts, one for each index of `groups`. The reference program is written for one: setup_inputs(seed, part) draws one part's arguments, and reference() takes and returns one part's arrays. A program takes and returns all parts, laid end to end along the dimension named above; an argument that names none is the same for every part. Nothing has to cross between parts.
All inputs are finite; a program needn't handle non-finite values.
Results may differ from the reference program's by a relative error of at most 0.013.
Values may be sent and summed in bfloat16 or wider, within the bound.
No kernel may reach another device: no remote copies, remote signals or barrier semaphores. Data moves between devices by JAX's collectives and lax.ppermute only.
A program may use at most 64 MiB of HBM per device.

```python
import math
import jax
import jax.numpy as jnp
from jax import lax

C = 256
EMB = 1024
FREQ = 256
CLASSES = 1000
GN_GROUPS = 32
COLS = 64
IMAGES = 4
H = 16


def scaled_field(key, offset_tag):
    folded = jax.random.fold_in(key, offset_tag)
    sample_key, row_key, chan_key = jax.random.split(folded, 3)
    extent = (IMAGES, H, COLS, C)
    sample = jnp.clip(jax.random.normal(sample_key, extent, jnp.float32), -4.0, 4.0)
    rising = 3.0 ** (jnp.arange(H, dtype=jnp.float32) / (H - 1))
    row_scale = rising[None, :] * jnp.exp(jax.random.uniform(row_key, (IMAGES, H), jnp.float32, 0.0, math.log(3.3))) / math.sqrt(10.0)
    chan_scale = jnp.exp(jax.random.uniform(chan_key, (IMAGES, C), jnp.float32, math.log(0.316), math.log(3.16)))
    return jnp.clip(sample * row_scale[:, :, None, None] * chan_scale[:, None, None, :], -12.0, 12.0)


def draw_images(key, part):
    return scaled_field(key, 11).astype(jnp.bfloat16)


def draw_cotangent(key, part):
    return scaled_field(key, 23).astype(jnp.bfloat16)


def with_ends(result, stream_key, smallest, top_value):
    spot = [jax.random.randint(jax.random.fold_in(stream_key, axis), (), 0, length) for axis, length in enumerate(result.shape)]
    main_axis = result.shape.index(max(result.shape))
    next_to = spot[:main_axis] + [(spot[main_axis] + 1) % result.shape[main_axis]] + spot[main_axis + 1:]
    return result.at[tuple(spot)].set(smallest).at[tuple(next_to)].set(top_value)


def steps_of(key, dims, cuts, least, top_value):
    def one(position, shards_of):
        heights = jax.random.uniform(jax.random.fold_in(jax.random.fold_in(key, 6), position), (shards_of,), jnp.float32, least / len(cuts), top_value / len(cuts))
        return jnp.repeat(jnp.exp(heights), dims[position] // shards_of).reshape((-1,) + (1,) * (len(dims) - position - 1))

    level = one(*cuts[0])
    for cut in cuts[1:]:
        level = level * one(*cut)
    return level


def gaussian(key, shape, width, bound, pieces=(), kind=jnp.bfloat16):
    entries = width * jax.random.normal(key, shape, jnp.float32)
    if pieces:
        entries = entries * steps_of(key, shape, pieces, -0.22, 0.18)
    return jnp.clip(entries, -bound, bound).astype(kind)


def setup_inputs(seed: int = 0, part: int = 0) -> dict:
    seeds = jax.random.split(jax.random.key(seed), 14)
    part_keys = jax.random.split(jax.random.fold_in(seeds[13], part), 14)
    images = draw_images(jax.random.fold_in(jax.random.fold_in(seeds[13], part), 71), part)
    cotangent = draw_cotangent(jax.random.fold_in(jax.random.fold_in(seeds[13], part), 71), part)
    timesteps = with_ends(jax.random.randint(part_keys[2], (IMAGES,), 0, 1000), jax.random.fold_in(part_keys[2], 1), 0, 999).astype(jnp.int32)
    class_ids = with_ends(jax.random.randint(part_keys[3], (IMAGES,), 0, CLASSES), jax.random.fold_in(part_keys[3], 1), 0, CLASSES - 1).astype(jnp.int32)
    norm_gain = jnp.clip(1.0 + 0.15 * jax.random.normal(seeds[4], (C,), jnp.float32), 0.25, 1.75)
    norm_bias = gaussian(seeds[5], (C,), 0.5, 3.0, (), jnp.float32)
    conv_first = gaussian(seeds[6], (3, 3, C, C), (9 * C) ** -0.5, 0.125)
    conv_second = gaussian(seeds[7], (3, 3, C, C), (9 * C) ** -0.5, 0.125)
    time_weight = gaussian(seeds[8], (FREQ, EMB), FREQ ** -0.5, 0.375, ((1, 4),))
    time_bias = gaussian(seeds[9], (EMB,), 0.5, 3.0, ((0, 4),), jnp.float32)
    class_table = gaussian(seeds[10], (CLASSES, EMB), 1.0, 5.0, ((1, 4),))
    adaptive_weight = gaussian(seeds[11], (EMB, 2 * C), EMB ** -0.5, 0.1875, ((0, 4),))
    adaptive_bias = gaussian(seeds[12], (2 * C,), 0.3, 2.0, (), jnp.float32)
    return {"images": images, "cotangent": cotangent, "timesteps": timesteps, "class_ids": class_ids, "norm_gain": norm_gain, "norm_bias": norm_bias, "conv_first": conv_first, "conv_second": conv_second, "time_weight": time_weight, "time_bias": time_bias, "class_table": class_table, "adaptive_weight": adaptive_weight, "adaptive_bias": adaptive_bias}


EPSILON = 1e-05

def rounded(values):
    return lax.optimization_barrier(values.astype(jnp.bfloat16)).astype(jnp.float32)

def conv_same(values, kernel):
    return lax.conv_general_dilated(values[None], kernel.astype(jnp.float32), (1, 1), 'SAME', dimension_numbers=('NHWC', 'HWIO', 'NHWC'), precision=lax.Precision.HIGHEST)[0]

def group_mean(values):
    per_group = values.reshape(-1, GN_GROUPS, C // GN_GROUPS).mean(axis=(0, 2))
    return jnp.repeat(per_group, C // GN_GROUPS)

def normalize(values):
    centred = values - group_mean(values)
    inverse = lax.rsqrt(group_mean(centred * centred) + EPSILON)
    return (centred * inverse, inverse)

def norm_backward(grad_norm, normed, inverse):
    return inverse * (grad_norm - group_mean(grad_norm) - normed * group_mean(grad_norm * normed))

def silu_grad(pre_values):
    sigma = jax.nn.sigmoid(pre_values)
    return sigma * (1.0 + pre_values * (1.0 - sigma))

def reference(images, cotangent, timesteps, class_ids, norm_gain, norm_bias, conv_first, conv_second, time_weight, time_bias, class_table, adaptive_weight, adaptive_bias):
    half_freq = FREQ // 2
    frequencies = jnp.exp(-math.log(10000.0) * jnp.arange(half_freq, dtype=jnp.float32) / half_freq)
    angles = timesteps.astype(jnp.float32)[:, None] * frequencies[None]
    sinusoid = jnp.concatenate([jnp.cos(angles), jnp.sin(angles)], axis=1)
    hidden = jnp.dot(sinusoid, time_weight.astype(jnp.float32), precision=lax.Precision.HIGHEST) + time_bias.astype(jnp.float32)
    onehot = (class_ids[:, None] == jnp.arange(CLASSES, dtype=jnp.int32)[None]).astype(jnp.float32)
    embedding = jax.nn.silu(hidden) + jnp.dot(onehot, class_table.astype(jnp.float32), precision=lax.Precision.HIGHEST)
    activated = jax.nn.silu(embedding)
    modulation = jnp.dot(activated, adaptive_weight.astype(jnp.float32), precision=lax.Precision.HIGHEST) + adaptive_bias.astype(jnp.float32)
    flipped_first = jnp.flip(conv_first, (0, 1)).transpose(0, 1, 3, 2)
    flipped_second = jnp.flip(conv_second, (0, 1)).transpose(0, 1, 3, 2)
    gain = norm_gain.astype(jnp.float32)
    bias_term = norm_bias.astype(jnp.float32)

    def one_image(inputs):
        picture, grad_out, modul_row = inputs
        normed_first, inverse_first = normalize(picture.astype(jnp.float32))
        pre_first = normed_first * gain + bias_term
        active_first = rounded(jax.nn.silu(pre_first))
        hidden_first = rounded(conv_same(active_first, conv_first))
        normed_second, inverse_second = normalize(hidden_first)
        factor = 1.0 + modul_row[:C]
        pre_second = normed_second * factor + modul_row[C:]
        active_second = rounded(jax.nn.silu(pre_second))
        branch = conv_same(active_second, conv_second).astype(jnp.bfloat16)
        grad_active = conv_same(grad_out.astype(jnp.float32), flipped_second)
        grad_pre = grad_active * silu_grad(pre_second)
        grad_scale = lax.optimization_barrier(jnp.sum(grad_pre * normed_second, axis=(0, 1)))
        grad_shift = lax.optimization_barrier(jnp.sum(grad_pre, axis=(0, 1)))
        grad_hidden = rounded(norm_backward(grad_pre * factor, normed_second, inverse_second))
        grad_active_first = conv_same(grad_hidden, flipped_first)
        grad_first = grad_active_first * silu_grad(pre_first) * gain
        input_grad = norm_backward(grad_first, normed_first, inverse_first).astype(jnp.bfloat16)
        return (branch, input_grad, jnp.concatenate([grad_scale, grad_shift]))
    branch, input_grad, pairs = lax.map(one_image, (images, cotangent, modulation))
    grad_weight = jnp.dot(activated.T, pairs, precision=lax.Precision.HIGHEST)
    grad_bias = lax.optimization_barrier(jnp.sum(pairs, axis=0))
    return (branch, input_grad, grad_weight, grad_bias)
```

```python
import functools
import math

import jax
import jax.numpy as jnp
from jax import lax
from jax.experimental import pallas as pl
from jax.experimental.pallas import tpu as pltpu
from jax.sharding import PartitionSpec as P

GN_GROUPS = 32
EPSILON = 1e-05
VMEM_LIMIT = 12 * 1024 * 1024
F32, BF16 = jnp.float32, jnp.bfloat16

STAT_ROWS = 32


def terms(values):
    high = values.astype(BF16).astype(F32)
    rest = values - high
    middle = rest.astype(BF16).astype(F32)
    low = (rest - middle).astype(BF16).astype(F32)
    return jnp.concatenate([high, middle, low, jnp.zeros_like(high)], axis=0).astype(BF16)


def joined(block):
    wide = block.astype(F32)
    return wide[0:8] + (wide[8:16] + wide[16:24])


def rows8(*rows):
    width = rows[0].shape[1]
    index = lax.broadcasted_iota(jnp.int32, (8, width), 0)
    out = jnp.zeros((8, width), F32)
    for place, row in enumerate(rows):
        out = jnp.where(index == place, jnp.broadcast_to(row, (8, width)), out)
    return out


def group_matrix(channels):
    shift = (channels // GN_GROUPS).bit_length() - 1
    row = lax.shift_right_logical(lax.broadcasted_iota(jnp.int32, (channels, channels), 0), shift)
    col = lax.shift_right_logical(lax.broadcasted_iota(jnp.int32, (channels, channels), 1), shift)
    return (row == col).astype(F32).astype(BF16)


def group_sums(rows, groups):
    out = jnp.dot(terms(rows), groups, preferred_element_type=F32)
    return out[0:8] + (out[8:16] + out[16:24])


def tree_sum(parts):
    parts = list(parts)
    while len(parts) > 1:
        parts = [
            parts[i] + parts[i + 1] if i + 1 < len(parts) else parts[i]
            for i in range(0, len(parts), 2)
        ]
    return parts[0]


def local_moments(values, groups, count):
    mean = group_sums(rows8(jnp.sum(values, axis=0, keepdims=True)), groups)[0:1] / count
    centred = values - mean
    spread = group_sums(rows8(jnp.sum(centred * centred, axis=0, keepdims=True)), groups)[0:1]
    return mean, spread


def joint_moments(stats, count):
    tiles = len(stats)
    mean = tree_sum([s[0:1] for s in stats]) / tiles
    spread = tree_sum([s[1:2] + count * (s[0:1] - mean) * (s[0:1] - mean) for s in stats])
    return mean, lax.rsqrt(spread / (count * tiles) + EPSILON)


def sigmoid(values):
    return 1.0 / (1.0 + jnp.exp(-values))


def column_index(cells, cols, channels):
    index = lax.broadcasted_iota(jnp.int32, (cells, channels), 0)
    return lax.bitwise_and(index, cols - 1)


def conv(padded_ref, kernel_ref, cells, cols, flipped):
    parts = []
    for j in range(3):
        total = None
        for i in range(3):
            rows = padded_ref[(2 - i if flipped else i) * cols : (2 - i if flipped else i) * cols + cells]
            weights = kernel_ref[3 * i + j]
            product = lax.dot_general(
                rows,
                weights,
                (((1,), (1 if flipped else 0,)), ((), ())),
                preferred_element_type=F32,
            )
            total = product if total is None else total + product
        parts.append(total)
    if flipped:
        parts = parts[::-1]
    column = column_index(cells, cols, parts[0].shape[1])
    left = jnp.where(column == 0, 0.0, pltpu.roll(parts[0], 1, 0))
    right = jnp.where(column == cols - 1, 0.0, pltpu.roll(parts[2], cells - 1, 0))
    return parts[1] + (left + right)


def stat_list(refs, start, tiles):
    if len(refs) == 1:
        return [joined(refs[0][STAT_ROWS * t : STAT_ROWS * (t + 1)]) for t in range(tiles)]
    return [joined(ref[s : s + STAT_ROWS]) for ref, s in zip(refs, start, strict=True)]


def edges(place_ref, one, three):
    odd = place_ref[1] == 1
    return jnp.where(odd, one, three), jnp.where(odd, three, one)


def starts(place_ref, cells, cols):
    odd = place_ref[1]
    first = pl.multiple_of((1 - odd) * (cells - cols), cols)
    third = pl.multiple_of(odd * (cells - cols), cols)
    return first, third


def first_kernel(dims, place, images, cotangent, one, two, three):
    cells, cols, channels, tiles = dims
    start_one, start_three = starts(place, cells, cols)
    one[0:cols] = images[pl.ds(start_one, cols)]
    one[cols : 2 * cols] = cotangent[pl.ds(start_one, cols)]
    three[0:cols] = images[pl.ds(start_three, cols)]
    three[cols : 2 * cols] = cotangent[pl.ds(start_three, cols)]
    groups = group_matrix(channels)
    mean, spread = local_moments(
        images[...].astype(F32), groups, cells * (channels // GN_GROUPS)
    )
    block = terms(rows8(mean, spread))
    one[2 * cols :] = block
    two[...] = block
    three[2 * cols :] = block


def embed_kernel(sinusoid, row, time_weight, time_bias, adaptive_weight, out):
    channels = adaptive_weight.shape[1] // 2

    def times(vector, weights):
        product = jnp.dot(terms(rows8(vector)), weights, preferred_element_type=F32)
        return (product[0:8] + (product[8:16] + product[16:24]))[0:1]

    hidden = times(sinusoid[...], time_weight[...]) + time_bias[...]
    embedding = hidden * sigmoid(hidden) + row[...]
    activated = embedding * sigmoid(embedding)
    partial = times(activated, adaptive_weight[...])
    out[...] = rows8(partial[:, :channels], partial[:, channels:], activated)


def second_kernel(dims, n_stats, place, images, one, three, weights, gain, bias, embed, *rest):
    cells, cols, channels, tiles = dims
    stat_refs, (hidden, stat, out_one, out_two, out_three, padded) = rest[:n_stats], rest[n_stats:]
    count = cells * (channels // GN_GROUPS)
    mean, inverse = joint_moments(
        stat_list(stat_refs, (0, 2 * cols, 0, 2 * cols), tiles), count
    )
    stat[...] = rows8(mean, inverse)
    above, below = edges(place, one[0:cols], three[0:cols])

    def active(block):
        pre = (block.astype(F32) - mean) * inverse * gain[...] + bias[...]
        return pre * sigmoid(pre)

    padded[0:cols] = jnp.where(place[0] > 0, active(above), 0.0).astype(BF16)
    padded[cols : cols + cells] = active(images[...]).astype(BF16)
    padded[cols + cells :] = jnp.where(place[0] < tiles - 1, active(below), 0.0).astype(BF16)
    rounded = conv(padded, weights, cells, cols, False).astype(BF16)
    hidden[...] = rounded
    mean_two, spread_two = local_moments(rounded.astype(F32), group_matrix(channels), count)
    block = terms(rows8(mean_two, spread_two, embed[0:1], embed[1:2]))
    start_one, start_three = starts(place, cells, cols)
    out_one[0:cols] = hidden[pl.ds(start_one, cols)]
    out_three[0:cols] = hidden[pl.ds(start_three, cols)]
    out_one[cols:] = block
    out_two[...] = block
    out_three[cols:] = block


def grad_kernel(dims, place, cotangent, one, three, weights, out, padded):
    cells, cols, channels, tiles = dims
    above, below = edges(place, one[cols : 2 * cols], three[cols : 2 * cols])
    padded[0:cols] = jnp.where(place[0] > 0, above, jnp.zeros_like(above))
    padded[cols : cols + cells] = cotangent[...]
    padded[cols + cells :] = jnp.where(place[0] < tiles - 1, below, jnp.zeros_like(below))
    out[...] = conv(padded, weights, cells, cols, True)


def third_kernel(dims, n_stats, place, hidden, one, three, grad_active, adaptive_bias, *rest):
    cells, cols, channels, tiles = dims
    stat_refs, (active, grad_norm, stat, out_one, out_two, out_three) = rest[:n_stats], rest[n_stats:]
    count = cells * (channels // GN_GROUPS)
    stats = stat_list(stat_refs, (0, cols, 0, cols), tiles)
    mean, inverse = joint_moments(stats, count)
    modulation = tree_sum(stats)
    factor = 1.0 + (modulation[2:3] + adaptive_bias[:, :channels])
    shift = modulation[3:4] + adaptive_bias[:, channels:]
    stat[...] = rows8(mean, inverse, factor)
    above, below = edges(place, one[0:cols], three[0:cols])

    def pieces(block):
        normed = (block.astype(F32) - mean) * inverse
        pre = normed * factor + shift
        return normed, pre, sigmoid(pre)

    _, pre, gate = pieces(above)
    active[0:cols] = jnp.where(place[0] > 0, pre * gate, 0.0).astype(BF16)
    _, pre, gate = pieces(below)
    active[cols + cells :] = jnp.where(place[0] < tiles - 1, pre * gate, 0.0).astype(BF16)
    normed, pre, gate = pieces(hidden[...])
    active[cols : cols + cells] = (pre * gate).astype(BF16)
    grad_pre = grad_active[...] * (gate * (1.0 + pre * (1.0 - gate)))
    grad_norm[...] = grad_pre * factor
    block = terms(
        rows8(
            jnp.sum(grad_pre * normed, axis=0, keepdims=True),
            jnp.sum(grad_pre, axis=0, keepdims=True),
        )
    )
    start_one, start_three = starts(place, cells, cols)
    out_one[0:cols] = grad_norm[pl.ds(start_one, cols)].astype(BF16)
    out_three[0:cols] = grad_norm[pl.ds(start_three, cols)].astype(BF16)
    out_one[cols:] = block
    out_two[...] = block
    out_three[cols:] = block


def branch_kernel(dims, active, weights, out):
    cells, cols, channels, tiles = dims
    out[...] = conv(active, weights, cells, cols, False).astype(BF16)


def fourth_kernel(
    dims, n_stats, place, grad_norm, one, three, hidden, hidden_one, hidden_three, stat_two,
    weights, images, stat_one, gain, bias, embed, *rest
):
    cells, cols, channels, tiles = dims
    stat_refs, (grad_first, out, pairs, padded) = rest[:n_stats], rest[n_stats:]
    total = cells * (channels // GN_GROUPS) * tiles
    sums = tree_sum(stat_list(stat_refs, (0, cols, 0, cols), tiles))
    pairs[...] = rows8(sums[0:1], sums[1:2], embed[2:3])
    mean, inverse, factor = stat_two[0:1], stat_two[1:2], stat_two[2:3]
    groups = group_matrix(channels)
    means = group_sums(sums * factor, groups) / total
    paired, plain = means[0:1], means[1:2]
    above, below = edges(place, one[0:cols], three[0:cols])
    hidden_above, hidden_below = edges(place, hidden_one[0:cols], hidden_three[0:cols])

    def grad_hidden(grad, block):
        normed = (block.astype(F32) - mean) * inverse
        return inverse * (grad.astype(F32) - plain - normed * paired)

    padded[0:cols] = jnp.where(place[0] > 0, grad_hidden(above, hidden_above), 0.0).astype(BF16)
    padded[cols : cols + cells] = grad_hidden(grad_norm[...], hidden[...]).astype(BF16)
    padded[cols + cells :] = jnp.where(
        place[0] < tiles - 1, grad_hidden(below, hidden_below), 0.0
    ).astype(BF16)
    grad_active = conv(padded, weights, cells, cols, True)
    normed = (images[...].astype(F32) - stat_one[0:1]) * stat_one[1:2]
    pre = normed * gain[...] + bias[...]
    gate = sigmoid(pre)
    grad = grad_active * (gate * (1.0 + pre * (1.0 - gate))) * gain[...]
    grad_first[...] = grad
    sums_first = rows8(
        jnp.sum(grad, axis=0, keepdims=True), jnp.sum(grad * normed, axis=0, keepdims=True)
    )
    out[...] = terms(group_sums(sums_first, groups))


def fifth_kernel(dims, n_stats, grad_first, images, stat_one, *rest):
    cells, cols, channels, tiles = dims
    stat_refs, (out,) = rest[:n_stats], rest[n_stats:]
    total = cells * (channels // GN_GROUPS) * tiles
    means = tree_sum(stat_list(stat_refs, (0, 0, 0, 0), tiles)) / total
    inverse = stat_one[1:2]
    normed = (images[...].astype(F32) - stat_one[0:1]) * inverse
    out[...] = (inverse * (grad_first[...] - means[0:1] - normed * means[1:2])).astype(BF16)


def weight_kernel(index, *rest):
    pair_refs, (weight, bias) = rest[:-2], rest[-2:]
    if len(pair_refs) == 1:
        blocks = [pair_refs[0][8 * n : 8 * n + 8] for n in range(pair_refs[0].shape[0] // 8)]
        places = list(range(len(blocks)))
    else:
        blocks = [ref[...] for ref in pair_refs]
        places = [lax.bitwise_xor(index[0], k) for k in range(len(blocks))]
    count = -(-len(blocks) // 8) * 8
    channels = blocks[0].shape[1]
    row = lax.broadcasted_iota(jnp.int32, (count, channels), 0)

    def ordered(which):
        out = jnp.zeros((count, channels), F32)
        for block, place in zip(blocks, places, strict=True):
            out = jnp.where(row == place, jnp.broadcast_to(block[which : which + 1], out.shape), out)
        return out

    scale, shift, activated = ordered(0), ordered(1), ordered(2)
    for start, part in ((0, scale), (channels, shift)):
        weight[:, start : start + channels] = lax.dot_general(
            activated,
            part,
            (((0,), (0,)), ((), ())),
            precision=lax.Precision.HIGHEST,
            preferred_element_type=F32,
        )
        bias[:, start : start + channels] = jnp.sum(part, axis=0, keepdims=True)


def call(kernel, out_shapes, operands, scratch=(), flops=1000, smem=1, name=None):
    size = sum(o.size * o.dtype.itemsize for o in operands)
    return pl.pallas_call(
        kernel,
        out_shape=out_shapes,
        in_specs=[
            pl.BlockSpec(memory_space=pltpu.SMEM if k < smem else pltpu.VMEM)
            for k in range(len(operands))
        ],
        out_specs=jax.tree.map(lambda _: pl.BlockSpec(memory_space=pltpu.VMEM), out_shapes),
        scratch_shapes=list(scratch),
        compiler_params=pltpu.CompilerParams(vmem_limit_bytes=VMEM_LIMIT),
        cost_estimate=pl.CostEstimate(flops=flops, bytes_accessed=size, transcendentals=0),
        name=name,
    )(*operands)


def swap(values, axis, size, distance):
    return lax.ppermute(values, axis, [(i, i ^ distance) for i in range(size)])


def exchange(one, two, three, stat_start):
    tiles = lax.axis_size("tile")
    if tiles == 4:
        got = [swap(part, "tile", tiles, k + 1) for k, part in enumerate((one, two, three))]
        return got[0], got[2], [two, *got]
    ahead = [(i, (i + 1) % tiles) for i in range(tiles)]
    behind = [(target, source) for source, target in ahead]
    below, above = lax.ppermute(three, "tile", behind), lax.ppermute(one, "tile", ahead)
    return below, above, [lax.all_gather(two, "tile", axis=0, tiled=True)]


def spread_small(block):
    tiles = lax.axis_size("tile")
    if tiles == 4:
        return [block, *(swap(block, "tile", tiles, k) for k in (1, 2, 3))]
    return [lax.all_gather(block, "tile", axis=0, tiled=True)]


def body(
    images,
    cotangent,
    timesteps,
    class_ids,
    norm_gain,
    norm_bias,
    conv_first,
    conv_second,
    time_weight,
    time_bias,
    class_table,
    adaptive_weight,
    adaptive_bias,
):
    _, rows, cols, channels = images.shape
    tiles, fleet = lax.axis_size("tile"), lax.axis_size("image")
    cells = rows * cols
    dims = (cells, cols, channels, tiles)
    tile = lax.axis_index("tile").astype(jnp.int32)
    odd = tile % 2 if tiles == 4 else jnp.zeros_like(tile)
    place = jnp.stack([tile, odd])
    flat = images.reshape(cells, channels)
    flat_cot = cotangent.reshape(cells, channels)
    weights_first = conv_first.reshape(9, channels, channels)
    weights_second = conv_second.reshape(9, channels, channels)
    gain, bias = norm_gain[None], norm_bias[None]
    shape = jax.ShapeDtypeStruct
    conv_flops = 18 * cells * channels * channels
    padded = pltpu.VMEM((cells + 2 * cols, channels), BF16)
    small = shape((STAT_ROWS, channels), BF16)
    halo = shape((cols + STAT_ROWS, channels), BF16)
    halos = shape((2 * cols + STAT_ROWS, channels), BF16)
    block = shape((8, channels), F32)
    wide = shape((cells, channels), F32)
    narrow = shape((cells, channels), BF16)

    one, two, three = call(
        functools.partial(first_kernel, dims), (halos, small, halos), (place, flat, flat_cot), name="first"
    )
    image_one, image_three, stats = exchange(one, two, three, 2 * cols)

    half = time_weight.shape[0] // 2
    frequencies = jnp.exp(-math.log(10000.0) * jnp.arange(half, dtype=F32) / half)
    angles = timesteps.astype(F32)[:, None] * frequencies[None]
    sinusoid = jnp.concatenate([jnp.cos(angles), jnp.sin(angles)], axis=1)
    class_row = lax.dynamic_slice_in_dim(class_table, class_ids[0], 1, axis=0).astype(F32)
    width = adaptive_weight.shape[0]
    spare = channels - width
    time_bias, mix = time_bias[None], adaptive_weight
    if spare:
        time_weight, time_bias, class_row = (
            jnp.pad(part, ((0, 0), (0, spare))) for part in (time_weight, time_bias, class_row)
        )
        mix = jnp.pad(mix, ((0, spare), (0, 0)))
    embed = call(embed_kernel, block, (sinusoid, class_row, time_weight, time_bias, mix), smem=0, name="embed")

    hidden, stat_one, one, two, three = call(
        functools.partial(second_kernel, dims, len(stats)),
        (narrow, block, halo, small, halo),
        (place, flat, image_one, image_three, weights_first, gain, bias, embed, *stats),
        (padded,),
        conv_flops,
        name="second",
    )
    hidden_one, hidden_three, stats = exchange(one, two, three, cols)
    grad_active = call(
        functools.partial(grad_kernel, dims),
        wide,
        (place, flat_cot, image_one, image_three, weights_second),
        (padded,),
        conv_flops,
        name="grad",
    )
    active, grad_norm, stat_two, one, two, three = call(
        functools.partial(third_kernel, dims, len(stats)),
        (shape((cells + 2 * cols, channels), BF16), wide, block, halo, small, halo),
        (place, hidden, hidden_one, hidden_three, grad_active, adaptive_bias[None], *stats),
        flops=1000,
        name="third",
    )
    grad_one, grad_three, stats = exchange(one, two, three, cols)
    branch = call(
        functools.partial(branch_kernel, dims), narrow, (active, weights_second), flops=conv_flops, smem=0, name="branch"
    )
    grad_first, sums, pairs = call(
        functools.partial(fourth_kernel, dims, len(stats)),
        (wide, small, block),
        (place, grad_norm, grad_one, grad_three, hidden, hidden_one, hidden_three, stat_two,
         weights_first, flat, stat_one, gain, bias, embed, *stats),
        (padded,),
        conv_flops,
        name="fourth",
    )
    stats = spread_small(sums)
    if fleet == 4:
        pair_list = [pairs, *(swap(pairs, "image", fleet, k) for k in (1, 2, 3))]
    else:
        pair_list = [lax.all_gather(pairs, "image", axis=0, tiled=True)]
    input_grad = call(
        functools.partial(fifth_kernel, dims, len(stats)), narrow, (grad_first, flat, stat_one, *stats), smem=0, name="fifth"
    )
    image = lax.axis_index("image").astype(jnp.int32)[None]
    grad_weight, grad_bias = call(
        weight_kernel,
        (shape((channels, 2 * channels), F32), shape((1, 2 * channels), F32)),
        (image, *pair_list),
        name="weight",
    )
    return (
        branch.reshape(images.shape),
        input_grad.reshape(images.shape),
        grad_weight[:width],
        grad_bias[0],
    )


def solution(mesh):
    return jax.shard_map(
        body,
        mesh=mesh,
        in_specs=(
            P(("groups", "image"), "tile", None, None),
            P(("groups", "image"), "tile", None, None),
            P(("groups", "image")),
            P(("groups", "image")),
            P(),
            P(),
            P(),
            P(),
            P(None, "tile"),
            P("tile"),
            P(None, "tile"),
            P("tile", None),
            P(),
        ),
        out_specs=(
            P(("groups", "image"), "tile", None, None),
            P(("groups", "image"), "tile", None, None),
            P(("groups", "tile"), None),
            P("groups"),
        ),
        check_vma=False,
    )
```

```python
import functools
import math

import jax
import jax.numpy as jnp
from jax import lax
from jax.experimental import pallas as pl
from jax.experimental.pallas import tpu as pltpu
from jax.sharding import PartitionSpec as P

GN_GROUPS = 32
EPSILON = 1e-05
VMEM_LIMIT = 12 * 1024 * 1024
F32, BF16 = jnp.float32, jnp.bfloat16

STAT_ROWS = 32


def terms(values):
    high = values.astype(BF16).astype(F32)
    rest = values - high
    middle = rest.astype(BF16).astype(F32)
    low = (rest - middle).astype(BF16).astype(F32)
    return jnp.concatenate([high, middle, low, jnp.zeros_like(high)], axis=0).astype(BF16)


def joined(block):
    wide = block.astype(F32)
    return wide[0:8] + (wide[8:16] + wide[16:24])


def rows8(*rows):
    width = rows[0].shape[1]
    index = lax.broadcasted_iota(jnp.int32, (8, width), 0)
    out = jnp.zeros((8, width), F32)
    for place, row in enumerate(rows):
        out = jnp.where(index == place, jnp.broadcast_to(row, (8, width)), out)
    return out


def group_matrix(channels):
    shift = (channels // GN_GROUPS).bit_length() - 1
    row = lax.shift_right_logical(lax.broadcasted_iota(jnp.int32, (channels, channels), 0), shift)
    col = lax.shift_right_logical(lax.broadcasted_iota(jnp.int32, (channels, channels), 1), shift)
    return (row == col).astype(F32).astype(BF16)


def group_sums(rows, groups):
    out = jnp.dot(terms(rows), groups, preferred_element_type=F32)
    return out[0:8] + (out[8:16] + out[16:24])


def tree_sum(parts):
    parts = list(parts)
    while len(parts) > 1:
        parts = [
            parts[i] + parts[i + 1] if i + 1 < len(parts) else parts[i]
            for i in range(0, len(parts), 2)
        ]
    return parts[0]


def local_moments(values, groups, count):
    mean = group_sums(rows8(jnp.sum(values, axis=0, keepdims=True)), groups)[0:1] / count
    centred = values - mean
    spread = group_sums(rows8(jnp.sum(centred * centred, axis=0, keepdims=True)), groups)[0:1]
    return mean, spread


def joint_moments(stats, count):
    tiles = len(stats)
    mean = tree_sum([s[0:1] for s in stats]) / tiles
    spread = tree_sum([s[1:2] + count * (s[0:1] - mean) * (s[0:1] - mean) for s in stats])
    return mean, lax.rsqrt(spread / (count * tiles) + EPSILON)


def sigmoid(values):
    return 1.0 / (1.0 + jnp.exp(-values))


def column_index(cells, cols, channels):
    index = lax.broadcasted_iota(jnp.int32, (cells, channels), 0)
    return lax.bitwise_and(index, cols - 1)


def conv(padded_ref, kernel_ref, cells, cols, flipped):
    parts = []
    for j in range(3):
        total = None
        for i in range(3):
            rows = padded_ref[(2 - i if flipped else i) * cols : (2 - i if flipped else i) * cols + cells]
            weights = kernel_ref[3 * i + j]
            product = lax.dot_general(
                rows,
                weights,
                (((1,), (1 if flipped else 0,)), ((), ())),
                preferred_element_type=F32,
            )
            total = product if total is None else total + product
        parts.append(total)
    if flipped:
        parts = parts[::-1]
    column = column_index(cells, cols, parts[0].shape[1])
    left = jnp.where(column == 0, 0.0, pltpu.roll(parts[0], 1, 0))
    right = jnp.where(column == cols - 1, 0.0, pltpu.roll(parts[2], cells - 1, 0))
    return parts[1] + (left + right)


def stat_list(refs, start, tiles):
    if len(refs) == 1:
        return [joined(refs[0][STAT_ROWS * t : STAT_ROWS * (t + 1)]) for t in range(tiles)]
    return [joined(ref[s : s + STAT_ROWS]) for ref, s in zip(refs, start, strict=True)]


def standing(tiles):
    tile = lax.axis_index("tile")
    return tile, lax.bitwise_and(tile, 1) if tiles == 4 else 0 * tile


def edges(place, one, three):
    odd = place[1] == 1
    return jnp.where(odd, one, three), jnp.where(odd, three, one)


def starts(place, cells, cols):
    odd = place[1]
    first = pl.multiple_of((1 - odd) * (cells - cols), cols)
    third = pl.multiple_of(odd * (cells - cols), cols)
    return first, third


def first_kernel(dims, *refs):
    cells, cols, channels, tiles = dims
    count = (len(refs) - 7) // 2
    sources, step, label = refs[:count], refs[count], refs[count + 1]
    copies_to = refs[count + 2 : 2 * count + 2]
    one, two, three, instant, sems = refs[2 * count + 2 :]
    copies = [
        pltpu.make_async_copy(source, target, sems.at[k])
        for k, (source, target) in enumerate(zip(sources, copies_to, strict=True))
    ]
    for copy in copies:
        copy.start()
    images, cotangent = copies_to[:2]
    place = standing(tiles)
    start_one, start_three = starts(place, cells, cols)
    groups = group_matrix(channels)
    copies[0].wait()
    mean, spread = local_moments(
        images[...].astype(F32), groups, cells * (channels // GN_GROUPS)
    )
    one[0:cols] = images[pl.ds(start_one, cols)]
    three[0:cols] = images[pl.ds(start_three, cols)]
    copies[1].wait()
    one[cols : 2 * cols] = cotangent[pl.ds(start_one, cols)]
    three[cols : 2 * cols] = cotangent[pl.ds(start_three, cols)]
    block = terms(rows8(mean, spread))
    one[2 * cols :] = block
    two[...] = block
    three[2 * cols :] = block
    for copy in copies[2:]:
        copy.wait()
    row = lax.broadcasted_iota(jnp.int32, instant.shape, 0)
    instant[...] = jnp.where(row == 0, step[0], label[0])


def embed_kernel(instant, table, time_weight, time_bias, adaptive_weight, out):
    channels = adaptive_weight.shape[1] // 2
    half = time_weight.shape[0] // 2

    def times(vector, weights):
        product = jnp.dot(terms(rows8(vector)), weights, preferred_element_type=F32)
        return (product[0:8] + (product[8:16] + product[16:24]))[0:1]

    place = lax.broadcasted_iota(jnp.int32, (8, half), 1).astype(F32)
    angles = instant[0:1, 0:1].astype(F32) * jnp.exp(-math.log(10000.0) * place / half)
    sinusoid = jnp.concatenate([jnp.cos(angles), jnp.sin(angles)], axis=1)[0:1]
    classes = lax.broadcasted_iota(jnp.int32, (16, table.shape[0]), 1)
    onehot = (classes == instant[1:2, 0:1]).astype(F32).astype(BF16)
    row = jnp.dot(onehot, table[...], preferred_element_type=F32)[0:1]
    hidden = times(sinusoid, time_weight[...]) + time_bias[...]
    embedding = hidden * sigmoid(hidden) + row
    activated = embedding * sigmoid(embedding)
    partial = times(activated, adaptive_weight[...])
    out[...] = rows8(partial[:, :channels], partial[:, channels:], activated)


def second_kernel(dims, n_stats, images, one, three, weights, gain, bias, embed, *rest):
    cells, cols, channels, tiles = dims
    place = standing(tiles)
    stat_refs, (hidden, stat, out_one, out_two, out_three, padded) = rest[:n_stats], rest[n_stats:]
    count = cells * (channels // GN_GROUPS)
    mean, inverse = joint_moments(
        stat_list(stat_refs, (0, 2 * cols, 0, 2 * cols), tiles), count
    )
    stat[...] = rows8(mean, inverse)
    above, below = edges(place, one[0:cols], three[0:cols])

    def active(block):
        pre = (block.astype(F32) - mean) * inverse * gain[...] + bias[...]
        return pre * sigmoid(pre)

    padded[0:cols] = jnp.where(place[0] > 0, active(above), 0.0).astype(BF16)
    padded[cols : cols + cells] = active(images[...]).astype(BF16)
    padded[cols + cells :] = jnp.where(place[0] < tiles - 1, active(below), 0.0).astype(BF16)
    rounded = conv(padded, weights, cells, cols, False).astype(BF16)
    hidden[...] = rounded
    mean_two, spread_two = local_moments(rounded.astype(F32), group_matrix(channels), count)
    block = terms(rows8(mean_two, spread_two, embed[0:1], embed[1:2]))
    start_one, start_three = starts(place, cells, cols)
    out_one[0:cols] = hidden[pl.ds(start_one, cols)]
    out_three[0:cols] = hidden[pl.ds(start_three, cols)]
    out_one[cols:] = block
    out_two[...] = block
    out_three[cols:] = block


def grad_kernel(dims, cotangent, one, three, weights, out, padded):
    cells, cols, channels, tiles = dims
    place = standing(tiles)
    above, below = edges(place, one[cols : 2 * cols], three[cols : 2 * cols])
    padded[0:cols] = jnp.where(place[0] > 0, above, jnp.zeros_like(above))
    padded[cols : cols + cells] = cotangent[...]
    padded[cols + cells :] = jnp.where(place[0] < tiles - 1, below, jnp.zeros_like(below))
    out[...] = conv(padded, weights, cells, cols, True)


def third_kernel(dims, n_stats, hidden, one, three, grad_active, adaptive_bias, *rest):
    cells, cols, channels, tiles = dims
    place = standing(tiles)
    stat_refs, (active, grad_norm, stat, out_one, out_two, out_three) = rest[:n_stats], rest[n_stats:]
    count = cells * (channels // GN_GROUPS)
    stats = stat_list(stat_refs, (0, cols, 0, cols), tiles)
    mean, inverse = joint_moments(stats, count)
    modulation = tree_sum(stats)
    factor = 1.0 + (modulation[2:3] + adaptive_bias[:, :channels])
    shift = modulation[3:4] + adaptive_bias[:, channels:]
    stat[...] = rows8(mean, inverse, factor)
    above, below = edges(place, one[0:cols], three[0:cols])

    def pieces(block):
        normed = (block.astype(F32) - mean) * inverse
        pre = normed * factor + shift
        return normed, pre, sigmoid(pre)

    _, pre, gate = pieces(above)
    active[0:cols] = jnp.where(place[0] > 0, pre * gate, 0.0).astype(BF16)
    _, pre, gate = pieces(below)
    active[cols + cells :] = jnp.where(place[0] < tiles - 1, pre * gate, 0.0).astype(BF16)
    normed, pre, gate = pieces(hidden[...])
    active[cols : cols + cells] = (pre * gate).astype(BF16)
    grad_pre = grad_active[...] * (gate * (1.0 + pre * (1.0 - gate)))
    grad_norm[...] = grad_pre * factor
    block = terms(
        rows8(
            jnp.sum(grad_pre * normed, axis=0, keepdims=True),
            jnp.sum(grad_pre, axis=0, keepdims=True),
        )
    )
    start_one, start_three = starts(place, cells, cols)
    out_one[0:cols] = grad_norm[pl.ds(start_one, cols)].astype(BF16)
    out_three[0:cols] = grad_norm[pl.ds(start_three, cols)].astype(BF16)
    out_one[cols:] = block
    out_two[...] = block
    out_three[cols:] = block


def branch_kernel(dims, active, weights, out):
    cells, cols, channels, tiles = dims
    out[...] = conv(active, weights, cells, cols, False).astype(BF16)


def fourth_kernel(
    dims, n_stats, branch, grad_norm, one, three, hidden, hidden_one, hidden_three, stat_two,
    weights, images, stat_one, gain, bias, embed, *rest
):
    cells, cols, channels, tiles = dims
    place = standing(tiles)
    stat_refs, (grad_first, out, pairs, padded) = rest[:n_stats], rest[n_stats:]
    total = cells * (channels // GN_GROUPS) * tiles
    sums = tree_sum(stat_list(stat_refs, (0, cols, 0, cols), tiles))
    pairs[...] = rows8(sums[0:1], sums[1:2], embed[2:3])
    mean, inverse, factor = stat_two[0:1], stat_two[1:2], stat_two[2:3]
    groups = group_matrix(channels)
    means = group_sums(sums * factor, groups) / total
    paired, plain = means[0:1], means[1:2]
    above, below = edges(place, one[0:cols], three[0:cols])
    hidden_above, hidden_below = edges(place, hidden_one[0:cols], hidden_three[0:cols])

    def grad_hidden(grad, block):
        normed = (block.astype(F32) - mean) * inverse
        return inverse * (grad.astype(F32) - plain - normed * paired)

    padded[0:cols] = jnp.where(place[0] > 0, grad_hidden(above, hidden_above), 0.0).astype(BF16)
    padded[cols : cols + cells] = grad_hidden(grad_norm[...], hidden[...]).astype(BF16)
    padded[cols + cells :] = jnp.where(
        place[0] < tiles - 1, grad_hidden(below, hidden_below), 0.0
    ).astype(BF16)
    grad_active = conv(padded, weights, cells, cols, True)
    normed = (images[...].astype(F32) - stat_one[0:1]) * stat_one[1:2]
    pre = normed * gain[...] + bias[...]
    gate = sigmoid(pre)
    grad = grad_active * (gate * (1.0 + pre * (1.0 - gate))) * gain[...]
    grad_first[...] = grad
    sums_first = rows8(
        jnp.sum(grad, axis=0, keepdims=True), jnp.sum(grad * normed, axis=0, keepdims=True)
    )
    out[...] = terms(group_sums(sums_first, groups))


def fifth_kernel(dims, n_stats, grad_first, images, stat_one, *rest):
    cells, cols, channels, tiles = dims
    stat_refs, (out,) = rest[:n_stats], rest[n_stats:]
    total = cells * (channels // GN_GROUPS) * tiles
    means = tree_sum(stat_list(stat_refs, (0, 0, 0, 0), tiles)) / total
    inverse = stat_one[1:2]
    normed = (images[...].astype(F32) - stat_one[0:1]) * inverse
    out[...] = (inverse * (grad_first[...] - means[0:1] - normed * means[1:2])).astype(BF16)


def weight_kernel(*rest):
    pair_refs, (weight, bias) = rest[:-2], rest[-2:]
    if len(pair_refs) == 1:
        blocks = [pair_refs[0][8 * n : 8 * n + 8] for n in range(pair_refs[0].shape[0] // 8)]
        places = list(range(len(blocks)))
    else:
        blocks = [ref[...] for ref in pair_refs]
        places = [lax.bitwise_xor(lax.axis_index("image"), k) for k in range(len(blocks))]
    count = -(-len(blocks) // 8) * 8
    channels = blocks[0].shape[1]
    row = lax.broadcasted_iota(jnp.int32, (count, channels), 0)

    def ordered(which):
        out = jnp.zeros((count, channels), F32)
        for block, place in zip(blocks, places, strict=True):
            out = jnp.where(row == place, jnp.broadcast_to(block[which : which + 1], out.shape), out)
        return out

    scale, shift, activated = ordered(0), ordered(1), ordered(2)
    for start, part in ((0, scale), (channels, shift)):
        weight[:, start : start + channels] = lax.dot_general(
            activated,
            part,
            (((0,), (0,)), ((), ())),
            precision=lax.Precision.HIGHEST,
            preferred_element_type=F32,
        )
        bias[:, start : start + channels] = jnp.sum(part, axis=0, keepdims=True)


def call(kernel, out_shapes, operands, scratch=(), flops=1000, name=None, spaces=None):
    size = sum(o.size * o.dtype.itemsize for o in operands)
    return pl.pallas_call(
        kernel,
        out_shape=out_shapes,
        in_specs=[
            pl.BlockSpec(memory_space=(spaces or {}).get(k, pltpu.VMEM)) for k in range(len(operands))
        ],
        out_specs=jax.tree.map(lambda _: pl.BlockSpec(memory_space=pltpu.VMEM), out_shapes),
        scratch_shapes=list(scratch),
        compiler_params=pltpu.CompilerParams(vmem_limit_bytes=VMEM_LIMIT),
        cost_estimate=pl.CostEstimate(flops=flops, bytes_accessed=size, transcendentals=0),
        name=name,
    )(*operands)


def swap(values, axis, size, distance):
    return lax.ppermute(values, axis, [(i, i ^ distance) for i in range(size)])


def exchange(one, two, three, stat_start):
    tiles = lax.axis_size("tile")
    if tiles == 4:
        got = [swap(part, "tile", tiles, k + 1) for k, part in enumerate((one, two, three))]
        return got[0], got[2], [two, *got]
    ahead = [(i, (i + 1) % tiles) for i in range(tiles)]
    behind = [(target, source) for source, target in ahead]
    below, above = lax.ppermute(three, "tile", behind), lax.ppermute(one, "tile", ahead)
    return below, above, [lax.all_gather(two, "tile", axis=0, tiled=True)]


def spread_small(block):
    tiles = lax.axis_size("tile")
    if tiles == 4:
        return [block, *(swap(block, "tile", tiles, k) for k in (1, 2, 3))]
    return [lax.all_gather(block, "tile", axis=0, tiled=True)]


def body(
    images,
    cotangent,
    timesteps,
    class_ids,
    norm_gain,
    norm_bias,
    conv_first,
    conv_second,
    time_weight,
    time_bias,
    class_table,
    adaptive_weight,
    adaptive_bias,
):
    _, rows, cols, channels = images.shape
    tiles, fleet = lax.axis_size("tile"), lax.axis_size("image")
    cells = rows * cols
    dims = (cells, cols, channels, tiles)
    shape = jax.ShapeDtypeStruct
    conv_flops = 18 * cells * channels * channels
    padded = pltpu.VMEM((cells + 2 * cols, channels), BF16)
    small = shape((STAT_ROWS, channels), BF16)
    halo = shape((cols + STAT_ROWS, channels), BF16)
    halos = shape((2 * cols + STAT_ROWS, channels), BF16)
    block = shape((8, channels), F32)
    wide = shape((cells, channels), F32)
    narrow = shape((cells, channels), BF16)

    width = adaptive_weight.shape[0]
    spare = channels - width
    time_bias, mix = time_bias[None], adaptive_weight
    if spare:
        time_weight, time_bias, class_table = (
            jnp.pad(part, ((0, 0), (0, spare))) for part in (time_weight, time_bias, class_table)
        )
        mix = jnp.pad(mix, ((0, spare), (0, 0)))
    loads = (
        images.reshape(cells, channels),
        cotangent.reshape(cells, channels),
        time_weight,
        mix,
        class_table,
        time_bias,
        norm_gain[None],
        norm_bias[None],
        adaptive_bias[None],
        conv_first.reshape(9, channels, channels),
        conv_second.reshape(9, channels, channels),
    )
    spaces = {k: pltpu.HBM for k in range(len(loads))}
    spaces[len(loads)] = spaces[len(loads) + 1] = pltpu.SMEM
    *held, one, two, three, instant = call(
        functools.partial(first_kernel, dims),
        (*(shape(part.shape, part.dtype) for part in loads), halos, small, halos, shape((8, 128), jnp.int32)),
        (*loads, timesteps, class_ids),
        (pltpu.SemaphoreType.DMA((len(loads),)),),
        name="first",
        spaces=spaces,
    )
    flat, flat_cot, time_weight, mix, class_table, time_bias, gain, bias, adaptive_bias, weights_first, weights_second = held
    image_one, image_three, stats = exchange(one, two, three, 2 * cols)
    embed = call(embed_kernel, block, (instant, class_table, time_weight, time_bias, mix), name="embed")

    hidden, stat_one, one, two, three = call(
        functools.partial(second_kernel, dims, len(stats)),
        (narrow, block, halo, small, halo),
        (flat, image_one, image_three, weights_first, gain, bias, embed, *stats),
        (padded,),
        conv_flops,
        name="second",
    )
    hidden_one, hidden_three, stats = exchange(one, two, three, cols)
    grad_active = call(
        functools.partial(grad_kernel, dims),
        wide,
        (flat_cot, image_one, image_three, weights_second),
        (padded,),
        conv_flops,
        name="grad",
    )
    active, grad_norm, stat_two, one, two, three = call(
        functools.partial(third_kernel, dims, len(stats)),
        (shape((cells + 2 * cols, channels), BF16), wide, block, halo, small, halo),
        (hidden, hidden_one, hidden_three, grad_active, adaptive_bias, *stats),
        flops=1000,
        name="third",
    )
    grad_one, grad_three, stats = exchange(one, two, three, cols)
    branch = call(
        functools.partial(branch_kernel, dims), narrow, (active, weights_second), flops=conv_flops, name="branch"
    )
    grad_first, sums, pairs = call(
        functools.partial(fourth_kernel, dims, len(stats)),
        (wide, small, block),
        (branch, grad_norm, grad_one, grad_three, hidden, hidden_one, hidden_three, stat_two,
         weights_first, flat, stat_one, gain, bias, embed, *stats),
        (padded,),
        conv_flops,
        name="fourth",
        spaces={0: pl.ANY},
    )
    stats = spread_small(sums)
    if fleet == 4:
        pair_list = [pairs, *(swap(pairs, "image", fleet, k) for k in (1, 2, 3))]
    else:
        pair_list = [lax.all_gather(pairs, "image", axis=0, tiled=True)]
    input_grad = call(
        functools.partial(fifth_kernel, dims, len(stats)), narrow, (grad_first, flat, stat_one, *stats), name="fifth"
    )
    grad_weight, grad_bias = call(
        weight_kernel,
        (shape((channels, 2 * channels), F32), shape((1, 2 * channels), F32)),
        tuple(pair_list),
        name="weight",
    )
    return (
        branch.reshape(images.shape),
        input_grad.reshape(images.shape),
        grad_weight[:width],
        grad_bias[0],
    )


def solution(mesh):
    return jax.shard_map(
        body,
        mesh=mesh,
        in_specs=(
            P(("groups", "image"), "tile", None, None),
            P(("groups", "image"), "tile", None, None),
            P(("groups", "image")),
            P(("groups", "image")),
            P(),
            P(),
            P(),
            P(),
            P(None, "tile"),
            P("tile"),
            P(None, "tile"),
            P("tile", None),
            P(),
        ),
        out_specs=(
            P(("groups", "image"), "tile", None, None),
            P(("groups", "image"), "tile", None, None),
            P(("groups", "tile"), None),
            P("groups"),
        ),
        check_vma=False,
    )
```

```python
import functools
import math

import jax
import jax.numpy as jnp
from jax import lax
from jax.experimental import pallas as pl
from jax.experimental.pallas import tpu as pltpu
from jax.sharding import PartitionSpec as P

GN_GROUPS = 32
EPSILON = 1e-05
VMEM_LIMIT = 12 * 1024 * 1024
F32, BF16 = jnp.float32, jnp.bfloat16

STAT_ROWS = 32


def terms(values):
    high = values.astype(BF16).astype(F32)
    rest = values - high
    middle = rest.astype(BF16).astype(F32)
    low = (rest - middle).astype(BF16).astype(F32)
    return jnp.concatenate([high, middle, low, jnp.zeros_like(high)], axis=0).astype(BF16)


def joined(block):
    wide = block.astype(F32)
    return wide[0:8] + (wide[8:16] + wide[16:24])


def rows8(*rows):
    width = rows[0].shape[1]
    index = lax.broadcasted_iota(jnp.int32, (8, width), 0)
    out = jnp.zeros((8, width), F32)
    for place, row in enumerate(rows):
        out = jnp.where(index == place, jnp.broadcast_to(row, (8, width)), out)
    return out


def group_matrix(channels):
    shift = (channels // GN_GROUPS).bit_length() - 1
    row = lax.shift_right_logical(lax.broadcasted_iota(jnp.int32, (channels, channels), 0), shift)
    col = lax.shift_right_logical(lax.broadcasted_iota(jnp.int32, (channels, channels), 1), shift)
    return (row == col).astype(F32).astype(BF16)


def group_sums(rows, groups):
    out = jnp.dot(terms(rows), groups, preferred_element_type=F32)
    return out[0:8] + (out[8:16] + out[16:24])


def tree_sum(parts):
    parts = list(parts)
    while len(parts) > 1:
        parts = [
            parts[i] + parts[i + 1] if i + 1 < len(parts) else parts[i]
            for i in range(0, len(parts), 2)
        ]
    return parts[0]


def local_moments(values, groups, count):
    mean = group_sums(rows8(jnp.sum(values, axis=0, keepdims=True)), groups)[0:1] / count
    centred = values - mean
    spread = group_sums(rows8(jnp.sum(centred * centred, axis=0, keepdims=True)), groups)[0:1]
    return mean, spread


def joint_moments(stats, count):
    tiles = len(stats)
    mean = tree_sum([s[0:1] for s in stats]) / tiles
    spread = tree_sum([s[1:2] + count * (s[0:1] - mean) * (s[0:1] - mean) for s in stats])
    return mean, lax.rsqrt(spread / (count * tiles) + EPSILON)


def sigmoid(values):
    return 1.0 / (1.0 + jnp.exp(-values))


def column_index(cells, cols, channels):
    index = lax.broadcasted_iota(jnp.int32, (cells, channels), 0)
    return lax.bitwise_and(index, cols - 1)


def conv(padded_ref, kernel_ref, cells, cols, flipped):
    parts = []
    for j in range(3):
        total = None
        for i in range(3):
            rows = padded_ref[(2 - i if flipped else i) * cols : (2 - i if flipped else i) * cols + cells]
            weights = kernel_ref[3 * i + j]
            product = lax.dot_general(
                rows,
                weights,
                (((1,), (1 if flipped else 0,)), ((), ())),
                preferred_element_type=F32,
            )
            total = product if total is None else total + product
        parts.append(total)
    if flipped:
        parts = parts[::-1]
    column = column_index(cells, cols, parts[0].shape[1])
    left = jnp.where(column == 0, 0.0, pltpu.roll(parts[0], 1, 0))
    right = jnp.where(column == cols - 1, 0.0, pltpu.roll(parts[2], cells - 1, 0))
    return parts[1] + (left + right)


def stat_list(refs, start, tiles):
    if len(refs) == 1:
        return [joined(refs[0][STAT_ROWS * t : STAT_ROWS * (t + 1)]) for t in range(tiles)]
    return [joined(ref[s : s + STAT_ROWS]) for ref, s in zip(refs, start, strict=True)]


def standing(tiles):
    tile = lax.axis_index("tile")
    return tile, lax.bitwise_and(tile, 1) if tiles == 4 else 0 * tile


def edges(place, one, three):
    odd = place[1] == 1
    return jnp.where(odd, one, three), jnp.where(odd, three, one)


def starts(place, cells, cols):
    odd = place[1]
    first = pl.multiple_of((1 - odd) * (cells - cols), cols)
    third = pl.multiple_of(odd * (cells - cols), cols)
    return first, third


def first_kernel(dims, *refs):
    cells, cols, channels, tiles = dims
    count = (len(refs) - 4) // 2
    sources, copies_to = refs[:count], refs[count : 2 * count]
    one, two, three, sems = refs[2 * count :]
    copies = [
        pltpu.make_async_copy(source, target, sems.at[k])
        for k, (source, target) in enumerate(zip(sources, copies_to, strict=True))
    ]
    for copy in copies:
        copy.start()
    images, cotangent = copies_to[:2]
    place = standing(tiles)
    start_one, start_three = starts(place, cells, cols)
    groups = group_matrix(channels)
    copies[0].wait()
    mean, spread = local_moments(
        images[...].astype(F32), groups, cells * (channels // GN_GROUPS)
    )
    one[0:cols] = images[pl.ds(start_one, cols)]
    three[0:cols] = images[pl.ds(start_three, cols)]
    copies[1].wait()
    one[cols : 2 * cols] = cotangent[pl.ds(start_one, cols)]
    three[cols : 2 * cols] = cotangent[pl.ds(start_three, cols)]
    block = terms(rows8(mean, spread))
    one[2 * cols :] = block
    two[...] = block
    three[2 * cols :] = block
    for copy in copies[2:]:
        copy.wait()


def embed_kernel(step, label, table, time_weight, time_bias, adaptive_weight, out):
    channels = adaptive_weight.shape[1] // 2
    half = time_weight.shape[0] // 2

    def times(vector, weights):
        product = jnp.dot(terms(rows8(vector)), weights, preferred_element_type=F32)
        return (product[0:8] + (product[8:16] + product[16:24]))[0:1]

    place = lax.broadcasted_iota(jnp.int32, (8, half), 1).astype(F32)
    angles = step[0].astype(F32) * jnp.exp(-math.log(10000.0) * place / half)
    sinusoid = jnp.concatenate([jnp.cos(angles), jnp.sin(angles)], axis=1)[0:1]
    classes = lax.broadcasted_iota(jnp.int32, (16, table.shape[0]), 1)
    onehot = (classes == label[0]).astype(F32).astype(BF16)
    row = jnp.dot(onehot, table[...], preferred_element_type=F32)[0:1]
    hidden = times(sinusoid, time_weight[...]) + time_bias[...]
    embedding = hidden * sigmoid(hidden) + row
    activated = embedding * sigmoid(embedding)
    partial = times(activated, adaptive_weight[...])
    out[...] = rows8(partial[:, :channels], partial[:, channels:], activated)


def second_kernel(dims, n_stats, images, one, three, weights, gain, bias, embed, *rest):
    cells, cols, channels, tiles = dims
    place = standing(tiles)
    stat_refs, (hidden, stat, out_one, out_two, out_three, padded) = rest[:n_stats], rest[n_stats:]
    count = cells * (channels // GN_GROUPS)
    mean, inverse = joint_moments(
        stat_list(stat_refs, (0, 2 * cols, 0, 2 * cols), tiles), count
    )
    stat[...] = rows8(mean, inverse)
    above, below = edges(place, one[0:cols], three[0:cols])

    def active(block):
        pre = (block.astype(F32) - mean) * inverse * gain[...] + bias[...]
        return pre * sigmoid(pre)

    padded[0:cols] = jnp.where(place[0] > 0, active(above), 0.0).astype(BF16)
    padded[cols : cols + cells] = active(images[...]).astype(BF16)
    padded[cols + cells :] = jnp.where(place[0] < tiles - 1, active(below), 0.0).astype(BF16)
    rounded = conv(padded, weights, cells, cols, False).astype(BF16)
    hidden[...] = rounded
    mean_two, spread_two = local_moments(rounded.astype(F32), group_matrix(channels), count)
    block = terms(rows8(mean_two, spread_two, embed[0:1], embed[1:2]))
    start_one, start_three = starts(place, cells, cols)
    out_one[0:cols] = hidden[pl.ds(start_one, cols)]
    out_three[0:cols] = hidden[pl.ds(start_three, cols)]
    out_one[cols:] = block
    out_two[...] = block
    out_three[cols:] = block


def grad_kernel(dims, cotangent, one, three, weights, out, padded):
    cells, cols, channels, tiles = dims
    place = standing(tiles)
    above, below = edges(place, one[cols : 2 * cols], three[cols : 2 * cols])
    padded[0:cols] = jnp.where(place[0] > 0, above, jnp.zeros_like(above))
    padded[cols : cols + cells] = cotangent[...]
    padded[cols + cells :] = jnp.where(place[0] < tiles - 1, below, jnp.zeros_like(below))
    out[...] = conv(padded, weights, cells, cols, True)


def third_kernel(dims, n_stats, hidden, one, three, grad_active, adaptive_bias, *rest):
    cells, cols, channels, tiles = dims
    place = standing(tiles)
    stat_refs, (active, grad_norm, stat, out_one, out_two, out_three) = rest[:n_stats], rest[n_stats:]
    count = cells * (channels // GN_GROUPS)
    stats = stat_list(stat_refs, (0, cols, 0, cols), tiles)
    mean, inverse = joint_moments(stats, count)
    modulation = tree_sum(stats)
    factor = 1.0 + (modulation[2:3] + adaptive_bias[:, :channels])
    shift = modulation[3:4] + adaptive_bias[:, channels:]
    stat[...] = rows8(mean, inverse, factor)
    above, below = edges(place, one[0:cols], three[0:cols])

    def pieces(block):
        normed = (block.astype(F32) - mean) * inverse
        pre = normed * factor + shift
        return normed, pre, sigmoid(pre)

    _, pre, gate = pieces(above)
    active[0:cols] = jnp.where(place[0] > 0, pre * gate, 0.0).astype(BF16)
    _, pre, gate = pieces(below)
    active[cols + cells :] = jnp.where(place[0] < tiles - 1, pre * gate, 0.0).astype(BF16)
    normed, pre, gate = pieces(hidden[...])
    active[cols : cols + cells] = (pre * gate).astype(BF16)
    grad_pre = grad_active[...] * (gate * (1.0 + pre * (1.0 - gate)))
    grad_norm[...] = grad_pre * factor
    block = terms(
        rows8(
            jnp.sum(grad_pre * normed, axis=0, keepdims=True),
            jnp.sum(grad_pre, axis=0, keepdims=True),
        )
    )
    start_one, start_three = starts(place, cells, cols)
    out_one[0:cols] = grad_norm[pl.ds(start_one, cols)].astype(BF16)
    out_three[0:cols] = grad_norm[pl.ds(start_three, cols)].astype(BF16)
    out_one[cols:] = block
    out_two[...] = block
    out_three[cols:] = block


def branch_kernel(dims, active, weights, out, token):
    cells, cols, channels, tiles = dims
    out[...] = conv(active, weights, cells, cols, False).astype(BF16)
    token[...] = jnp.zeros_like(token)


def fourth_kernel(
    dims, n_stats, token, grad_norm, one, three, hidden, hidden_one, hidden_three, stat_two,
    weights, images, stat_one, gain, bias, embed, *rest
):
    cells, cols, channels, tiles = dims
    place = standing(tiles)
    stat_refs, (grad_first, out, pairs, padded) = rest[:n_stats], rest[n_stats:]
    total = cells * (channels // GN_GROUPS) * tiles
    sums = tree_sum(stat_list(stat_refs, (0, cols, 0, cols), tiles))
    pairs[...] = rows8(sums[0:1], sums[1:2], embed[2:3])
    mean, inverse, factor = stat_two[0:1], stat_two[1:2], stat_two[2:3]
    groups = group_matrix(channels)
    means = group_sums(sums * factor, groups) / total
    paired, plain = means[0:1], means[1:2]
    above, below = edges(place, one[0:cols], three[0:cols])
    hidden_above, hidden_below = edges(place, hidden_one[0:cols], hidden_three[0:cols])

    def grad_hidden(grad, block):
        normed = (block.astype(F32) - mean) * inverse
        return inverse * (grad.astype(F32) - plain - normed * paired)

    padded[0:cols] = jnp.where(place[0] > 0, grad_hidden(above, hidden_above), 0.0).astype(BF16)
    padded[cols : cols + cells] = grad_hidden(grad_norm[...], hidden[...]).astype(BF16)
    padded[cols + cells :] = jnp.where(
        place[0] < tiles - 1, grad_hidden(below, hidden_below), 0.0
    ).astype(BF16)
    grad_active = conv(padded, weights, cells, cols, True)
    normed = (images[...].astype(F32) - stat_one[0:1]) * stat_one[1:2]
    pre = normed * gain[...] + bias[...]
    gate = sigmoid(pre)
    grad = grad_active * (gate * (1.0 + pre * (1.0 - gate))) * gain[...]
    grad_first[...] = grad
    sums_first = rows8(
        jnp.sum(grad, axis=0, keepdims=True), jnp.sum(grad * normed, axis=0, keepdims=True)
    )
    out[...] = terms(group_sums(sums_first, groups))


def fifth_kernel(dims, n_stats, grad_first, images, stat_one, *rest):
    cells, cols, channels, tiles = dims
    stat_refs, (out,) = rest[:n_stats], rest[n_stats:]
    total = cells * (channels // GN_GROUPS) * tiles
    means = tree_sum(stat_list(stat_refs, (0, 0, 0, 0), tiles)) / total
    inverse = stat_one[1:2]
    normed = (images[...].astype(F32) - stat_one[0:1]) * inverse
    out[...] = (inverse * (grad_first[...] - means[0:1] - normed * means[1:2])).astype(BF16)


def weight_kernel(*rest):
    pair_refs, (weight, bias) = rest[:-2], rest[-2:]
    if len(pair_refs) == 1:
        blocks = [pair_refs[0][8 * n : 8 * n + 8] for n in range(pair_refs[0].shape[0] // 8)]
        places = list(range(len(blocks)))
    else:
        blocks = [ref[...] for ref in pair_refs]
        places = [lax.bitwise_xor(lax.axis_index("image"), k) for k in range(len(blocks))]
    count = -(-len(blocks) // 8) * 8
    channels = blocks[0].shape[1]
    row = lax.broadcasted_iota(jnp.int32, (count, channels), 0)

    def ordered(which):
        out = jnp.zeros((count, channels), F32)
        for block, place in zip(blocks, places, strict=True):
            out = jnp.where(row == place, jnp.broadcast_to(block[which : which + 1], out.shape), out)
        return out

    scale, shift, activated = ordered(0), ordered(1), ordered(2)
    for start, part in ((0, scale), (channels, shift)):
        weight[:, start : start + channels] = lax.dot_general(
            activated,
            part,
            (((0,), (0,)), ((), ())),
            precision=lax.Precision.HIGHEST,
            preferred_element_type=F32,
        )
        bias[:, start : start + channels] = jnp.sum(part, axis=0, keepdims=True)


def call(kernel, out_shapes, operands, scratch=(), flops=1000, name=None, spaces=None):
    size = sum(o.size * o.dtype.itemsize for o in operands)
    return pl.pallas_call(
        kernel,
        out_shape=out_shapes,
        in_specs=[
            pl.BlockSpec(memory_space=(spaces or {}).get(k, pltpu.VMEM)) for k in range(len(operands))
        ],
        out_specs=jax.tree.map(lambda _: pl.BlockSpec(memory_space=pltpu.VMEM), out_shapes),
        scratch_shapes=list(scratch),
        compiler_params=pltpu.CompilerParams(vmem_limit_bytes=VMEM_LIMIT),
        cost_estimate=pl.CostEstimate(flops=flops, bytes_accessed=size, transcendentals=0),
        name=name,
    )(*operands)


def swap(values, axis, size, distance):
    return lax.ppermute(values, axis, [(i, i ^ distance) for i in range(size)])


def exchange(one, two, three, stat_start):
    tiles = lax.axis_size("tile")
    if tiles == 4:
        got = [swap(part, "tile", tiles, k + 1) for k, part in enumerate((one, two, three))]
        return got[0], got[2], [two, *got]
    ahead = [(i, (i + 1) % tiles) for i in range(tiles)]
    behind = [(target, source) for source, target in ahead]
    below, above = lax.ppermute(three, "tile", behind), lax.ppermute(one, "tile", ahead)
    return below, above, [lax.all_gather(two, "tile", axis=0, tiled=True)]


def spread_small(block):
    tiles = lax.axis_size("tile")
    if tiles == 4:
        return [block, *(swap(block, "tile", tiles, k) for k in (1, 2, 3))]
    return [lax.all_gather(block, "tile", axis=0, tiled=True)]


def body(
    images,
    cotangent,
    timesteps,
    class_ids,
    norm_gain,
    norm_bias,
    conv_first,
    conv_second,
    time_weight,
    time_bias,
    class_table,
    adaptive_weight,
    adaptive_bias,
):
    _, rows, cols, channels = images.shape
    tiles, fleet = lax.axis_size("tile"), lax.axis_size("image")
    cells = rows * cols
    dims = (cells, cols, channels, tiles)
    shape = jax.ShapeDtypeStruct
    conv_flops = 18 * cells * channels * channels
    padded = pltpu.VMEM((cells + 2 * cols, channels), BF16)
    small = shape((STAT_ROWS, channels), BF16)
    halo = shape((cols + STAT_ROWS, channels), BF16)
    halos = shape((2 * cols + STAT_ROWS, channels), BF16)
    block = shape((8, channels), F32)
    wide = shape((cells, channels), F32)
    narrow = shape((cells, channels), BF16)

    width = adaptive_weight.shape[0]
    spare = channels - width
    time_bias, mix = time_bias[None], adaptive_weight
    if spare:
        time_weight, time_bias, class_table = (
            jnp.pad(part, ((0, 0), (0, spare))) for part in (time_weight, time_bias, class_table)
        )
        mix = jnp.pad(mix, ((0, spare), (0, 0)))
    loads = (
        images.reshape(cells, channels),
        cotangent.reshape(cells, channels),
        time_weight,
        mix,
        class_table,
        time_bias,
        norm_gain[None],
        norm_bias[None],
        adaptive_bias[None],
        conv_first.reshape(9, channels, channels),
        conv_second.reshape(9, channels, channels),
    )
    spaces = {k: pl.ANY for k in range(len(loads))}
    *held, one, two, three = call(
        functools.partial(first_kernel, dims),
        (*(shape(part.shape, part.dtype) for part in loads), halos, small, halos),
        tuple(pltpu.with_memory_space_constraint(part, pltpu.HBM) for part in loads),
        (pltpu.SemaphoreType.DMA((len(loads),)),),
        name="first",
        spaces=spaces,
    )
    flat, flat_cot, time_weight, mix, class_table, time_bias, gain, bias, adaptive_bias, weights_first, weights_second = held
    image_one, image_three, stats = exchange(one, two, three, 2 * cols)
    embed = call(
        embed_kernel,
        block,
        (timesteps, class_ids, class_table, time_weight, time_bias, mix),
        name="embed",
        spaces={0: pltpu.SMEM, 1: pltpu.SMEM},
    )

    hidden, stat_one, one, two, three = call(
        functools.partial(second_kernel, dims, len(stats)),
        (narrow, block, halo, small, halo),
        (flat, image_one, image_three, weights_first, gain, bias, embed, *stats),
        (padded,),
        conv_flops,
        name="second",
    )
    hidden_one, hidden_three, stats = exchange(one, two, three, cols)
    grad_active = call(
        functools.partial(grad_kernel, dims),
        wide,
        (flat_cot, image_one, image_three, weights_second),
        (padded,),
        conv_flops,
        name="grad",
    )
    active, grad_norm, stat_two, one, two, three = call(
        functools.partial(third_kernel, dims, len(stats)),
        (shape((cells + 2 * cols, channels), BF16), wide, block, halo, small, halo),
        (hidden, hidden_one, hidden_three, grad_active, adaptive_bias, *stats),
        flops=1000,
        name="third",
    )
    grad_one, grad_three, stats = exchange(one, two, three, cols)
    branch, token = call(
        functools.partial(branch_kernel, dims), (narrow, shape((8, 128), F32)), (active, weights_second), flops=conv_flops, name="branch"
    )
    grad_first, sums, pairs = call(
        functools.partial(fourth_kernel, dims, len(stats)),
        (wide, small, block),
        (token, grad_norm, grad_one, grad_three, hidden, hidden_one, hidden_three, stat_two,
         weights_first, flat, stat_one, gain, bias, embed, *stats),
        (padded,),
        conv_flops,
        name="fourth",
    )
    stats = spread_small(sums)
    if fleet == 4:
        pair_list = [pairs, *(swap(pairs, "image", fleet, k) for k in (1, 2, 3))]
    else:
        pair_list = [lax.all_gather(pairs, "image", axis=0, tiled=True)]
    input_grad = call(
        functools.partial(fifth_kernel, dims, len(stats)), narrow, (grad_first, flat, stat_one, *stats), name="fifth"
    )
    grad_weight, grad_bias = call(
        weight_kernel,
        (shape((channels, 2 * channels), F32), shape((1, 2 * channels), F32)),
        tuple(pair_list),
        name="weight",
    )
    return (
        branch.reshape(images.shape),
        input_grad.reshape(images.shape),
        grad_weight[:width],
        grad_bias[0],
    )


def solution(mesh):
    return jax.shard_map(
        body,
        mesh=mesh,
        in_specs=(
            P(("groups", "image"), "tile", None, None),
            P(("groups", "image"), "tile", None, None),
            P(("groups", "image")),
            P(("groups", "image")),
            P(),
            P(),
            P(),
            P(),
            P(None, "tile"),
            P("tile"),
            P(None, "tile"),
            P("tile", None),
            P(),
        ),
        out_specs=(
            P(("groups", "image"), "tile", None, None),
            P(("groups", "image"), "tile", None, None),
            P(("groups", "tile"), None),
            P("groups"),
        ),
        check_vma=False,
    )
```

```python
import functools
import math

import jax
import jax.numpy as jnp
from jax import lax
from jax.experimental import pallas as pl
from jax.experimental.pallas import tpu as pltpu
from jax.sharding import PartitionSpec as P

GN_GROUPS = 32
EPSILON = 1e-05
VMEM_LIMIT = 12 * 1024 * 1024
F32, BF16 = jnp.float32, jnp.bfloat16

STAT_ROWS = 32


def terms(values):
    high = values.astype(BF16).astype(F32)
    rest = values - high
    middle = rest.astype(BF16).astype(F32)
    low = (rest - middle).astype(BF16).astype(F32)
    return jnp.concatenate([high, middle, low, jnp.zeros_like(high)], axis=0).astype(BF16)


def joined(block):
    wide = block.astype(F32)
    return wide[0:8] + (wide[8:16] + wide[16:24])


def rows8(*rows):
    width = rows[0].shape[1]
    index = lax.broadcasted_iota(jnp.int32, (8, width), 0)
    out = jnp.zeros((8, width), F32)
    for place, row in enumerate(rows):
        out = jnp.where(index == place, jnp.broadcast_to(row, (8, width)), out)
    return out


def group_matrix(channels):
    shift = (channels // GN_GROUPS).bit_length() - 1
    row = lax.shift_right_logical(lax.broadcasted_iota(jnp.int32, (channels, channels), 0), shift)
    col = lax.shift_right_logical(lax.broadcasted_iota(jnp.int32, (channels, channels), 1), shift)
    return (row == col).astype(F32).astype(BF16)


def group_sums(rows, groups):
    out = jnp.dot(terms(rows), groups, preferred_element_type=F32)
    return out[0:8] + (out[8:16] + out[16:24])


def tree_sum(parts):
    parts = list(parts)
    while len(parts) > 1:
        parts = [
            parts[i] + parts[i + 1] if i + 1 < len(parts) else parts[i]
            for i in range(0, len(parts), 2)
        ]
    return parts[0]


def local_moments(values, groups, count):
    mean = group_sums(rows8(jnp.sum(values, axis=0, keepdims=True)), groups)[0:1] / count
    centred = values - mean
    spread = group_sums(rows8(jnp.sum(centred * centred, axis=0, keepdims=True)), groups)[0:1]
    return mean, spread


def joint_moments(stats, count):
    tiles = len(stats)
    mean = tree_sum([s[0:1] for s in stats]) / tiles
    spread = tree_sum([s[1:2] + count * (s[0:1] - mean) * (s[0:1] - mean) for s in stats])
    return mean, lax.rsqrt(spread / (count * tiles) + EPSILON)


def sigmoid(values):
    return 1.0 / (1.0 + jnp.exp(-values))


def column_index(cells, cols, channels):
    index = lax.broadcasted_iota(jnp.int32, (cells, channels), 0)
    return lax.bitwise_and(index, cols - 1)


def conv(padded_ref, kernel_ref, cells, cols, flipped, turned=False):
    parts = []
    for j in range(3):
        total = None
        for i in range(3):
            start = (2 - i if flipped else i) * cols
            product = lax.dot_general(
                padded_ref[start : start + cells],
                kernel_ref[3 * i + j],
                (((1,), (1 if flipped and not turned else 0,)), ((), ())),
                preferred_element_type=F32,
            )
            total = product if total is None else total + product
        parts.append(total)
    if flipped:
        parts = parts[::-1]
    return parts[1] + (shifted(parts[0], cols, 1) + shifted(parts[2], cols, -1))


def shifted(values, cols, step):
    cells = values.shape[0]
    column = column_index(cells, cols, values.shape[1])
    if step == 1:
        return jnp.where(column == 0, 0.0, pltpu.roll(values, 1, 0))
    return jnp.where(column == cols - 1, 0.0, pltpu.roll(values, cells - 1, 0))


def stat_list(refs, start, tiles):
    if len(refs) == 1:
        size = refs[0].shape[0] // tiles
        return [joined(refs[0][size * t : size * t + STAT_ROWS]) for t in range(tiles)]
    return [joined(ref[s : s + STAT_ROWS]) for ref, s in zip(refs, start, strict=True)]


def standing(tiles):
    tile = lax.axis_index("tile")
    return tile, lax.bitwise_and(tile, 1) if tiles == 4 else 0 * tile


def edges(place, one, three):
    odd = place[1] == 1
    return jnp.where(odd, one, three), jnp.where(odd, three, one)


def starts(place, cells, cols):
    odd = place[1]
    first = pl.multiple_of((1 - odd) * (cells - cols), cols)
    third = pl.multiple_of(odd * (cells - cols), cols)
    return first, third


def first_kernel(dims, *refs):
    cells, cols, channels, tiles = dims
    count = (len(refs) - 4) // 2
    sources, copies_to = refs[:count], refs[count : 2 * count]
    one, two, three, sems = refs[2 * count :]
    copies = [
        pltpu.make_async_copy(source, target, sems.at[k])
        for k, (source, target) in enumerate(zip(sources, copies_to, strict=True))
    ]
    for copy in copies:
        copy.start()
    images, cotangent = copies_to[:2]
    place = standing(tiles)
    start_one, start_three = starts(place, cells, cols)
    groups = group_matrix(channels)
    copies[0].wait()
    mean, spread = local_moments(
        images[...].astype(F32), groups, cells * (channels // GN_GROUPS)
    )
    one[0:cols] = images[pl.ds(start_one, cols)]
    three[0:cols] = images[pl.ds(start_three, cols)]
    copies[1].wait()
    odd = place[1]
    near, far = (1 - odd) * (cells - 2 * cols), odd * (cells - 2 * cols)
    one[cols : 3 * cols] = cotangent[pl.ds(pl.multiple_of(near, cols), 2 * cols)]
    three[cols : 3 * cols] = cotangent[pl.ds(pl.multiple_of(far, cols), 2 * cols)]
    block = terms(rows8(mean, spread))
    one[3 * cols :] = block
    two[...] = block
    three[3 * cols :] = block
    for copy in copies[2:]:
        copy.wait()


def embed_kernel(step, label, table, time_weight, time_bias, adaptive_weight, out):
    channels = adaptive_weight.shape[1] // 2
    half = time_weight.shape[0] // 2

    def times(vector, weights):
        product = jnp.dot(terms(rows8(vector)), weights, preferred_element_type=F32)
        return (product[0:8] + (product[8:16] + product[16:24]))[0:1]

    place = lax.broadcasted_iota(jnp.int32, (8, half), 1).astype(F32)
    angles = step[0].astype(F32) * jnp.exp(-math.log(10000.0) * place / half)
    sinusoid = jnp.concatenate([jnp.cos(angles), jnp.sin(angles)], axis=1)[0:1]
    classes = lax.broadcasted_iota(jnp.int32, (16, table.shape[0]), 1)
    onehot = (classes == label[0]).astype(F32).astype(BF16)
    row = jnp.dot(onehot, table[...], preferred_element_type=F32)[0:1]
    hidden = times(sinusoid, time_weight[...]) + time_bias[...]
    embedding = hidden * sigmoid(hidden) + row
    activated = embedding * sigmoid(embedding)
    partial = times(activated, adaptive_weight[...])
    out[...] = rows8(partial[:, :channels], partial[:, channels:], activated)


def second_kernel(dims, n_stats, images, one, three, weights, gain, bias, embed, *rest):
    cells, cols, channels, tiles = dims
    place = standing(tiles)
    stat_refs, (hidden, stat, out_one, out_two, out_three, padded) = rest[:n_stats], rest[n_stats:]
    count = cells * (channels // GN_GROUPS)
    mean, inverse = joint_moments(
        stat_list(stat_refs, (0, 3 * cols, 0, 3 * cols), tiles), count
    )
    stat[...] = rows8(mean, inverse)
    above, below = edges(place, one[0:cols], three[0:cols])

    def active(block):
        pre = (block.astype(F32) - mean) * inverse * gain[...] + bias[...]
        return pre * sigmoid(pre)

    padded[0:cols] = jnp.where(place[0] > 0, active(above), 0.0).astype(BF16)
    padded[cols : cols + cells] = active(images[...]).astype(BF16)
    padded[cols + cells :] = jnp.where(place[0] < tiles - 1, active(below), 0.0).astype(BF16)
    rounded = conv(padded, weights, cells, cols, False).astype(BF16)
    hidden[...] = rounded
    mean_two, spread_two = local_moments(rounded.astype(F32), group_matrix(channels), count)
    block = terms(rows8(mean_two, spread_two, embed[0:1], embed[1:2]))
    start_one, start_three = starts(place, cells, cols)
    out_one[0:cols] = hidden[pl.ds(start_one, cols)]
    out_three[0:cols] = hidden[pl.ds(start_three, cols)]
    out_one[cols:] = block
    out_two[...] = block
    out_three[cols:] = block


def turn_kernel(weights, turned, grouped):
    channels = weights.shape[1]
    unit = 1.0 * (lax.broadcasted_iota(jnp.int32, (channels, channels), 0) == lax.broadcasted_iota(jnp.int32, (channels, channels), 1))
    unit = unit.astype(BF16)
    picks = group_columns(channels, 0, GN_GROUPS, 0)
    for tap in range(weights.shape[0]):
        matrix = lax.dot_general(
            unit, weights[tap], (((1,), (1,)), ((), ())), preferred_element_type=F32
        ).astype(BF16)
        turned[tap] = matrix
        grouped[tap] = jnp.dot(picks, matrix, preferred_element_type=F32)


def group_columns(channels, offset, length, axis):
    size = (channels, length) if axis else (length, channels)
    shift = (channels // GN_GROUPS).bit_length() - 1
    channel = lax.broadcasted_iota(jnp.int32, size, 1 - axis)
    short = lax.broadcasted_iota(jnp.int32, size, axis)
    hit = lax.shift_right_logical(channel, shift) + offset == short
    return (1.0 * hit).astype(BF16)


def grad_kernel(dims, cotangent, one, three, weights, out, padded):
    cells, cols, channels, tiles = dims
    place = standing(tiles)
    above, below = edges(place, one[cols : 3 * cols], three[cols : 3 * cols])
    padded[0 : 2 * cols] = jnp.where(place[0] > 0, above, jnp.zeros_like(above))
    padded[2 * cols : 2 * cols + cells] = cotangent[...]
    padded[2 * cols + cells :] = jnp.where(place[0] < tiles - 1, below, jnp.zeros_like(below))
    out[...] = conv(padded, weights, cells + 2 * cols, cols, True)


def halves(values):
    high = values.astype(BF16)
    return high, (values - high.astype(F32)).astype(BF16)


def cross_kernel(
    dims, images, one, three, stat_one, gain, bias, hidden, turned, grouped, slope, moved, matrix, shifts
):
    cells, cols, channels, tiles = dims
    place = standing(tiles)
    above, below = edges(place, one[0:cols], three[0:cols])

    def pieces(block):
        normed = (block.astype(F32) - stat_one[0:1]) * stat_one[1:2]
        pre = normed * gain[...] + bias[...]
        gate = sigmoid(pre)
        grade = gate * (1.0 + pre * (1.0 - gate)) * gain[...]
        return grade, grade * normed

    own = pieces(images[...])
    slope[...], moved[...] = own
    top = [jnp.where(place[0] > 0, part, 0.0) for part in pieces(above)]
    bottom = [jnp.where(place[0] < tiles - 1, part, 0.0) for part in pieces(below)]
    for which in range(2):
        whole = jnp.concatenate([top[which], own[which], bottom[which]], axis=0)
        shifts[which, 0] = shifted(whole, cols, 1).astype(BF16)
        shifts[which, 1] = whole.astype(BF16)
        shifts[which, 2] = shifted(whole, cols, -1).astype(BF16)
    unit = 1.0 * (lax.broadcasted_iota(jnp.int32, (channels, channels), 0) == lax.broadcasted_iota(jnp.int32, (channels, channels), 1))
    hidden_turned = lax.dot_general(
        unit.astype(BF16), hidden[...], (((1,), (1,)), ((), ())), preferred_element_type=F32
    ).astype(BF16)
    spread = jnp.zeros((channels, 4 * GN_GROUPS), F32)
    flat = jnp.zeros((GN_GROUPS, 4 * GN_GROUPS), F32)
    for which in range(2):
        total, plain = None, None
        for j in range(3):
            lines = [
                jnp.sum(shifts[which, j, r * cols : (r + 1) * cols].astype(F32), axis=0, keepdims=True)
                for r in range(cells // cols + 2)
            ]
            for i in range(3):
                product = jnp.dot(
                    hidden_turned,
                    shifts[which, j, i * cols : i * cols + cells],
                    preferred_element_type=F32,
                ) * turned[3 * i + j].astype(F32)
                total = product if total is None else total + product
                line = grouped[3 * i + j] * tree_sum(lines[i : i + cells // cols])
                plain = line if plain is None else plain + line
        for part in halves(total):
            spread += jnp.dot(
                part, group_columns(channels, which * GN_GROUPS, 4 * GN_GROUPS, 1), preferred_element_type=F32
            )
        for part in halves(plain):
            flat += jnp.dot(
                part, group_columns(channels, (2 + which) * GN_GROUPS, 4 * GN_GROUPS, 1), preferred_element_type=F32
            )
    summed = jnp.sum(spread.reshape(GN_GROUPS, channels // GN_GROUPS, 4 * GN_GROUPS), axis=1)
    matrix[...] = jnp.concatenate(halves(summed + flat), axis=1)


def third_kernel(
    dims, n_stats, hidden, one, three, grad_active, adaptive_bias, turned, slope, moved, matrix, *rest
):
    cells, cols, channels, tiles = dims
    place = standing(tiles)
    stat_refs, (active, grad_norm, stat, out, padded) = rest[:n_stats], rest[n_stats:]
    count = cells * (channels // GN_GROUPS)
    stats = stat_list(stat_refs, (0, cols, 0, cols), tiles)
    mean, inverse = joint_moments(stats, count)
    modulation = tree_sum(stats)
    factor = 1.0 + (modulation[2:3] + adaptive_bias[:, :channels])
    shift = modulation[3:4] + adaptive_bias[:, channels:]
    stat[...] = rows8(mean, inverse, factor)
    above, below = edges(place, one[0:cols], three[0:cols])

    def piece(block, start, inside):
        stop = start + block.shape[0]
        normed = (block.astype(F32) - mean) * inverse
        pre = normed * factor + shift
        gate = sigmoid(pre)
        grad_pre = grad_active[start:stop] * (gate * (1.0 + pre * (1.0 - gate)))
        grad = grad_pre * factor
        grad_norm[start:stop] = grad
        result, scaled = pre * gate, grad * inverse
        if inside is not None:
            result, scaled = jnp.where(inside, result, 0.0), jnp.where(inside, scaled, 0.0)
        active[start:stop] = result.astype(BF16)
        padded[start:stop] = scaled.astype(BF16)
        return normed, grad_pre

    piece(above, 0, place[0] > 0)
    normed, grad_pre = piece(hidden[...], cols, None)
    piece(below, cols + cells, place[0] < tiles - 1)
    base = conv(padded, turned, cells, cols, True, True)
    out[0:STAT_ROWS] = terms(
        rows8(
            jnp.sum(grad_pre * normed, axis=0, keepdims=True),
            jnp.sum(grad_pre, axis=0, keepdims=True),
            jnp.sum(base * slope[...], axis=0, keepdims=True),
            jnp.sum(base * moved[...], axis=0, keepdims=True),
        )
    )
    out[STAT_ROWS:] = matrix[...]


def pairs_kernel(dims, n_stats, embed, *rest):
    cells, cols, channels, tiles = dims
    sums = tree_sum(stat_list(rest[:n_stats], (0, 0, 0, 0), tiles))
    rest[n_stats][...] = rows8(sums[0:1], sums[1:2], embed[2:3])


def branch_kernel(dims, active, weights, out, token):
    cells, cols, channels, tiles = dims
    out[...] = conv(active, weights, cells, cols, False).astype(BF16)
    token[...] = jnp.zeros_like(token)


def fourth_kernel(
    dims, n_stats, token, grad_norm, hidden, one, three, stat_two, turned, images, stat_one, slope, *rest
):
    cells, cols, channels, tiles = dims
    place = standing(tiles)
    stat_refs, (out, padded) = rest[:n_stats], rest[n_stats:]
    total = cells * (channels // GN_GROUPS) * tiles
    if len(stat_refs) == 1:
        size = stat_refs[0].shape[0] // tiles
        blocks = [stat_refs[0][size * t + STAT_ROWS : size * (t + 1)] for t in range(tiles)]
    else:
        blocks = [ref[STAT_ROWS:] for ref in stat_refs]
    width = 4 * GN_GROUPS
    matrix = tree_sum([b[:, :width].astype(F32) + b[:, width:].astype(F32) for b in blocks])
    sums = tree_sum(stat_list(stat_refs, (0, 0, 0, 0), tiles))
    mean, inverse, factor = stat_two[0:1], stat_two[1:2], stat_two[2:3]
    row = lax.broadcasted_iota(jnp.int32, (8, channels), 0)
    reduced = group_sums(jnp.where(row < 2, sums * factor, sums), group_matrix(channels))
    paired, plain = reduced[0:1] / total, reduced[1:2] / total
    above, below = edges(place, one[0:cols], three[0:cols])

    def grad_hidden(grad, block):
        normed = (block.astype(F32) - mean) * inverse
        return inverse * (grad - plain - normed * paired)

    padded[0:cols] = jnp.where(place[0] > 0, grad_hidden(grad_norm[0:cols], above), 0.0).astype(BF16)
    padded[cols : cols + cells] = grad_hidden(grad_norm[cols : cols + cells], hidden[...]).astype(BF16)
    padded[cols + cells :] = jnp.where(
        place[0] < tiles - 1, grad_hidden(grad_norm[cols + cells :], below), 0.0
    ).astype(BF16)
    grad = conv(padded, turned, cells, cols, True, True) * slope[...]
    beta = paired * inverse * inverse
    alpha = plain * inverse - beta * mean
    per = channels // GN_GROUPS
    weights = terms(rows8(alpha / per, beta / per))
    picked = jnp.dot(weights, group_columns(channels, 0, GN_GROUPS, 1), preferred_element_type=F32)
    picked = picked[0:8] + (picked[8:16] + picked[16:24])
    found = jnp.dot(picked, matrix, precision=lax.Precision.HIGHEST, preferred_element_type=F32)
    found = terms(rows8(pltpu.roll(found, width // 2, 1)[0:1] + found[1:2]))
    means = []
    for which in range(2):
        back = jnp.dot(
            found, group_columns(channels, which * GN_GROUPS, width, 0), preferred_element_type=F32
        )
        back = back[0:8] + (back[8:16] + back[16:24])
        means.append((reduced[2 + which : 3 + which] - back[0:1]) / total)
    normed = (images[...].astype(F32) - stat_one[0:1]) * stat_one[1:2]
    out[...] = (stat_one[1:2] * (grad - means[0] - normed * means[1])).astype(BF16)


def weight_kernel(*rest):
    pair_refs, (weight, bias) = rest[:-2], rest[-2:]
    if len(pair_refs) == 1:
        blocks = [pair_refs[0][8 * n : 8 * n + 8] for n in range(pair_refs[0].shape[0] // 8)]
        places = list(range(len(blocks)))
    else:
        blocks = [ref[...] for ref in pair_refs]
        places = [lax.bitwise_xor(lax.axis_index("image"), k) for k in range(len(blocks))]
    count = -(-len(blocks) // 8) * 8
    channels = blocks[0].shape[1]
    row = lax.broadcasted_iota(jnp.int32, (count, channels), 0)

    def ordered(which):
        out = jnp.zeros((count, channels), F32)
        for block, place in zip(blocks, places, strict=True):
            out = jnp.where(row == place, jnp.broadcast_to(block[which : which + 1], out.shape), out)
        return out

    scale, shift, activated = ordered(0), ordered(1), ordered(2)
    for start, part in ((0, scale), (channels, shift)):
        weight[:, start : start + channels] = lax.dot_general(
            activated,
            part,
            (((0,), (0,)), ((), ())),
            precision=lax.Precision.HIGHEST,
            preferred_element_type=F32,
        )
        bias[:, start : start + channels] = jnp.sum(part, axis=0, keepdims=True)


def call(kernel, out_shapes, operands, scratch=(), flops=1000, name=None, spaces=None):
    size = sum(o.size * o.dtype.itemsize for o in operands)
    return pl.pallas_call(
        kernel,
        out_shape=out_shapes,
        in_specs=[
            pl.BlockSpec(memory_space=(spaces or {}).get(k, pltpu.VMEM)) for k in range(len(operands))
        ],
        out_specs=jax.tree.map(lambda _: pl.BlockSpec(memory_space=pltpu.VMEM), out_shapes),
        scratch_shapes=list(scratch),
        compiler_params=pltpu.CompilerParams(vmem_limit_bytes=VMEM_LIMIT),
        cost_estimate=pl.CostEstimate(flops=flops, bytes_accessed=size, transcendentals=0),
        name=name,
    )(*operands)


def swap(values, axis, size, distance):
    return lax.ppermute(values, axis, [(i, i ^ distance) for i in range(size)])


def exchange(one, two, three):
    tiles = lax.axis_size("tile")
    if tiles == 4:
        got = [swap(part, "tile", tiles, k + 1) for k, part in enumerate((one, two, three))]
        return got[0], got[2], [two, *got]
    ahead = [(i, (i + 1) % tiles) for i in range(tiles)]
    behind = [(target, source) for source, target in ahead]
    below, above = lax.ppermute(three, "tile", behind), lax.ppermute(one, "tile", ahead)
    return below, above, [lax.all_gather(two, "tile", axis=0, tiled=True)]


def spread_small(block):
    tiles = lax.axis_size("tile")
    if tiles == 4:
        return [block, *(swap(block, "tile", tiles, k) for k in (1, 2, 3))]
    return [lax.all_gather(block, "tile", axis=0, tiled=True)]


def body(
    images,
    cotangent,
    timesteps,
    class_ids,
    norm_gain,
    norm_bias,
    conv_first,
    conv_second,
    time_weight,
    time_bias,
    class_table,
    adaptive_weight,
    adaptive_bias,
):
    _, rows, cols, channels = images.shape
    tiles, fleet = lax.axis_size("tile"), lax.axis_size("image")
    cells = rows * cols
    dims = (cells, cols, channels, tiles)
    shape = jax.ShapeDtypeStruct
    conv_flops = 18 * cells * channels * channels
    padded = pltpu.VMEM((cells + 2 * cols, channels), BF16)
    small = shape((STAT_ROWS, channels), BF16)
    halo = shape((cols + STAT_ROWS, channels), BF16)
    halos = shape((3 * cols + STAT_ROWS, channels), BF16)
    block = shape((8, channels), F32)
    wide = shape((cells, channels), F32)
    narrow = shape((cells, channels), BF16)

    width = adaptive_weight.shape[0]
    spare = channels - width
    time_bias, mix = time_bias[None], adaptive_weight
    if spare:
        time_weight, time_bias, class_table = (
            jnp.pad(part, ((0, 0), (0, spare))) for part in (time_weight, time_bias, class_table)
        )
        mix = jnp.pad(mix, ((0, spare), (0, 0)))
    loads = (
        images.reshape(cells, channels),
        cotangent.reshape(cells, channels),
        time_weight,
        mix,
        class_table,
        time_bias,
        norm_gain[None],
        norm_bias[None],
        adaptive_bias[None],
        conv_first.reshape(9, channels, channels),
        conv_second.reshape(9, channels, channels),
    )
    spaces = {k: pl.ANY for k in range(len(loads))}
    *held, one, two, three = call(
        functools.partial(first_kernel, dims),
        (*(shape(part.shape, part.dtype) for part in loads), halos, small, halos),
        tuple(pltpu.with_memory_space_constraint(part, pltpu.HBM) for part in loads),
        (pltpu.SemaphoreType.DMA((len(loads),)),),
        name="first",
        spaces=spaces,
    )
    flat, flat_cot, time_weight, mix, class_table, time_bias, gain, bias, adaptive_bias, weights_first, weights_second = held
    image_one, image_three, stats = exchange(one, two, three)
    turned, grouped = call(
        turn_kernel,
        (shape((9, channels, channels), BF16), shape((9, GN_GROUPS, channels), F32)),
        (weights_first,),
        flops=conv_flops,
        name="turn",
    )
    embed = call(
        embed_kernel,
        block,
        (timesteps, class_ids, class_table, time_weight, time_bias, mix),
        name="embed",
        spaces={0: pltpu.SMEM, 1: pltpu.SMEM},
    )

    hidden, stat_one, one, two, three = call(
        functools.partial(second_kernel, dims, len(stats)),
        (narrow, block, halo, small, halo),
        (flat, image_one, image_three, weights_first, gain, bias, embed, *stats),
        (padded,),
        conv_flops,
        name="second",
    )
    hidden_one, hidden_three, stats = exchange(one, two, three)
    grad_active = call(
        functools.partial(grad_kernel, dims),
        shape((cells + 2 * cols, channels), F32),
        (flat_cot, image_one, image_three, weights_second),
        (pltpu.VMEM((cells + 4 * cols, channels), BF16),),
        conv_flops,
        name="grad",
    )
    slope, moved, matrix = call(
        functools.partial(cross_kernel, dims),
        (wide, wide, shape((GN_GROUPS, 8 * GN_GROUPS), BF16)),
        (flat, image_one, image_three, stat_one, gain, bias, hidden, turned, grouped),
        (pltpu.VMEM((2, 3, cells + 2 * cols, channels), BF16),),
        conv_flops,
        name="cross",
    )
    active, grad_norm, stat_two, message = call(
        functools.partial(third_kernel, dims, len(stats)),
        (
            shape((cells + 2 * cols, channels), BF16),
            shape((cells + 2 * cols, channels), F32),
            block,
            shape((STAT_ROWS + GN_GROUPS, channels), BF16),
        ),
        (hidden, hidden_one, hidden_three, grad_active, adaptive_bias, turned, slope, moved, matrix, *stats),
        (padded,),
        conv_flops,
        name="third",
    )
    stats = spread_small(message)
    branch, token = call(
        functools.partial(branch_kernel, dims),
        (narrow, shape((8, 128), F32)),
        (active, weights_second),
        flops=conv_flops,
        name="branch",
    )
    pairs = call(
        functools.partial(pairs_kernel, dims, len(stats)), block, (embed, *stats), name="pairs"
    )
    if fleet == 4:
        pair_list = [pairs, *(swap(pairs, "image", fleet, k) for k in (1, 2, 3))]
    else:
        pair_list = [lax.all_gather(pairs, "image", axis=0, tiled=True)]
    input_grad = call(
        functools.partial(fourth_kernel, dims, len(stats)),
        narrow,
        (token, grad_norm, hidden, hidden_one, hidden_three, stat_two, turned, flat, stat_one, slope, *stats),
        (padded,),
        conv_flops,
        name="fourth",
    )
    grad_weight, grad_bias = call(
        weight_kernel,
        (shape((channels, 2 * channels), F32), shape((1, 2 * channels), F32)),
        tuple(pair_list),
        name="weight",
    )
    return (
        branch.reshape(images.shape),
        input_grad.reshape(images.shape),
        grad_weight[:width],
        grad_bias[0],
    )


def solution(mesh):
    return jax.shard_map(
        body,
        mesh=mesh,
        in_specs=(
            P(("groups", "image"), "tile", None, None),
            P(("groups", "image"), "tile", None, None),
            P(("groups", "image")),
            P(("groups", "image")),
            P(),
            P(),
            P(),
            P(),
            P(None, "tile"),
            P("tile"),
            P(None, "tile"),
            P("tile", None),
            P(),
        ),
        out_specs=(
            P(("groups", "image"), "tile", None, None),
            P(("groups", "image"), "tile", None, None),
            P(("groups", "tile"), None),
            P("groups"),
        ),
        check_vma=False,
    )
```

```python
import functools
import math

import jax
import jax.numpy as jnp
from jax import lax
from jax.experimental import pallas as pl
from jax.experimental.pallas import tpu as pltpu
from jax.sharding import PartitionSpec as P

GN_GROUPS = 32
EPSILON = 1e-05
VMEM_LIMIT = 12 * 1024 * 1024
F32, BF16 = jnp.float32, jnp.bfloat16

STAT_ROWS = 16


def split(values):
    high = values.astype(BF16).astype(F32)
    rest = values - high
    middle = rest.astype(BF16).astype(F32)
    return high, middle, (rest - middle).astype(BF16).astype(F32)


def terms(values):
    high, middle, low = split(values)
    return jnp.concatenate([high + pltpu.roll(middle, 4, 0), low], axis=0).astype(BF16)


def joined(block):
    wide = block.astype(F32)
    total = wide[0:8] + (pltpu.roll(wide[0:8], 4, 0) + wide[8:16])
    return jnp.where(lax.broadcasted_iota(jnp.int32, total.shape, 0) < 4, total, 0.0)


def rows8(*rows):
    width = rows[0].shape[1]
    index = lax.broadcasted_iota(jnp.int32, (8, width), 0)
    out = jnp.zeros((8, width), F32)
    for place, row in enumerate(rows):
        out = jnp.where(index == place, jnp.broadcast_to(row, (8, width)), out)
    return out


def group_matrix(channels):
    shift = (channels // GN_GROUPS).bit_length() - 1
    row = lax.shift_right_logical(lax.broadcasted_iota(jnp.int32, (channels, channels), 0), shift)
    col = lax.shift_right_logical(lax.broadcasted_iota(jnp.int32, (channels, channels), 1), shift)
    return (row == col).astype(F32).astype(BF16)


def group_sums(rows, groups):
    return joined(jnp.dot(terms(rows), groups, preferred_element_type=F32))


def tree_sum(parts):
    parts = list(parts)
    while len(parts) > 1:
        parts = [
            parts[i] + parts[i + 1] if i + 1 < len(parts) else parts[i]
            for i in range(0, len(parts), 2)
        ]
    return parts[0]


def local_moments(values, groups, count):
    mean = group_sums(rows8(jnp.sum(values, axis=0, keepdims=True)), groups)[0:1] / count
    centred = values - mean
    spread = group_sums(rows8(jnp.sum(centred * centred, axis=0, keepdims=True)), groups)[0:1]
    return mean, spread


def joint_moments(stats, count):
    tiles = len(stats)
    mean = tree_sum([s[0:1] for s in stats]) / tiles
    spread = tree_sum([s[1:2] + count * (s[0:1] - mean) * (s[0:1] - mean) for s in stats])
    return mean, lax.rsqrt(spread / (count * tiles) + EPSILON)


def sigmoid(values):
    return 1.0 / (1.0 + jnp.exp(-values))


def column_index(cells, cols, channels):
    index = lax.broadcasted_iota(jnp.int32, (cells, channels), 0)
    return lax.bitwise_and(index, cols - 1)


def conv(padded_ref, kernel_ref, cells, cols, flipped, turned=False):
    parts = []
    for j in range(3):
        total = None
        for i in range(3):
            start = (2 - i if flipped else i) * cols
            product = lax.dot_general(
                padded_ref[start : start + cells],
                kernel_ref[3 * i + j],
                (((1,), (1 if flipped and not turned else 0,)), ((), ())),
                preferred_element_type=F32,
            )
            total = product if total is None else total + product
        parts.append(total)
    if flipped:
        parts = parts[::-1]
    return parts[1] + (shifted(parts[0], cols, 1) + shifted(parts[2], cols, -1))


def shifted(values, cols, step):
    cells = values.shape[0]
    column = column_index(cells, cols, values.shape[1])
    if step == 1:
        return jnp.where(column == 0, 0.0, pltpu.roll(values, 1, 0))
    return jnp.where(column == cols - 1, 0.0, pltpu.roll(values, cells - 1, 0))


def stat_list(refs, start, tiles):
    if len(refs) == 1:
        size = refs[0].shape[0] // tiles
        return [joined(refs[0][size * t : size * t + STAT_ROWS]) for t in range(tiles)]
    return [joined(ref[s : s + STAT_ROWS]) for ref, s in zip(refs, start, strict=True)]


def standing(tiles):
    tile = lax.axis_index("tile")
    return tile, lax.bitwise_and(tile, 1) if tiles == 4 else 0 * tile


def edges(place, one, three):
    odd = place[1] == 1
    return jnp.where(odd, one, three), jnp.where(odd, three, one)


def starts(place, cells, cols):
    odd = place[1]
    first = pl.multiple_of((1 - odd) * (cells - cols), cols)
    third = pl.multiple_of(odd * (cells - cols), cols)
    return first, third


def first_kernel(dims, *refs):
    cells, cols, channels, tiles = dims
    count = (len(refs) - 4) // 2
    sources, copies_to = refs[:count], refs[count : 2 * count]
    one, two, three, sems = refs[2 * count :]
    copies = [
        pltpu.make_async_copy(source, target, sems.at[k])
        for k, (source, target) in enumerate(zip(sources, copies_to, strict=True))
    ]
    for copy in copies:
        copy.start()
    images, cotangent = copies_to[:2]
    place = standing(tiles)
    start_one, start_three = starts(place, cells, cols)
    groups = group_matrix(channels)
    copies[0].wait()
    mean, spread = local_moments(
        images[...].astype(F32), groups, cells * (channels // GN_GROUPS)
    )
    one[0:cols] = images[pl.ds(start_one, cols)]
    three[0:cols] = images[pl.ds(start_three, cols)]
    copies[1].wait()
    odd = place[1]
    near, far = (1 - odd) * (cells - 2 * cols), odd * (cells - 2 * cols)
    one[cols : 3 * cols] = cotangent[pl.ds(pl.multiple_of(near, cols), 2 * cols)]
    three[cols : 3 * cols] = cotangent[pl.ds(pl.multiple_of(far, cols), 2 * cols)]
    block = terms(rows8(mean, spread))
    one[3 * cols :] = block
    two[...] = block
    three[3 * cols :] = block
    for copy in copies[2:]:
        copy.wait()


def embed_kernel(instant, table, time_weight, time_bias, adaptive_weight, out):
    channels = adaptive_weight.shape[1] // 2
    half = time_weight.shape[0] // 2

    def times(vector, weights):
        return joined(jnp.dot(terms(rows8(vector)), weights, preferred_element_type=F32))[0:1]

    place = lax.broadcasted_iota(jnp.int32, (8, half), 1).astype(F32)
    angles = instant[0:1, 0:1].astype(F32) * jnp.exp(-math.log(10000.0) * place / half)
    sinusoid = jnp.concatenate([jnp.cos(angles), jnp.sin(angles)], axis=1)[0:1]
    classes = lax.broadcasted_iota(jnp.int32, (16, table.shape[0]), 1)
    onehot = (classes == instant[1:2, 0:1]).astype(F32).astype(BF16)
    row = jnp.dot(onehot, table[...], preferred_element_type=F32)[0:1]
    hidden = times(sinusoid, time_weight[...]) + time_bias[...]
    embedding = hidden * sigmoid(hidden) + row
    activated = embedding * sigmoid(embedding)
    partial = times(activated, adaptive_weight[...])
    out[...] = rows8(partial[:, :channels], partial[:, channels:], activated)


def second_kernel(dims, n_stats, images, one, three, weights, gain, bias, embed, *rest):
    cells, cols, channels, tiles = dims
    place = standing(tiles)
    stat_refs, (hidden, stat, out_one, out_two, out_three, padded) = rest[:n_stats], rest[n_stats:]
    count = cells * (channels // GN_GROUPS)
    mean, inverse = joint_moments(
        stat_list(stat_refs, (0, 3 * cols, 0, 3 * cols), tiles), count
    )
    stat[...] = rows8(mean, inverse)
    above, below = edges(place, one[0:cols], three[0:cols])

    def active(block):
        pre = (block.astype(F32) - mean) * inverse * gain[...] + bias[...]
        return pre * sigmoid(pre)

    padded[0:cols] = jnp.where(place[0] > 0, active(above), 0.0).astype(BF16)
    padded[cols : cols + cells] = active(images[...]).astype(BF16)
    padded[cols + cells :] = jnp.where(place[0] < tiles - 1, active(below), 0.0).astype(BF16)
    rounded = conv(padded, weights, cells, cols, False).astype(BF16)
    hidden[...] = rounded
    mean_two, spread_two = local_moments(rounded.astype(F32), group_matrix(channels), count)
    block = terms(rows8(mean_two, spread_two, embed[0:1], embed[1:2]))
    start_one, start_three = starts(place, cells, cols)
    out_one[0:cols] = hidden[pl.ds(start_one, cols)]
    out_three[0:cols] = hidden[pl.ds(start_three, cols)]
    out_one[cols:] = block
    out_two[...] = block
    out_three[cols:] = block


def identity(size):
    row = lax.broadcasted_iota(jnp.int32, (size, size), 0)
    return (1.0 * (row == lax.broadcasted_iota(jnp.int32, (size, size), 1))).astype(BF16)


def turn_kernel(count, source, *refs):
    sources, weights, copies_to = refs[:count], refs[count], refs[count + 1 : 2 * count + 1]
    turned, grouped, sems = refs[2 * count + 1 :]
    main = pltpu.make_async_copy(source, weights, sems.at[count])
    copies = [
        pltpu.make_async_copy(start, end, sems.at[k])
        for k, (start, end) in enumerate(zip(sources, copies_to, strict=True))
    ]
    for copy in (main, *copies):
        copy.start()
    channels = weights.shape[1]
    rows = jnp.concatenate([identity(channels), group_columns(channels, 0, GN_GROUPS, 0)], axis=0)
    main.wait()
    for k in range(source.shape[0]):
        product = lax.dot_general(
            rows, weights[k], (((1,), (1,)), ((), ())), preferred_element_type=F32
        )
        turned[k] = product[:channels].astype(BF16)
        grouped[k] = product[channels:]
    for copy in copies:
        copy.wait()


def group_columns(channels, offset, length, axis):
    size = (channels, length) if axis else (length, channels)
    shift = (channels // GN_GROUPS).bit_length() - 1
    channel = lax.broadcasted_iota(jnp.int32, size, 1 - axis)
    short = lax.broadcasted_iota(jnp.int32, size, axis)
    hit = lax.shift_right_logical(channel, shift) + offset == short
    return (1.0 * hit).astype(BF16)


def grad_kernel(dims, cotangent, one, three, weights, out, padded):
    cells, cols, channels, tiles = dims
    place = standing(tiles)
    above, below = edges(place, one[cols : 3 * cols], three[cols : 3 * cols])
    padded[0 : 2 * cols] = jnp.where(place[0] > 0, above, jnp.zeros_like(above))
    padded[2 * cols : 2 * cols + cells] = cotangent[...]
    padded[2 * cols + cells :] = jnp.where(place[0] < tiles - 1, below, jnp.zeros_like(below))
    out[...] = conv(padded, weights, cells + 2 * cols, cols, True)


def halves(values):
    high = values.astype(BF16)
    return high, (values - high.astype(F32)).astype(BF16)


def cross_kernel(
    dims, images, one, three, stat_one, gain, bias, hidden, turned, grouped, slope, moved, matrix, factors, left, products
):
    cells, cols, channels, tiles = dims
    place = standing(tiles)
    above, below = edges(place, one[0:cols], three[0:cols])

    def pieces(block):
        normed = (block.astype(F32) - stat_one[0:1]) * stat_one[1:2]
        pre = normed * gain[...] + bias[...]
        gate = sigmoid(pre)
        grade = gate * (1.0 + pre * (1.0 - gate)) * gain[...]
        return grade, grade * normed

    own = pieces(images[...])
    slope[...], moved[...] = own
    for which, (top, bottom) in enumerate(zip(pieces(above), pieces(below), strict=True)):
        factors[which, 0:cols] = jnp.where(place[0] > 0, top, 0.0).astype(BF16)
        factors[which, cols : cols + cells] = own[which].astype(BF16)
        factors[which, cols + cells :] = jnp.where(place[0] < tiles - 1, bottom, 0.0).astype(BF16)
    wide = hidden[...].astype(F32)
    unit = identity(channels)
    for j, line in enumerate((shifted(wide, cols, -1).astype(BF16), hidden[...], shifted(wide, cols, 1).astype(BF16))):
        left[j * channels : (j + 1) * channels] = lax.dot_general(
            unit, line, (((1,), (1,)), ((), ())), preferred_element_type=F32
        ).astype(BF16)
    row = lax.broadcasted_iota(jnp.int32, (16, cells), 0)
    column = lax.bitwise_and(lax.broadcasted_iota(jnp.int32, (16, cells), 1), cols - 1)
    inside = jnp.where(row == 0, 1.0 * (column < cols - 1), jnp.where(row == 2, 1.0 * (column > 0), 1.0))
    left[3 * channels :] = inside.astype(BF16)
    for i in range(3):
        for which in range(2):
            products[which, i] = jnp.dot(
                left[...], factors[which, i * cols : i * cols + cells], preferred_element_type=F32
            )
    step = channels // 8
    totals = ([], [])
    for start in range(0, channels, step):
        parts = ([], [])
        for k in range(9):
            matrix_rows = turned[k, start : start + step].astype(F32)
            for which in range(2):
                begin = (k % 3) * channels + start
                parts[which].append(products[which, k // 3, begin : begin + step] * matrix_rows)
        for which in range(2):
            totals[which].append(tree_sum(parts[which]))
    spread = jnp.zeros((channels, 4 * GN_GROUPS), F32)
    flat = jnp.zeros((GN_GROUPS, 4 * GN_GROUPS), F32)
    for which in range(2):
        total = jnp.concatenate(totals[which], axis=0)
        plain = tree_sum(
            [
                grouped[k] * products[which, k // 3, 3 * channels + k % 3 : 3 * channels + k % 3 + 1]
                for k in range(9)
            ]
        )
        for part in halves(total):
            spread += jnp.dot(
                part, group_columns(channels, which * GN_GROUPS, 4 * GN_GROUPS, 1), preferred_element_type=F32
            )
        for part in halves(plain):
            flat += jnp.dot(
                part, group_columns(channels, (2 + which) * GN_GROUPS, 4 * GN_GROUPS, 1), preferred_element_type=F32
            )
    summed = jnp.sum(spread.reshape(GN_GROUPS, channels // GN_GROUPS, 4 * GN_GROUPS), axis=1)
    matrix[...] = jnp.concatenate(halves(summed + flat), axis=1)


def third_kernel(
    dims, n_stats, hidden, one, three, grad_active, adaptive_bias, turned, slope, moved, matrix, *rest
):
    cells, cols, channels, tiles = dims
    place = standing(tiles)
    stat_refs, (active, grad_norm, stat, out, padded) = rest[:n_stats], rest[n_stats:]
    count = cells * (channels // GN_GROUPS)
    stats = stat_list(stat_refs, (0, cols, 0, cols), tiles)
    mean, inverse = joint_moments(stats, count)
    modulation = tree_sum(stats)
    factor = 1.0 + (modulation[2:3] + adaptive_bias[:, :channels])
    shift = modulation[3:4] + adaptive_bias[:, channels:]
    stat[...] = rows8(mean, inverse, factor)
    above, below = edges(place, one[0:cols], three[0:cols])

    def piece(block, start, inside):
        stop = start + block.shape[0]
        normed = (block.astype(F32) - mean) * inverse
        pre = normed * factor + shift
        gate = sigmoid(pre)
        grad_pre = grad_active[start:stop] * (gate * (1.0 + pre * (1.0 - gate)))
        grad = grad_pre * factor
        grad_norm[start:stop] = grad
        result, scaled = pre * gate, grad * inverse
        if inside is not None:
            result, scaled = jnp.where(inside, result, 0.0), jnp.where(inside, scaled, 0.0)
        active[start:stop] = result.astype(BF16)
        padded[start:stop] = scaled.astype(BF16)
        return normed, grad_pre

    piece(above, 0, place[0] > 0)
    normed, grad_pre = piece(hidden[...], cols, None)
    piece(below, cols + cells, place[0] < tiles - 1)
    base = conv(padded, turned, cells, cols, True, True)
    out[0:STAT_ROWS] = terms(
        rows8(
            jnp.sum(grad_pre * normed, axis=0, keepdims=True),
            jnp.sum(grad_pre, axis=0, keepdims=True),
            jnp.sum(base * slope[...], axis=0, keepdims=True),
            jnp.sum(base * moved[...], axis=0, keepdims=True),
        )
    )
    out[STAT_ROWS:] = matrix[...]


def pairs_kernel(dims, n_stats, embed, *rest):
    cells, cols, channels, tiles = dims
    sums = tree_sum(stat_list(rest[:n_stats], (0, 0, 0, 0), tiles))
    rest[n_stats][...] = rows8(sums[0:1], sums[1:2], embed[2:3])


def branch_kernel(dims, active, weights, out, token):
    cells, cols, channels, tiles = dims
    out[...] = conv(active, weights, cells, cols, False).astype(BF16)
    token[...] = jnp.zeros_like(token)


def fourth_kernel(
    dims, n_stats, token, grad_norm, hidden, one, three, stat_two, turned, images, stat_one, slope, *rest
):
    cells, cols, channels, tiles = dims
    place = standing(tiles)
    stat_refs, (out, padded) = rest[:n_stats], rest[n_stats:]
    total = cells * (channels // GN_GROUPS) * tiles
    if len(stat_refs) == 1:
        size = stat_refs[0].shape[0] // tiles
        blocks = [stat_refs[0][size * t + STAT_ROWS : size * (t + 1)] for t in range(tiles)]
    else:
        blocks = [ref[STAT_ROWS:] for ref in stat_refs]
    width = 4 * GN_GROUPS
    matrix = tree_sum([b[:, :width].astype(F32) + b[:, width:].astype(F32) for b in blocks])
    sums = tree_sum(stat_list(stat_refs, (0, 0, 0, 0), tiles))
    mean, inverse, factor = stat_two[0:1], stat_two[1:2], stat_two[2:3]
    row = lax.broadcasted_iota(jnp.int32, (8, channels), 0)
    reduced = group_sums(jnp.where(row < 2, sums * factor, sums), group_matrix(channels))
    paired, plain = reduced[0:1] / total, reduced[1:2] / total
    above, below = edges(place, one[0:cols], three[0:cols])

    def grad_hidden(grad, block):
        normed = (block.astype(F32) - mean) * inverse
        return inverse * (grad - plain - normed * paired)

    padded[0:cols] = jnp.where(place[0] > 0, grad_hidden(grad_norm[0:cols], above), 0.0).astype(BF16)
    padded[cols : cols + cells] = grad_hidden(grad_norm[cols : cols + cells], hidden[...]).astype(BF16)
    padded[cols + cells :] = jnp.where(
        place[0] < tiles - 1, grad_hidden(grad_norm[cols + cells :], below), 0.0
    ).astype(BF16)
    grad = conv(padded, turned, cells, cols, True, True) * slope[...]
    beta = paired * inverse * inverse
    alpha = plain * inverse - beta * mean
    per = channels // GN_GROUPS
    weights = terms(rows8(alpha / per, beta / per))
    picked = joined(
        jnp.dot(weights, group_columns(channels, 0, GN_GROUPS, 1), preferred_element_type=F32)
    )
    found = jnp.dot(picked, matrix, precision=lax.Precision.HIGHEST, preferred_element_type=F32)
    found = terms(rows8(pltpu.roll(found, width // 2, 1)[0:1] + found[1:2]))
    means = []
    for which in range(2):
        back = joined(
            jnp.dot(found, group_columns(channels, which * GN_GROUPS, width, 0), preferred_element_type=F32)
        )
        means.append((reduced[2 + which : 3 + which] - back[0:1]) / total)
    normed = (images[...].astype(F32) - stat_one[0:1]) * stat_one[1:2]
    out[...] = (stat_one[1:2] * (grad - means[0] - normed * means[1])).astype(BF16)


def weight_kernel(*rest):
    pair_refs, (weight, bias) = rest[:-2], rest[-2:]
    if len(pair_refs) == 1:
        blocks = [pair_refs[0][8 * n : 8 * n + 8] for n in range(pair_refs[0].shape[0] // 8)]
        places = list(range(len(blocks)))
    else:
        blocks = [ref[...] for ref in pair_refs]
        places = [lax.bitwise_xor(lax.axis_index("image"), k) for k in range(len(blocks))]
    count = -(-len(blocks) // 8) * 8
    channels = blocks[0].shape[1]
    row = lax.broadcasted_iota(jnp.int32, (count, channels), 0)

    def ordered(which):
        out = jnp.zeros((count, channels), F32)
        for block, place in zip(blocks, places, strict=True):
            out = jnp.where(row == place, jnp.broadcast_to(block[which : which + 1], out.shape), out)
        return out

    activated = split(ordered(2))
    left = jnp.concatenate([activated[k] for k in (0, 0, 1, 0, 2, 1)], axis=0).astype(BF16)
    for start, which in ((0, 0), (channels, 1)):
        part = ordered(which)
        pieces = split(part)
        right = jnp.concatenate([pieces[k] for k in (0, 1, 0, 2, 0, 1)], axis=0).astype(BF16)
        weight[:, start : start + channels] = lax.dot_general(
            left, right, (((0,), (0,)), ((), ())), preferred_element_type=F32
        )
        bias[:, start : start + channels] = jnp.sum(part, axis=0, keepdims=True)


def call(kernel, out_shapes, operands, scratch=(), flops=1000, name=None, spaces=None):
    size = sum(o.size * o.dtype.itemsize for o in operands)
    return pl.pallas_call(
        kernel,
        out_shape=out_shapes,
        in_specs=[
            pl.BlockSpec(memory_space=(spaces or {}).get(k, pltpu.VMEM)) for k in range(len(operands))
        ],
        out_specs=jax.tree.map(lambda _: pl.BlockSpec(memory_space=pltpu.VMEM), out_shapes),
        scratch_shapes=list(scratch),
        compiler_params=pltpu.CompilerParams(vmem_limit_bytes=VMEM_LIMIT),
        cost_estimate=pl.CostEstimate(flops=flops, bytes_accessed=size, transcendentals=0),
        name=name,
    )(*operands)


def swap(values, axis, size, distance):
    return lax.ppermute(values, axis, [(i, i ^ distance) for i in range(size)])


def exchange(one, two, three):
    tiles = lax.axis_size("tile")
    if tiles == 4:
        got = [swap(part, "tile", tiles, k + 1) for k, part in enumerate((one, two, three))]
        return got[0], got[2], [two, *got]
    ahead = [(i, (i + 1) % tiles) for i in range(tiles)]
    behind = [(target, source) for source, target in ahead]
    below, above = lax.ppermute(three, "tile", behind), lax.ppermute(one, "tile", ahead)
    return below, above, [lax.all_gather(two, "tile", axis=0, tiled=True)]


def spread_small(block):
    tiles = lax.axis_size("tile")
    if tiles == 4:
        return [block, *(swap(block, "tile", tiles, k) for k in (1, 2, 3))]
    return [lax.all_gather(block, "tile", axis=0, tiled=True)]


def body(
    images,
    cotangent,
    timesteps,
    class_ids,
    norm_gain,
    norm_bias,
    conv_first,
    conv_second,
    time_weight,
    time_bias,
    class_table,
    adaptive_weight,
    adaptive_bias,
):
    _, rows, cols, channels = images.shape
    tiles, fleet = lax.axis_size("tile"), lax.axis_size("image")
    cells = rows * cols
    dims = (cells, cols, channels, tiles)
    shape = jax.ShapeDtypeStruct
    conv_flops = 18 * cells * channels * channels
    padded = pltpu.VMEM((cells + 2 * cols, channels), BF16)
    small = shape((STAT_ROWS, channels), BF16)
    halo = shape((cols + STAT_ROWS, channels), BF16)
    halos = shape((3 * cols + STAT_ROWS, channels), BF16)
    block = shape((8, channels), F32)
    wide = shape((cells, channels), F32)
    narrow = shape((cells, channels), BF16)

    width = adaptive_weight.shape[0]
    spare = channels - width
    time_bias, mix = time_bias[None], adaptive_weight
    if spare:
        time_weight, time_bias, class_table = (
            jnp.pad(part, ((0, 0), (0, spare))) for part in (time_weight, time_bias, class_table)
        )
        mix = jnp.pad(mix, ((0, spare), (0, 0)))
    pin = lambda part: pltpu.with_memory_space_constraint(part, pltpu.HBM)
    like = lambda parts: tuple(shape(part.shape, part.dtype) for part in parts)
    loads = (
        images.reshape(cells, channels),
        cotangent.reshape(cells, channels),
        norm_gain[None],
        norm_bias[None],
    )
    flat, flat_cot, gain, bias, one, two, three = call(
        functools.partial(first_kernel, dims),
        (*like(loads), halos, small, halos),
        tuple(pin(part) for part in loads),
        (pltpu.SemaphoreType.DMA((len(loads),)),),
        name="first",
        spaces={k: pl.ANY for k in range(len(loads))},
    )
    image_one, image_three, stats = exchange(one, two, three)
    taps = conv_first.reshape(9, channels, channels)
    weights_second = conv_second.reshape(9, channels, channels)
    loads = (time_weight, mix, class_table, time_bias, adaptive_bias[None])
    weights_first, time_weight, mix, class_table, time_bias, adaptive_bias, turned, grouped = call(
        functools.partial(turn_kernel, len(loads)),
        (*like((taps, *loads)), shape(taps.shape, BF16), shape((9, GN_GROUPS, channels), F32)),
        tuple(pin(part) for part in (taps, *loads)),
        (pltpu.SemaphoreType.DMA((len(loads) + 1,)),),
        flops=conv_flops,
        name="turn",
        spaces={k: pl.ANY for k in range(len(loads) + 1)},
    )
    instant = jnp.broadcast_to(jnp.concatenate([timesteps[:1], class_ids[:1]])[:, None], (2, 128))
    embed = call(
        embed_kernel,
        block,
        (instant, class_table, time_weight, time_bias, mix),
        name="embed",
    )

    hidden, stat_one, one, two, three = call(
        functools.partial(second_kernel, dims, len(stats)),
        (narrow, block, halo, small, halo),
        (flat, image_one, image_three, weights_first, gain, bias, embed, *stats),
        (padded,),
        conv_flops,
        name="second",
    )
    hidden_one, hidden_three, stats = exchange(one, two, three)
    grad_active = call(
        functools.partial(grad_kernel, dims),
        shape((cells + 2 * cols, channels), F32),
        (flat_cot, image_one, image_three, weights_second),
        (pltpu.VMEM((cells + 4 * cols, channels), BF16),),
        conv_flops,
        name="grad",
    )
    slope, moved, matrix = call(
        functools.partial(cross_kernel, dims),
        (wide, wide, shape((GN_GROUPS, 8 * GN_GROUPS), BF16)),
        (flat, image_one, image_three, stat_one, gain, bias, hidden, turned, grouped),
        (
            pltpu.VMEM((2, cells + 2 * cols, channels), BF16),
            pltpu.VMEM((3 * channels + 16, cells), BF16),
            pltpu.VMEM((2, 3, 3 * channels + 16, channels), F32),
        ),
        conv_flops,
        name="cross",
    )
    active, grad_norm, stat_two, message = call(
        functools.partial(third_kernel, dims, len(stats)),
        (
            shape((cells + 2 * cols, channels), BF16),
            shape((cells + 2 * cols, channels), F32),
            block,
            shape((STAT_ROWS + GN_GROUPS, channels), BF16),
        ),
        (hidden, hidden_one, hidden_three, grad_active, adaptive_bias, turned, slope, moved, matrix, *stats),
        (padded,),
        conv_flops,
        name="third",
    )
    stats = spread_small(message)
    branch, token = call(
        functools.partial(branch_kernel, dims),
        (narrow, shape((8, 128), F32)),
        (active, weights_second),
        flops=conv_flops,
        name="branch",
    )
    pairs = call(
        functools.partial(pairs_kernel, dims, len(stats)), block, (embed, *stats), name="pairs"
    )
    if fleet == 4:
        pair_list = [pairs, *(swap(pairs, "image", fleet, k) for k in (1, 2, 3))]
    else:
        pair_list = [lax.all_gather(pairs, "image", axis=0, tiled=True)]
    input_grad = call(
        functools.partial(fourth_kernel, dims, len(stats)),
        narrow,
        (token, grad_norm, hidden, hidden_one, hidden_three, stat_two, turned, flat, stat_one, slope, *stats),
        (padded,),
        conv_flops,
        name="fourth",
    )
    grad_weight, grad_bias = call(
        weight_kernel,
        (shape((channels, 2 * channels), F32), shape((1, 2 * channels), F32)),
        tuple(pair_list),
        name="weight",
    )
    return (
        branch.reshape(images.shape),
        input_grad.reshape(images.shape),
        grad_weight[:width],
        grad_bias[0],
    )


def solution(mesh):
    return jax.shard_map(
        body,
        mesh=mesh,
        in_specs=(
            P(("groups", "image"), "tile", None, None),
            P(("groups", "image"), "tile", None, None),
            P(("groups", "image")),
            P(("groups", "image")),
            P(),
            P(),
            P(),
            P(),
            P(None, "tile"),
            P("tile"),
            P(None, "tile"),
            P("tile", None),
            P(),
        ),
        out_specs=(
            P(("groups", "image"), "tile", None, None),
            P(("groups", "image"), "tile", None, None),
            P(("groups", "tile"), None),
            P("groups"),
        ),
        check_vma=False,
    )
```

```python
import functools
import math

import jax
import jax.numpy as jnp
from jax import lax
from jax.experimental import pallas as pl
from jax.experimental.pallas import tpu as pltpu
from jax.sharding import PartitionSpec as P

GN_GROUPS = 32
EPSILON = 1e-05
VMEM_LIMIT = 12 * 1024 * 1024
F32, BF16 = jnp.float32, jnp.bfloat16

STAT_ROWS = 16


def split(values):
    high = values.astype(BF16).astype(F32)
    rest = values - high
    middle = rest.astype(BF16).astype(F32)
    return high, middle, (rest - middle).astype(BF16).astype(F32)


def terms(values):
    high, middle, low = split(values)
    return jnp.concatenate([high + pltpu.roll(middle, 4, 0), low], axis=0).astype(BF16)


def joined(block):
    wide = block.astype(F32)
    total = wide[0:8] + (pltpu.roll(wide[0:8], 4, 0) + wide[8:16])
    return jnp.where(lax.broadcasted_iota(jnp.int32, total.shape, 0) < 4, total, 0.0)


def rows8(*rows):
    width = rows[0].shape[1]
    index = lax.broadcasted_iota(jnp.int32, (8, width), 0)
    out = jnp.zeros((8, width), F32)
    for place, row in enumerate(rows):
        out = jnp.where(index == place, jnp.broadcast_to(row, (8, width)), out)
    return out


def group_matrix(channels):
    shift = (channels // GN_GROUPS).bit_length() - 1
    row = lax.shift_right_logical(lax.broadcasted_iota(jnp.int32, (channels, channels), 0), shift)
    col = lax.shift_right_logical(lax.broadcasted_iota(jnp.int32, (channels, channels), 1), shift)
    return (row == col).astype(F32).astype(BF16)


def group_sums(rows, groups):
    return joined(jnp.dot(terms(rows), groups, preferred_element_type=F32))


def tree_sum(parts):
    parts = list(parts)
    while len(parts) > 1:
        parts = [
            parts[i] + parts[i + 1] if i + 1 < len(parts) else parts[i]
            for i in range(0, len(parts), 2)
        ]
    return parts[0]


def local_moments(values, groups, count):
    mean = group_sums(rows8(jnp.sum(values, axis=0, keepdims=True)), groups)[0:1] / count
    centred = values - mean
    spread = group_sums(rows8(jnp.sum(centred * centred, axis=0, keepdims=True)), groups)[0:1]
    return mean, spread


def joint_moments(stats, count):
    tiles = len(stats)
    mean = tree_sum([s[0:1] for s in stats]) / tiles
    spread = tree_sum([s[1:2] + count * (s[0:1] - mean) * (s[0:1] - mean) for s in stats])
    return mean, lax.rsqrt(spread / (count * tiles) + EPSILON)


def sigmoid(values):
    return 1.0 / (1.0 + jnp.exp(-values))


def column_index(cells, cols, channels):
    index = lax.broadcasted_iota(jnp.int32, (cells, channels), 0)
    return lax.bitwise_and(index, cols - 1)


def conv(padded_ref, kernel_ref, cells, cols, flipped, turned=False):
    parts = []
    for j in range(3):
        total = None
        for i in range(3):
            start = (2 - i if flipped else i) * cols
            product = lax.dot_general(
                padded_ref[start : start + cells],
                kernel_ref[3 * i + j],
                (((1,), (1 if flipped and not turned else 0,)), ((), ())),
                preferred_element_type=F32,
            )
            total = product if total is None else total + product
        parts.append(total)
    if flipped:
        parts = parts[::-1]
    return parts[1] + (shifted(parts[0], cols, 1) + shifted(parts[2], cols, -1))


def shifted(values, cols, step):
    cells = values.shape[0]
    column = column_index(cells, cols, values.shape[1])
    if step == 1:
        return jnp.where(column == 0, 0.0, pltpu.roll(values, 1, 0))
    return jnp.where(column == cols - 1, 0.0, pltpu.roll(values, cells - 1, 0))


def stat_list(refs, start, tiles):
    if len(refs) == 1:
        size = refs[0].shape[0] // tiles
        return [joined(refs[0][size * t : size * t + STAT_ROWS]) for t in range(tiles)]
    return [joined(ref[s : s + STAT_ROWS]) for ref, s in zip(refs, start, strict=True)]


def standing(tiles):
    tile = lax.axis_index("tile")
    return tile, lax.bitwise_and(tile, 1) if tiles == 4 else 0 * tile


def edges(place, one, three):
    odd = place[1] == 1
    return jnp.where(odd, one, three), jnp.where(odd, three, one)


def starts(place, cells, cols):
    odd = place[1]
    first = pl.multiple_of((1 - odd) * (cells - cols), cols)
    third = pl.multiple_of(odd * (cells - cols), cols)
    return first, third


def first_kernel(dims, *refs):
    cells, cols, channels, tiles = dims
    count = (len(refs) - 4) // 2
    sources, copies_to = refs[:count], refs[count : 2 * count]
    one, two, three, sems = refs[2 * count :]
    copies = [
        pltpu.make_async_copy(source, target, sems.at[k])
        for k, (source, target) in enumerate(zip(sources, copies_to, strict=True))
    ]
    for copy in copies:
        copy.start()
    images, cotangent = copies_to[:2]
    place = standing(tiles)
    start_one, start_three = starts(place, cells, cols)
    groups = group_matrix(channels)
    copies[0].wait()
    mean, spread = local_moments(
        images[...].astype(F32), groups, cells * (channels // GN_GROUPS)
    )
    one[0:cols] = images[pl.ds(start_one, cols)]
    three[0:cols] = images[pl.ds(start_three, cols)]
    copies[1].wait()
    one[cols : 2 * cols] = cotangent[pl.ds(start_one, cols)]
    three[cols : 2 * cols] = cotangent[pl.ds(start_three, cols)]
    block = terms(rows8(mean, spread))
    one[2 * cols :] = block
    two[...] = block
    three[2 * cols :] = block
    for copy in copies[2:]:
        copy.wait()


def embed_kernel(instant, table, time_weight, time_bias, adaptive_weight, out):
    channels = adaptive_weight.shape[1] // 2
    half = time_weight.shape[0] // 2

    def times(vector, weights):
        return joined(jnp.dot(terms(rows8(vector)), weights, preferred_element_type=F32))[0:1]

    place = lax.broadcasted_iota(jnp.int32, (8, half), 1).astype(F32)
    angles = instant[0:1, 0:1].astype(F32) * jnp.exp(-math.log(10000.0) * place / half)
    sinusoid = jnp.concatenate([jnp.cos(angles), jnp.sin(angles)], axis=1)[0:1]
    classes = lax.broadcasted_iota(jnp.int32, (16, table.shape[0]), 1)
    onehot = (classes == instant[1:2, 0:1]).astype(F32).astype(BF16)
    row = jnp.dot(onehot, table[...], preferred_element_type=F32)[0:1]
    hidden = times(sinusoid, time_weight[...]) + time_bias[...]
    embedding = hidden * sigmoid(hidden) + row
    activated = embedding * sigmoid(embedding)
    partial = times(activated, adaptive_weight[...])
    out[...] = rows8(partial[:, :channels], partial[:, channels:], activated)


def second_kernel(dims, n_stats, images, one, three, weights, gain, bias, embed, *rest):
    cells, cols, channels, tiles = dims
    place = standing(tiles)
    stat_refs, (hidden, stat, out_one, out_two, out_three, padded) = rest[:n_stats], rest[n_stats:]
    count = cells * (channels // GN_GROUPS)
    mean, inverse = joint_moments(
        stat_list(stat_refs, (0, 2 * cols, 0, 2 * cols), tiles), count
    )
    stat[...] = rows8(mean, inverse)
    above, below = edges(place, one[0:cols], three[0:cols])

    def active(block):
        pre = (block.astype(F32) - mean) * inverse * gain[...] + bias[...]
        return pre * sigmoid(pre)

    padded[0:cols] = jnp.where(place[0] > 0, active(above), 0.0).astype(BF16)
    padded[cols : cols + cells] = active(images[...]).astype(BF16)
    padded[cols + cells :] = jnp.where(place[0] < tiles - 1, active(below), 0.0).astype(BF16)
    rounded = conv(padded, weights, cells, cols, False).astype(BF16)
    hidden[...] = rounded
    mean_two, spread_two = local_moments(rounded.astype(F32), group_matrix(channels), count)
    block = terms(rows8(mean_two, spread_two, embed[0:1], embed[1:2]))
    start_one, start_three = starts(place, cells, cols)
    out_one[0:cols] = hidden[pl.ds(start_one, cols)]
    out_three[0:cols] = hidden[pl.ds(start_three, cols)]
    out_one[cols:] = block
    out_two[...] = block
    out_three[cols:] = block


def identity(size):
    row = lax.broadcasted_iota(jnp.int32, (size, size), 0)
    return (1.0 * (row == lax.broadcasted_iota(jnp.int32, (size, size), 1))).astype(BF16)


def turn_kernel(count, source, *refs):
    sources, weights, copies_to = refs[:count], refs[count], refs[count + 1 : 2 * count + 1]
    turned, grouped, sems = refs[2 * count + 1 :]
    main = pltpu.make_async_copy(source, weights, sems.at[count])
    copies = [
        pltpu.make_async_copy(start, end, sems.at[k])
        for k, (start, end) in enumerate(zip(sources, copies_to, strict=True))
    ]
    for copy in (main, *copies):
        copy.start()
    channels = weights.shape[1]
    rows = jnp.concatenate([identity(channels), group_columns(channels, 0, GN_GROUPS, 0)], axis=0)
    main.wait()
    for k in range(source.shape[0]):
        product = lax.dot_general(
            rows, weights[k], (((1,), (1,)), ((), ())), preferred_element_type=F32
        )
        turned[k] = product[:channels].astype(BF16)
        grouped[k] = product[channels:]
    for copy in copies:
        copy.wait()


def group_columns(channels, offset, length, axis):
    size = (channels, length) if axis else (length, channels)
    shift = (channels // GN_GROUPS).bit_length() - 1
    channel = lax.broadcasted_iota(jnp.int32, size, 1 - axis)
    short = lax.broadcasted_iota(jnp.int32, size, axis)
    hit = lax.shift_right_logical(channel, shift) + offset == short
    return (1.0 * hit).astype(BF16)


def grad_kernel(dims, cotangent, one, three, weights, out, padded):
    cells, cols, channels, tiles = dims
    place = standing(tiles)
    above, below = edges(place, one[cols : 2 * cols], three[cols : 2 * cols])
    padded[0:cols] = jnp.where(place[0] > 0, above, jnp.zeros_like(above))
    padded[cols : cols + cells] = cotangent[...]
    padded[cols + cells :] = jnp.where(place[0] < tiles - 1, below, jnp.zeros_like(below))
    out[...] = conv(padded, weights, cells, cols, True)


def halves(values):
    high = values.astype(BF16)
    return high, (values - high.astype(F32)).astype(BF16)


def cross_kernel(
    dims, images, one, three, stat_one, gain, bias, hidden, turned, grouped, slope, factors, matrix, left, products
):
    cells, cols, channels, tiles = dims
    place = standing(tiles)
    above, below = edges(place, one[0:cols], three[0:cols])

    def pieces(block):
        normed = (block.astype(F32) - stat_one[0:1]) * stat_one[1:2]
        pre = normed * gain[...] + bias[...]
        gate = sigmoid(pre)
        grade = gate * (1.0 + pre * (1.0 - gate)) * gain[...]
        return grade, grade * normed

    own = pieces(images[...])
    slope[...] = own[0]
    for which, (top, bottom) in enumerate(zip(pieces(above), pieces(below), strict=True)):
        factors[which, 0:cols] = jnp.where(place[0] > 0, top, 0.0).astype(BF16)
        factors[which, cols : cols + cells] = own[which].astype(BF16)
        factors[which, cols + cells :] = jnp.where(place[0] < tiles - 1, bottom, 0.0).astype(BF16)
    wide = hidden[...].astype(F32)
    unit = identity(channels)
    for j, line in enumerate((shifted(wide, cols, -1).astype(BF16), hidden[...], shifted(wide, cols, 1).astype(BF16))):
        left[j * channels : (j + 1) * channels] = lax.dot_general(
            unit, line, (((1,), (1,)), ((), ())), preferred_element_type=F32
        ).astype(BF16)
    row = lax.broadcasted_iota(jnp.int32, (16, cells), 0)
    column = lax.bitwise_and(lax.broadcasted_iota(jnp.int32, (16, cells), 1), cols - 1)
    inside = jnp.where(row == 0, 1.0 * (column < cols - 1), jnp.where(row == 2, 1.0 * (column > 0), 1.0))
    left[3 * channels :] = inside.astype(BF16)
    for i in range(3):
        for which in range(2):
            products[which, i] = jnp.dot(
                left[...], factors[which, i * cols : i * cols + cells], preferred_element_type=F32
            )
    step = channels // 8
    totals = ([], [])
    for start in range(0, channels, step):
        parts = ([], [])
        for k in range(9):
            matrix_rows = turned[k, start : start + step].astype(F32)
            for which in range(2):
                begin = (k % 3) * channels + start
                parts[which].append(products[which, k // 3, begin : begin + step] * matrix_rows)
        for which in range(2):
            totals[which].append(tree_sum(parts[which]))
    spread = jnp.zeros((channels, 4 * GN_GROUPS), F32)
    flat = jnp.zeros((GN_GROUPS, 4 * GN_GROUPS), F32)
    for which in range(2):
        total = jnp.concatenate(totals[which], axis=0)
        plain = tree_sum(
            [
                grouped[k] * products[which, k // 3, 3 * channels + k % 3 : 3 * channels + k % 3 + 1]
                for k in range(9)
            ]
        )
        for part in halves(total):
            spread += jnp.dot(
                part, group_columns(channels, which * GN_GROUPS, 4 * GN_GROUPS, 1), preferred_element_type=F32
            )
        for part in halves(plain):
            flat += jnp.dot(
                part, group_columns(channels, (2 + which) * GN_GROUPS, 4 * GN_GROUPS, 1), preferred_element_type=F32
            )
    summed = jnp.sum(spread.reshape(GN_GROUPS, channels // GN_GROUPS, 4 * GN_GROUPS), axis=1)
    matrix[...] = jnp.concatenate(halves(summed + flat), axis=1)


def third_kernel(
    dims, n_stats, hidden, one, three, grad_active, adaptive_bias, turned, factors, matrix, *rest
):
    cells, cols, channels, tiles = dims
    place = standing(tiles)
    stat_refs, (active, grad_norm, stat, out_one, out_two, out_three, padded) = rest[:n_stats], rest[n_stats:]
    count = cells * (channels // GN_GROUPS)
    stats = stat_list(stat_refs, (0, cols, 0, cols), tiles)
    mean, inverse = joint_moments(stats, count)
    modulation = tree_sum(stats)
    factor = 1.0 + (modulation[2:3] + adaptive_bias[:, :channels])
    shift = modulation[3:4] + adaptive_bias[:, channels:]
    stat[...] = rows8(mean, inverse, factor)
    above, below = edges(place, one[0:cols], three[0:cols])

    def pieces(block):
        normed = (block.astype(F32) - mean) * inverse
        pre = normed * factor + shift
        return normed, pre, sigmoid(pre)

    normed, pre, gate = pieces(hidden[...])
    active[cols : cols + cells] = (pre * gate).astype(BF16)
    grad_pre = grad_active[...] * (gate * (1.0 + pre * (1.0 - gate)))
    grad = grad_pre * factor
    grad_norm[...] = grad
    edge = jnp.zeros((2 * cols, channels), BF16)
    padded[0 : 2 * cols] = edge
    padded[2 * cols : 2 * cols + cells] = (grad * inverse).astype(BF16)
    padded[2 * cols + cells :] = edge
    base = conv(padded, turned, cells + 2 * cols, cols, True, True)
    _, pre, gate = pieces(above)
    active[0:cols] = jnp.where(place[0] > 0, pre * gate, 0.0).astype(BF16)
    _, pre, gate = pieces(below)
    active[cols + cells :] = jnp.where(place[0] < tiles - 1, pre * gate, 0.0).astype(BF16)
    block = terms(
        rows8(
            jnp.sum(grad_pre * normed, axis=0, keepdims=True),
            jnp.sum(grad_pre, axis=0, keepdims=True),
            jnp.sum(base * factors[0].astype(F32), axis=0, keepdims=True),
            jnp.sum(base * factors[1].astype(F32), axis=0, keepdims=True),
        )
    )
    start_one, start_three = starts(place, cells, cols)
    out_one[0:cols] = grad_norm[pl.ds(start_one, cols)].astype(BF16)
    out_three[0:cols] = grad_norm[pl.ds(start_three, cols)].astype(BF16)
    for out, start in ((out_one, cols), (out_two, 0), (out_three, cols)):
        out[start : start + STAT_ROWS] = block
        out[start + STAT_ROWS :] = matrix[...]


def pairs_kernel(dims, n_stats, embed, *rest):
    cells, cols, channels, tiles = dims
    sums = tree_sum(stat_list(rest[:n_stats], (0, cols, 0, cols), tiles))
    rest[n_stats][...] = rows8(sums[0:1], sums[1:2], embed[2:3])


def branch_kernel(dims, active, weights, out, token):
    cells, cols, channels, tiles = dims
    out[...] = conv(active, weights, cells, cols, False).astype(BF16)
    token[...] = jnp.zeros_like(token)


def fourth_kernel(
    dims, n_stats, token, grad_norm, grad_one, grad_three, hidden, one, three, stat_two, turned, images, stat_one, slope, *rest
):
    cells, cols, channels, tiles = dims
    place = standing(tiles)
    stat_refs, (out, padded) = rest[:n_stats], rest[n_stats:]
    total = cells * (channels // GN_GROUPS) * tiles
    if len(stat_refs) == 1:
        size = stat_refs[0].shape[0] // tiles
        blocks = [stat_refs[0][size * t + STAT_ROWS : size * (t + 1)] for t in range(tiles)]
    else:
        blocks = [ref[ref.shape[0] - GN_GROUPS :] for ref in stat_refs]
    width = 4 * GN_GROUPS
    matrix = tree_sum([b[:, :width].astype(F32) + b[:, width:].astype(F32) for b in blocks])
    sums = tree_sum(stat_list(stat_refs, (0, cols, 0, cols), tiles))
    mean, inverse, factor = stat_two[0:1], stat_two[1:2], stat_two[2:3]
    row = lax.broadcasted_iota(jnp.int32, (8, channels), 0)
    reduced = group_sums(jnp.where(row < 2, sums * factor, sums), group_matrix(channels))
    paired, plain = reduced[0:1] / total, reduced[1:2] / total
    above, below = edges(place, one[0:cols], three[0:cols])
    grad_above, grad_below = edges(place, grad_one[0:cols], grad_three[0:cols])

    def grad_hidden(grad, block):
        normed = (block.astype(F32) - mean) * inverse
        return inverse * (grad.astype(F32) - plain - normed * paired)

    padded[0:cols] = jnp.where(place[0] > 0, grad_hidden(grad_above, above), 0.0).astype(BF16)
    padded[cols : cols + cells] = grad_hidden(grad_norm[...], hidden[...]).astype(BF16)
    padded[cols + cells :] = jnp.where(
        place[0] < tiles - 1, grad_hidden(grad_below, below), 0.0
    ).astype(BF16)
    grad = conv(padded, turned, cells, cols, True, True) * slope[...]
    beta = paired * inverse * inverse
    alpha = plain * inverse - beta * mean
    per = channels // GN_GROUPS
    weights = terms(rows8(alpha / per, beta / per))
    picked = joined(
        jnp.dot(weights, group_columns(channels, 0, GN_GROUPS, 1), preferred_element_type=F32)
    )
    found = jnp.dot(picked, matrix, precision=lax.Precision.HIGHEST, preferred_element_type=F32)
    found = terms(rows8(pltpu.roll(found, width // 2, 1)[0:1] + found[1:2]))
    means = []
    for which in range(2):
        back = joined(
            jnp.dot(found, group_columns(channels, which * GN_GROUPS, width, 0), preferred_element_type=F32)
        )
        means.append((reduced[2 + which : 3 + which] - back[0:1]) / total)
    normed = (images[...].astype(F32) - stat_one[0:1]) * stat_one[1:2]
    out[...] = (stat_one[1:2] * (grad - means[0] - normed * means[1])).astype(BF16)


def weight_kernel(*rest):
    pair_refs, (weight, bias) = rest[:-2], rest[-2:]
    if len(pair_refs) == 1:
        blocks = [pair_refs[0][8 * n : 8 * n + 8] for n in range(pair_refs[0].shape[0] // 8)]
        places = list(range(len(blocks)))
    else:
        blocks = [ref[...] for ref in pair_refs]
        places = [lax.bitwise_xor(lax.axis_index("image"), k) for k in range(len(blocks))]
    count = -(-len(blocks) // 8) * 8
    channels = blocks[0].shape[1]
    row = lax.broadcasted_iota(jnp.int32, (count, channels), 0)

    def ordered(which):
        out = jnp.zeros((count, channels), F32)
        for block, place in zip(blocks, places, strict=True):
            out = jnp.where(row == place, jnp.broadcast_to(block[which : which + 1], out.shape), out)
        return out

    activated = split(ordered(2))
    left = jnp.concatenate([activated[k] for k in (0, 0, 1, 0, 2, 1)], axis=0).astype(BF16)
    for start, which in ((0, 0), (channels, 1)):
        part = ordered(which)
        pieces = split(part)
        right = jnp.concatenate([pieces[k] for k in (0, 1, 0, 2, 0, 1)], axis=0).astype(BF16)
        weight[:, start : start + channels] = lax.dot_general(
            left, right, (((0,), (0,)), ((), ())), preferred_element_type=F32
        )
        bias[:, start : start + channels] = jnp.sum(part, axis=0, keepdims=True)


def call(kernel, out_shapes, operands, scratch=(), flops=1000, name=None, spaces=None):
    size = sum(o.size * o.dtype.itemsize for o in operands)
    return pl.pallas_call(
        kernel,
        out_shape=out_shapes,
        in_specs=[
            pl.BlockSpec(memory_space=(spaces or {}).get(k, pltpu.VMEM)) for k in range(len(operands))
        ],
        out_specs=jax.tree.map(lambda _: pl.BlockSpec(memory_space=pltpu.VMEM), out_shapes),
        scratch_shapes=list(scratch),
        compiler_params=pltpu.CompilerParams(vmem_limit_bytes=VMEM_LIMIT),
        cost_estimate=pl.CostEstimate(flops=flops, bytes_accessed=size, transcendentals=0),
        name=name,
    )(*operands)


def swap(values, axis, size, distance):
    return lax.ppermute(values, axis, [(i, i ^ distance) for i in range(size)])


def exchange(one, two, three):
    tiles = lax.axis_size("tile")
    if tiles == 4:
        got = [swap(part, "tile", tiles, k + 1) for k, part in enumerate((one, two, three))]
        return got[0], got[2], [two, *got]
    ahead = [(i, (i + 1) % tiles) for i in range(tiles)]
    behind = [(target, source) for source, target in ahead]
    below, above = lax.ppermute(three, "tile", behind), lax.ppermute(one, "tile", ahead)
    return below, above, [lax.all_gather(two, "tile", axis=0, tiled=True)]


def body(
    images,
    cotangent,
    timesteps,
    class_ids,
    norm_gain,
    norm_bias,
    conv_first,
    conv_second,
    time_weight,
    time_bias,
    class_table,
    adaptive_weight,
    adaptive_bias,
):
    _, rows, cols, channels = images.shape
    tiles, fleet = lax.axis_size("tile"), lax.axis_size("image")
    cells = rows * cols
    dims = (cells, cols, channels, tiles)
    shape = jax.ShapeDtypeStruct
    conv_flops = 18 * cells * channels * channels
    padded = pltpu.VMEM((cells + 2 * cols, channels), BF16)
    small = shape((STAT_ROWS, channels), BF16)
    halo = shape((cols + STAT_ROWS, channels), BF16)
    halos = shape((2 * cols + STAT_ROWS, channels), BF16)
    block = shape((8, channels), F32)
    wide = shape((cells, channels), F32)
    narrow = shape((cells, channels), BF16)

    width = adaptive_weight.shape[0]
    spare = channels - width
    time_bias, mix = time_bias[None], adaptive_weight
    if spare:
        time_weight, time_bias, class_table = (
            jnp.pad(part, ((0, 0), (0, spare))) for part in (time_weight, time_bias, class_table)
        )
        mix = jnp.pad(mix, ((0, spare), (0, 0)))
    pin = lambda part: pltpu.with_memory_space_constraint(part, pltpu.HBM)
    like = lambda parts: tuple(shape(part.shape, part.dtype) for part in parts)
    loads = (
        images.reshape(cells, channels),
        cotangent.reshape(cells, channels),
        norm_gain[None],
        norm_bias[None],
    )
    flat, flat_cot, gain, bias, one, two, three = call(
        functools.partial(first_kernel, dims),
        (*like(loads), halos, small, halos),
        tuple(pin(part) for part in loads),
        (pltpu.SemaphoreType.DMA((len(loads),)),),
        name="first",
        spaces={k: pl.ANY for k in range(len(loads))},
    )
    image_one, image_three, stats = exchange(one, two, three)
    taps = conv_first.reshape(9, channels, channels)
    weights_second = conv_second.reshape(9, channels, channels)
    loads = (time_weight, mix, class_table, time_bias, adaptive_bias[None])
    weights_first, time_weight, mix, class_table, time_bias, adaptive_bias, turned, grouped = call(
        functools.partial(turn_kernel, len(loads)),
        (*like((taps, *loads)), shape(taps.shape, BF16), shape((9, GN_GROUPS, channels), F32)),
        tuple(pin(part) for part in (taps, *loads)),
        (pltpu.SemaphoreType.DMA((len(loads) + 1,)),),
        flops=conv_flops,
        name="turn",
        spaces={k: pl.ANY for k in range(len(loads) + 1)},
    )
    instant = jnp.broadcast_to(jnp.concatenate([timesteps[:1], class_ids[:1]])[:, None], (2, 128))
    embed = call(
        embed_kernel,
        block,
        (instant, class_table, time_weight, time_bias, mix),
        name="embed",
    )

    hidden, stat_one, one, two, three = call(
        functools.partial(second_kernel, dims, len(stats)),
        (narrow, block, halo, small, halo),
        (flat, image_one, image_three, weights_first, gain, bias, embed, *stats),
        (padded,),
        conv_flops,
        name="second",
    )
    hidden_one, hidden_three, stats = exchange(one, two, three)
    grad_active = call(
        functools.partial(grad_kernel, dims),
        wide,
        (flat_cot, image_one, image_three, weights_second),
        (padded,),
        conv_flops,
        name="grad",
    )
    slope, factors, matrix = call(
        functools.partial(cross_kernel, dims),
        (wide, shape((2, cells + 2 * cols, channels), BF16), shape((GN_GROUPS, 8 * GN_GROUPS), BF16)),
        (flat, image_one, image_three, stat_one, gain, bias, hidden, turned, grouped),
        (
            pltpu.VMEM((3 * channels + 16, cells), BF16),
            pltpu.VMEM((2, 3, 3 * channels + 16, channels), F32),
        ),
        conv_flops,
        name="cross",
    )
    mail = shape((STAT_ROWS + GN_GROUPS, channels), BF16)
    mail_halo = shape((cols + STAT_ROWS + GN_GROUPS, channels), BF16)
    active, grad_norm, stat_two, one, two, three = call(
        functools.partial(third_kernel, dims, len(stats)),
        (shape((cells + 2 * cols, channels), BF16), wide, block, mail_halo, mail, mail_halo),
        (hidden, hidden_one, hidden_three, grad_active, adaptive_bias, turned, factors, matrix, *stats),
        (pltpu.VMEM((cells + 4 * cols, channels), BF16),),
        conv_flops,
        name="third",
    )
    grad_one, grad_three, stats = exchange(one, two, three)
    branch, token = call(
        functools.partial(branch_kernel, dims),
        (pltpu.VMEM((cells, channels), BF16), shape((8, 128), F32)),
        (active, weights_second),
        flops=conv_flops,
        name="branch",
    )
    pairs = call(
        functools.partial(pairs_kernel, dims, len(stats)), block, (embed, *stats), name="pairs"
    )
    if fleet == 4:
        pair_list = [pairs, *(swap(pairs, "image", fleet, k) for k in (1, 2, 3))]
    else:
        pair_list = [lax.all_gather(pairs, "image", axis=0, tiled=True)]
    input_grad = call(
        functools.partial(fourth_kernel, dims, len(stats)),
        pltpu.VMEM((cells, channels), BF16),
        (token, grad_norm, grad_one, grad_three, hidden, hidden_one, hidden_three, stat_two, turned, flat, stat_one, slope, *stats),
        (padded,),
        conv_flops,
        name="fourth",
    )
    grad_weight, grad_bias = call(
        weight_kernel,
        (shape((channels, 2 * channels), F32), shape((1, 2 * channels), F32)),
        tuple(pair_list),
        name="weight",
    )
    return (
        branch.reshape(images.shape),
        input_grad.reshape(images.shape),
        grad_weight[:width],
        grad_bias[0],
    )


def solution(mesh):
    return jax.shard_map(
        body,
        mesh=mesh,
        in_specs=(
            P(("groups", "image"), "tile", None, None),
            P(("groups", "image"), "tile", None, None),
            P(("groups", "image")),
            P(("groups", "image")),
            P(),
            P(),
            P(),
            P(),
            P(None, "tile"),
            P("tile"),
            P(None, "tile"),
            P("tile", None),
            P(),
        ),
        out_specs=(
            P(("groups", "image"), "tile", None, None),
            P(("groups", "image"), "tile", None, None),
            P(("groups", "tile"), None),
            P("groups"),
        ),
        check_vma=False,
    )
```

```python
import functools
import math

import jax
import jax.numpy as jnp
from jax import lax
from jax.experimental import pallas as pl
from jax.experimental.pallas import tpu as pltpu
from jax.sharding import PartitionSpec as P

GN_GROUPS = 32
EPSILON = 1e-05
VMEM_LIMIT = 12 * 1024 * 1024
F32, BF16 = jnp.float32, jnp.bfloat16

STAT_ROWS = 16


def split(values):
    high = values.astype(BF16).astype(F32)
    rest = values - high
    middle = rest.astype(BF16).astype(F32)
    return high, middle, (rest - middle).astype(BF16).astype(F32)


def terms(values):
    high, middle, low = split(values)
    return jnp.concatenate([high + pltpu.roll(middle, 4, 0), low], axis=0).astype(BF16)


def joined(block):
    wide = block.astype(F32)
    total = wide[0:8] + (pltpu.roll(wide[0:8], 4, 0) + wide[8:16])
    return jnp.where(lax.broadcasted_iota(jnp.int32, total.shape, 0) < 4, total, 0.0)


def rows8(*rows):
    width = rows[0].shape[1]
    index = lax.broadcasted_iota(jnp.int32, (8, width), 0)
    out = jnp.zeros((8, width), F32)
    for place, row in enumerate(rows):
        out = jnp.where(index == place, jnp.broadcast_to(row, (8, width)), out)
    return out


def group_matrix(channels):
    shift = (channels // GN_GROUPS).bit_length() - 1
    row = lax.shift_right_logical(lax.broadcasted_iota(jnp.int32, (channels, channels), 0), shift)
    col = lax.shift_right_logical(lax.broadcasted_iota(jnp.int32, (channels, channels), 1), shift)
    return (row == col).astype(F32).astype(BF16)


def group_sums(rows, groups):
    return joined(jnp.dot(terms(rows), groups, preferred_element_type=F32))


def tree_sum(parts):
    parts = list(parts)
    while len(parts) > 1:
        parts = [
            parts[i] + parts[i + 1] if i + 1 < len(parts) else parts[i]
            for i in range(0, len(parts), 2)
        ]
    return parts[0]


def local_moments(values, groups, count):
    mean = group_sums(rows8(jnp.sum(values, axis=0, keepdims=True)), groups)[0:1] / count
    centred = values - mean
    spread = group_sums(rows8(jnp.sum(centred * centred, axis=0, keepdims=True)), groups)[0:1]
    return mean, spread


def joint_moments(stats, count):
    tiles = len(stats)
    mean = tree_sum([s[0:1] for s in stats]) / tiles
    spread = tree_sum([s[1:2] + count * (s[0:1] - mean) * (s[0:1] - mean) for s in stats])
    return mean, lax.rsqrt(spread / (count * tiles) + EPSILON)


def sigmoid(values):
    return 1.0 / (1.0 + jnp.exp(-values))


def column_index(cells, cols, channels):
    index = lax.broadcasted_iota(jnp.int32, (cells, channels), 0)
    return lax.bitwise_and(index, cols - 1)


def conv(padded_ref, kernel_ref, cells, cols, flipped):
    parts = []
    for j in range(3):
        total = None
        for i in range(3):
            start = (2 - i if flipped else i) * cols
            product = lax.dot_general(
                padded_ref[start : start + cells],
                kernel_ref[3 * i + j],
                (((1,), (1 if flipped else 0,)), ((), ())),
                preferred_element_type=F32,
            )
            total = product if total is None else total + product
        parts.append(total)
    if flipped:
        parts = parts[::-1]
    return parts[1] + (shifted(parts[0], cols, 1) + shifted(parts[2], cols, -1))


def shifted(values, cols, step):
    cells = values.shape[0]
    column = column_index(cells, cols, values.shape[1])
    if step == 1:
        return jnp.where(column == 0, 0.0, pltpu.roll(values, 1, 0))
    return jnp.where(column == cols - 1, 0.0, pltpu.roll(values, cells - 1, 0))


def stat_list(refs, start, tiles):
    if len(refs) == 1:
        size = refs[0].shape[0] // tiles
        return [joined(refs[0][size * t : size * t + STAT_ROWS]) for t in range(tiles)]
    return [joined(ref[s : s + STAT_ROWS]) for ref, s in zip(refs, start, strict=True)]


def standing(tiles):
    tile = lax.axis_index("tile")
    return tile, lax.bitwise_and(tile, 1) if tiles == 4 else 0 * tile


def edges(place, one, three):
    odd = place[1] == 1
    return jnp.where(odd, one, three), jnp.where(odd, three, one)


def starts(place, cells, cols):
    odd = place[1]
    first = pl.multiple_of((1 - odd) * (cells - cols), cols)
    third = pl.multiple_of(odd * (cells - cols), cols)
    return first, third


def first_kernel(dims, *refs):
    cells, cols, channels, tiles = dims
    count = (len(refs) - 4) // 2
    sources, copies_to = refs[:count], refs[count : 2 * count]
    one, two, three, sems = refs[2 * count :]
    copies = [
        pltpu.make_async_copy(source, target, sems.at[k])
        for k, (source, target) in enumerate(zip(sources, copies_to, strict=True))
    ]
    for copy in copies:
        copy.start()
    images, cotangent = copies_to[:2]
    place = standing(tiles)
    start_one, start_three = starts(place, cells, cols)
    groups = group_matrix(channels)
    copies[0].wait()
    mean, spread = local_moments(
        images[...].astype(F32), groups, cells * (channels // GN_GROUPS)
    )
    one[0:cols] = images[pl.ds(start_one, cols)]
    three[0:cols] = images[pl.ds(start_three, cols)]
    copies[1].wait()
    one[cols : 2 * cols] = cotangent[pl.ds(start_one, cols)]
    three[cols : 2 * cols] = cotangent[pl.ds(start_three, cols)]
    block = terms(rows8(mean, spread))
    one[2 * cols :] = block
    two[...] = block
    three[2 * cols :] = block
    for copy in copies[2:]:
        copy.wait()


def embedding(step, label, table, time_weight, time_bias, adaptive_weight):
    channels = adaptive_weight.shape[1] // 2
    half = time_weight.shape[0] // 2

    def times(vector, weights):
        return joined(jnp.dot(terms(rows8(vector)), weights, preferred_element_type=F32))[0:1]

    place = lax.broadcasted_iota(jnp.int32, (8, half), 1).astype(F32)
    angles = step.astype(F32) * jnp.exp(-math.log(10000.0) * place / half)
    sinusoid = jnp.concatenate([jnp.cos(angles), jnp.sin(angles)], axis=1)[0:1]
    classes = lax.broadcasted_iota(jnp.int32, (16, table.shape[0]), 1)
    onehot = (classes == label).astype(F32).astype(BF16)
    row = jnp.dot(onehot, table[...], preferred_element_type=F32)[0:1]
    hidden = times(sinusoid, time_weight[...]) + time_bias[...]
    embedded = hidden * sigmoid(hidden) + row
    activated = embedded * sigmoid(embedded)
    partial = times(activated, adaptive_weight[...])
    return rows8(partial[:, :channels], partial[:, channels:], activated)


def second_kernel(dims, n_stats, images, one, three, weights, gain, bias, embed, *rest):
    cells, cols, channels, tiles = dims
    place = standing(tiles)
    stat_refs, (hidden, stat, out_one, out_two, out_three, padded) = rest[:n_stats], rest[n_stats:]
    count = cells * (channels // GN_GROUPS)
    mean, inverse = joint_moments(
        stat_list(stat_refs, (0, 2 * cols, 0, 2 * cols), tiles), count
    )
    stat[...] = rows8(mean, inverse)
    above, below = edges(place, one[0:cols], three[0:cols])

    def active(block):
        pre = (block.astype(F32) - mean) * inverse * gain[...] + bias[...]
        return pre * sigmoid(pre)

    padded[0:cols] = jnp.where(place[0] > 0, active(above), 0.0).astype(BF16)
    padded[cols : cols + cells] = active(images[...]).astype(BF16)
    padded[cols + cells :] = jnp.where(place[0] < tiles - 1, active(below), 0.0).astype(BF16)
    rounded = conv(padded, weights, cells, cols, False).astype(BF16)
    hidden[...] = rounded
    mean_two, spread_two = local_moments(rounded.astype(F32), group_matrix(channels), count)
    block = terms(rows8(mean_two, spread_two, embed[0:1], embed[1:2]))
    start_one, start_three = starts(place, cells, cols)
    out_one[0:cols] = hidden[pl.ds(start_one, cols)]
    out_three[0:cols] = hidden[pl.ds(start_three, cols)]
    out_one[cols:] = block
    out_two[...] = block
    out_three[cols:] = block


def identity(size):
    row = lax.broadcasted_iota(jnp.int32, (size, size), 0)
    return (1.0 * (row == lax.broadcasted_iota(jnp.int32, (size, size), 1))).astype(BF16)


def turn_kernel(step, label, table, time_weight, time_bias, mix, source, bias_source, weights, bias, embed, grouped, sems):
    copies = [
        pltpu.make_async_copy(source, weights, sems.at[0]),
        pltpu.make_async_copy(bias_source, bias, sems.at[1]),
    ]
    for copy in copies:
        copy.start()
    embed[...] = embedding(step[0], label[0], table, time_weight, time_bias, mix)
    columns = tiled_columns(weights.shape[1])
    for copy in copies:
        copy.wait()
    for k in range(source.shape[0]):
        grouped[k] = jnp.dot(weights[k], columns, preferred_element_type=F32)


def tiled_columns(channels):
    size = (channels, 4 * GN_GROUPS)
    shift = (channels // GN_GROUPS).bit_length() - 1
    group = lax.shift_right_logical(lax.broadcasted_iota(jnp.int32, size, 0), shift)
    column = lax.bitwise_and(lax.broadcasted_iota(jnp.int32, size, 1), GN_GROUPS - 1)
    return (1.0 * (group == column)).astype(BF16)


def group_columns(channels, offset, length, axis):
    size = (channels, length) if axis else (length, channels)
    shift = (channels // GN_GROUPS).bit_length() - 1
    channel = lax.broadcasted_iota(jnp.int32, size, 1 - axis)
    short = lax.broadcasted_iota(jnp.int32, size, axis)
    hit = lax.shift_right_logical(channel, shift) + offset == short
    return (1.0 * hit).astype(BF16)


def grad_kernel(dims, cotangent, one, three, weights, out, padded):
    cells, cols, channels, tiles = dims
    place = standing(tiles)
    above, below = edges(place, one[cols : 2 * cols], three[cols : 2 * cols])
    padded[0:cols] = jnp.where(place[0] > 0, above, jnp.zeros_like(above))
    padded[cols : cols + cells] = cotangent[...]
    padded[cols + cells :] = jnp.where(place[0] < tiles - 1, below, jnp.zeros_like(below))
    out[...] = conv(padded, weights, cells, cols, True)


def halves(values):
    high = values.astype(BF16)
    return high, (values - high.astype(F32)).astype(BF16)


def cross_kernel(
    dims, images, one, three, stat_one, gain, bias, hidden, weights, grouped, slope, factors, matrix, left, products
):
    cells, cols, channels, tiles = dims
    place = standing(tiles)
    above, below = edges(place, one[0:cols], three[0:cols])

    def pieces(block):
        normed = (block.astype(F32) - stat_one[0:1]) * stat_one[1:2]
        pre = normed * gain[...] + bias[...]
        gate = sigmoid(pre)
        grade = gate * (1.0 + pre * (1.0 - gate)) * gain[...]
        return grade, grade * normed

    own = pieces(images[...])
    slope[...] = own[0]
    for which, (top, bottom) in enumerate(zip(pieces(above), pieces(below), strict=True)):
        factors[which, 0:cols] = jnp.where(place[0] > 0, top, 0.0).astype(BF16)
        factors[which, cols : cols + cells] = own[which].astype(BF16)
        factors[which, cols + cells :] = jnp.where(place[0] < tiles - 1, bottom, 0.0).astype(BF16)
    unit = identity(channels)
    for which in range(2):
        for i in range(3):
            place_at = (3 * which + i) * channels
            left[place_at : place_at + channels] = lax.dot_general(
                unit,
                factors[which, i * cols : i * cols + cells],
                (((1,), (1,)), ((), ())),
                preferred_element_type=F32,
            ).astype(BF16)
    wide = hidden[...].astype(F32)
    lines = (shifted(wide, cols, -1).astype(BF16), hidden[...], shifted(wide, cols, 1).astype(BF16))
    for j, line in enumerate(lines):
        products[j] = jnp.dot(left[...], line, preferred_element_type=F32)
    column = lax.bitwise_and(lax.broadcasted_iota(jnp.int32, (cells, 128), 0), cols - 1)
    which_column = lax.broadcasted_iota(jnp.int32, (cells, 128), 1)
    inside = jnp.where(
        which_column == 0, 1.0 * (column < cols - 1), jnp.where(which_column == 2, 1.0 * (column > 0), 1.0)
    )
    plain_sums = jnp.dot(left[...], inside.astype(BF16), preferred_element_type=F32)
    step = channels // 8
    totals = ([], [])
    for start in range(0, channels, step):
        parts = ([], [])
        for k in range(9):
            matrix_rows = weights[k, start : start + step].astype(F32)
            for which in range(2):
                begin = (3 * which + k // 3) * channels + start
                parts[which].append(products[k % 3, begin : begin + step] * matrix_rows)
        for which in range(2):
            totals[which].append(tree_sum(parts[which]))
    block = lax.shift_right_logical(
        lax.broadcasted_iota(jnp.int32, (channels, 4 * GN_GROUPS), 1), GN_GROUPS.bit_length() - 1
    )
    spread = jnp.zeros((channels, 4 * GN_GROUPS), F32)
    for which in range(2):
        for part in halves(jnp.concatenate(totals[which], axis=0)):
            spread += jnp.dot(
                part, group_columns(channels, which * GN_GROUPS, 4 * GN_GROUPS, 1), preferred_element_type=F32
            )
        plain = tree_sum(
            [
                grouped[k]
                * plain_sums[(3 * which + k // 3) * channels : (3 * which + k // 3 + 1) * channels, k % 3 : k % 3 + 1]
                for k in range(9)
            ]
        )
        spread += jnp.where(block == 2 + which, plain, 0.0)
    summed = jnp.sum(spread.reshape(GN_GROUPS, channels // GN_GROUPS, 4 * GN_GROUPS), axis=1)
    matrix[...] = jnp.concatenate(halves(summed), axis=1)


def third_kernel(
    dims, n_stats, hidden, one, three, grad_active, adaptive_bias, weights, factors, matrix, *rest
):
    cells, cols, channels, tiles = dims
    place = standing(tiles)
    stat_refs, (active, grad_norm, stat, out_one, out_two, out_three, padded) = rest[:n_stats], rest[n_stats:]
    count = cells * (channels // GN_GROUPS)
    stats = stat_list(stat_refs, (0, cols, 0, cols), tiles)
    mean, inverse = joint_moments(stats, count)
    modulation = tree_sum(stats)
    factor = 1.0 + (modulation[2:3] + adaptive_bias[:, :channels])
    shift = modulation[3:4] + adaptive_bias[:, channels:]
    stat[...] = rows8(mean, inverse, factor)
    above, below = edges(place, one[0:cols], three[0:cols])

    def pieces(block):
        normed = (block.astype(F32) - mean) * inverse
        pre = normed * factor + shift
        return normed, pre, sigmoid(pre)

    normed, pre, gate = pieces(hidden[...])
    active[cols : cols + cells] = (pre * gate).astype(BF16)
    grad_pre = grad_active[...] * (gate * (1.0 + pre * (1.0 - gate)))
    grad = grad_pre * factor
    grad_norm[...] = grad
    edge = jnp.zeros((2 * cols, channels), BF16)
    padded[0 : 2 * cols] = edge
    padded[2 * cols : 2 * cols + cells] = (grad * inverse).astype(BF16)
    padded[2 * cols + cells :] = edge
    base = conv(padded, weights, cells + 2 * cols, cols, True)
    _, pre, gate = pieces(above)
    active[0:cols] = jnp.where(place[0] > 0, pre * gate, 0.0).astype(BF16)
    _, pre, gate = pieces(below)
    active[cols + cells :] = jnp.where(place[0] < tiles - 1, pre * gate, 0.0).astype(BF16)
    block = terms(
        rows8(
            jnp.sum(grad_pre * normed, axis=0, keepdims=True),
            jnp.sum(grad_pre, axis=0, keepdims=True),
            jnp.sum(base * factors[0].astype(F32), axis=0, keepdims=True),
            jnp.sum(base * factors[1].astype(F32), axis=0, keepdims=True),
        )
    )
    start_one, start_three = starts(place, cells, cols)
    out_one[0:cols] = grad_norm[pl.ds(start_one, cols)].astype(BF16)
    out_three[0:cols] = grad_norm[pl.ds(start_three, cols)].astype(BF16)
    for out, start in ((out_one, cols), (out_two, 0), (out_three, cols)):
        out[start : start + STAT_ROWS] = block
        out[start + STAT_ROWS :] = matrix[...]


def pairs_kernel(dims, n_stats, embed, *rest):
    cells, cols, channels, tiles = dims
    sums = tree_sum(stat_list(rest[:n_stats], (0, cols, 0, cols), tiles))
    rest[n_stats][...] = rows8(sums[0:1], sums[1:2], embed[2:3])


def branch_kernel(dims, active, weights, out, token):
    cells, cols, channels, tiles = dims
    out[...] = conv(active, weights, cells, cols, False).astype(BF16)
    token[...] = jnp.zeros_like(token)


def fourth_kernel(
    dims, n_stats, token, grad_norm, grad_one, grad_three, hidden, one, three, stat_two, weights, images, stat_one, slope, *rest
):
    cells, cols, channels, tiles = dims
    place = standing(tiles)
    stat_refs, (out, padded) = rest[:n_stats], rest[n_stats:]
    total = cells * (channels // GN_GROUPS) * tiles
    if len(stat_refs) == 1:
        size = stat_refs[0].shape[0] // tiles
        blocks = [stat_refs[0][size * t + STAT_ROWS : size * (t + 1)] for t in range(tiles)]
    else:
        blocks = [ref[ref.shape[0] - GN_GROUPS :] for ref in stat_refs]
    width = 4 * GN_GROUPS
    matrix = tree_sum([b[:, :width].astype(F32) + b[:, width:].astype(F32) for b in blocks])
    sums = tree_sum(stat_list(stat_refs, (0, cols, 0, cols), tiles))
    mean, inverse, factor = stat_two[0:1], stat_two[1:2], stat_two[2:3]
    row = lax.broadcasted_iota(jnp.int32, (8, channels), 0)
    reduced = group_sums(jnp.where(row < 2, sums * factor, sums), group_matrix(channels))
    paired, plain = reduced[0:1] / total, reduced[1:2] / total
    above, below = edges(place, one[0:cols], three[0:cols])
    grad_above, grad_below = edges(place, grad_one[0:cols], grad_three[0:cols])

    def grad_hidden(grad, block):
        normed = (block.astype(F32) - mean) * inverse
        return inverse * (grad.astype(F32) - plain - normed * paired)

    padded[0:cols] = jnp.where(place[0] > 0, grad_hidden(grad_above, above), 0.0).astype(BF16)
    padded[cols : cols + cells] = grad_hidden(grad_norm[...], hidden[...]).astype(BF16)
    padded[cols + cells :] = jnp.where(
        place[0] < tiles - 1, grad_hidden(grad_below, below), 0.0
    ).astype(BF16)
    grad = conv(padded, weights, cells, cols, True) * slope[...]
    beta = paired * inverse * inverse
    alpha = plain * inverse - beta * mean
    per = channels // GN_GROUPS
    picked = joined(
        jnp.dot(terms(rows8(alpha / per, beta / per)), tiled_columns(channels), preferred_element_type=F32)
    )
    block = lax.shift_right_logical(
        lax.broadcasted_iota(jnp.int32, (1, width), 1), GN_GROUPS.bit_length() - 1
    )
    vectors = [
        jnp.where(block == which, picked[1:2], jnp.where(block == 2 + which, picked[0:1], 0.0))
        for which in range(2)
    ]
    found = lax.dot_general(
        rows8(*vectors),
        matrix,
        (((1,), (1,)), ((), ())),
        precision=lax.Precision.HIGHEST,
        preferred_element_type=F32,
    )
    back = joined(
        jnp.dot(terms(found), group_columns(channels, 0, GN_GROUPS, 0), preferred_element_type=F32)
    )
    means = [(reduced[2 + which : 3 + which] - back[which : which + 1]) / total for which in range(2)]
    normed = (images[...].astype(F32) - stat_one[0:1]) * stat_one[1:2]
    out[...] = (stat_one[1:2] * (grad - means[0] - normed * means[1])).astype(BF16)


def weight_kernel(*rest):
    pair_refs, (weight, bias) = rest[:-2], rest[-2:]
    if len(pair_refs) == 1:
        blocks = [pair_refs[0][8 * n : 8 * n + 8] for n in range(pair_refs[0].shape[0] // 8)]
        places = list(range(len(blocks)))
    else:
        blocks = [ref[...] for ref in pair_refs]
        places = [lax.bitwise_xor(lax.axis_index("image"), k) for k in range(len(blocks))]
    count = -(-len(blocks) // 8) * 8
    channels = blocks[0].shape[1]
    row = lax.broadcasted_iota(jnp.int32, (count, channels), 0)

    def ordered(which):
        out = jnp.zeros((count, channels), F32)
        for block, place in zip(blocks, places, strict=True):
            out = jnp.where(row == place, jnp.broadcast_to(block[which : which + 1], out.shape), out)
        return out

    activated = split(ordered(2))
    left = jnp.concatenate([activated[k] for k in (0, 0, 1, 0, 2, 1)], axis=0).astype(BF16)
    for start, which in ((0, 0), (channels, 1)):
        part = ordered(which)
        pieces = split(part)
        right = jnp.concatenate([pieces[k] for k in (0, 1, 0, 2, 0, 1)], axis=0).astype(BF16)
        weight[:, start : start + channels] = lax.dot_general(
            left, right, (((0,), (0,)), ((), ())), preferred_element_type=F32
        )
        bias[:, start : start + channels] = jnp.sum(part, axis=0, keepdims=True)


def call(kernel, out_shapes, operands, scratch=(), flops=1000, name=None, spaces=None):
    size = sum(o.size * o.dtype.itemsize for o in operands)
    return pl.pallas_call(
        kernel,
        out_shape=out_shapes,
        in_specs=[
            pl.BlockSpec(memory_space=(spaces or {}).get(k, pltpu.VMEM)) for k in range(len(operands))
        ],
        out_specs=jax.tree.map(lambda _: pl.BlockSpec(memory_space=pltpu.VMEM), out_shapes),
        scratch_shapes=list(scratch),
        compiler_params=pltpu.CompilerParams(vmem_limit_bytes=VMEM_LIMIT),
        cost_estimate=pl.CostEstimate(flops=flops, bytes_accessed=size, transcendentals=0),
        name=name,
    )(*operands)


def swap(values, axis, size, distance):
    return lax.ppermute(values, axis, [(i, i ^ distance) for i in range(size)])


def exchange(one, two, three):
    tiles = lax.axis_size("tile")
    if tiles == 4:
        got = [swap(part, "tile", tiles, k + 1) for k, part in enumerate((one, two, three))]
        return got[0], got[2], [two, *got]
    ahead = [(i, (i + 1) % tiles) for i in range(tiles)]
    behind = [(target, source) for source, target in ahead]
    below, above = lax.ppermute(three, "tile", behind), lax.ppermute(one, "tile", ahead)
    return below, above, [lax.all_gather(two, "tile", axis=0, tiled=True)]


def body(
    images,
    cotangent,
    timesteps,
    class_ids,
    norm_gain,
    norm_bias,
    conv_first,
    conv_second,
    time_weight,
    time_bias,
    class_table,
    adaptive_weight,
    adaptive_bias,
):
    _, rows, cols, channels = images.shape
    tiles, fleet = lax.axis_size("tile"), lax.axis_size("image")
    cells = rows * cols
    dims = (cells, cols, channels, tiles)
    shape = jax.ShapeDtypeStruct
    conv_flops = 18 * cells * channels * channels
    padded = pltpu.VMEM((cells + 2 * cols, channels), BF16)
    small = shape((STAT_ROWS, channels), BF16)
    halo = shape((cols + STAT_ROWS, channels), BF16)
    halos = shape((2 * cols + STAT_ROWS, channels), BF16)
    block = shape((8, channels), F32)
    wide = shape((cells, channels), F32)
    narrow = shape((cells, channels), BF16)

    width = adaptive_weight.shape[0]
    spare = channels - width
    time_bias, mix = time_bias[None], adaptive_weight
    if spare:
        time_weight, time_bias, class_table = (
            jnp.pad(part, ((0, 0), (0, spare))) for part in (time_weight, time_bias, class_table)
        )
        mix = jnp.pad(mix, ((0, spare), (0, 0)))
    pin = lambda part: pltpu.with_memory_space_constraint(part, pltpu.HBM)
    like = lambda parts: tuple(shape(part.shape, part.dtype) for part in parts)
    loads = (
        images.reshape(cells, channels),
        cotangent.reshape(cells, channels),
        norm_gain[None],
        norm_bias[None],
        class_table,
        time_weight,
        time_bias,
        mix,
    )
    flat, flat_cot, gain, bias, class_table, time_weight, time_bias, mix, one, two, three = call(
        functools.partial(first_kernel, dims),
        (*like(loads), halos, small, halos),
        tuple(pin(part) for part in loads),
        (pltpu.SemaphoreType.DMA((len(loads),)),),
        name="first",
        spaces={k: pl.ANY for k in range(len(loads))},
    )
    image_one, image_three, stats = exchange(one, two, three)
    taps = conv_first.reshape(9, channels, channels)
    weights_second = conv_second.reshape(9, channels, channels)
    weights_first, adaptive_bias, embed, grouped = call(
        turn_kernel,
        (
            shape(taps.shape, BF16),
            shape((1, 2 * channels), F32),
            block,
            shape((9, channels, 4 * GN_GROUPS), F32),
        ),
        (timesteps, class_ids, class_table, time_weight, time_bias, mix, pin(taps), pin(adaptive_bias[None])),
        (pltpu.SemaphoreType.DMA((2,)),),
        flops=conv_flops,
        name="turn",
        spaces={0: pltpu.SMEM, 1: pltpu.SMEM, 6: pl.ANY, 7: pl.ANY},
    )

    hidden, stat_one, one, two, three = call(
        functools.partial(second_kernel, dims, len(stats)),
        (narrow, block, halo, small, halo),
        (flat, image_one, image_three, weights_first, gain, bias, embed, *stats),
        (padded,),
        conv_flops,
        name="second",
    )
    hidden_one, hidden_three, stats = exchange(one, two, three)
    grad_active = call(
        functools.partial(grad_kernel, dims),
        wide,
        (flat_cot, image_one, image_three, weights_second),
        (padded,),
        conv_flops,
        name="grad",
    )
    slope, factors, matrix = call(
        functools.partial(cross_kernel, dims),
        (wide, shape((2, cells + 2 * cols, channels), BF16), shape((GN_GROUPS, 8 * GN_GROUPS), BF16)),
        (flat, image_one, image_three, stat_one, gain, bias, hidden, weights_first, grouped),
        (
            pltpu.VMEM((6 * channels, cells), BF16),
            pltpu.VMEM((3, 6 * channels, channels), F32),
        ),
        conv_flops,
        name="cross",
    )
    mail = shape((STAT_ROWS + GN_GROUPS, channels), BF16)
    mail_halo = shape((cols + STAT_ROWS + GN_GROUPS, channels), BF16)
    active, grad_norm, stat_two, one, two, three = call(
        functools.partial(third_kernel, dims, len(stats)),
        (shape((cells + 2 * cols, channels), BF16), wide, block, mail_halo, mail, mail_halo),
        (hidden, hidden_one, hidden_three, grad_active, adaptive_bias, weights_first, factors, matrix, *stats),
        (pltpu.VMEM((cells + 4 * cols, channels), BF16),),
        conv_flops,
        name="third",
    )
    grad_one, grad_three, stats = exchange(one, two, three)
    branch, token = call(
        functools.partial(branch_kernel, dims),
        (pltpu.VMEM((cells, channels), BF16), shape((8, 128), F32)),
        (active, weights_second),
        flops=conv_flops,
        name="branch",
    )
    pairs = call(
        functools.partial(pairs_kernel, dims, len(stats)), block, (embed, *stats), name="pairs"
    )
    if fleet == 4:
        pair_list = [pairs, *(swap(pairs, "image", fleet, k) for k in (1, 2, 3))]
    else:
        pair_list = [lax.all_gather(pairs, "image", axis=0, tiled=True)]
    input_grad = call(
        functools.partial(fourth_kernel, dims, len(stats)),
        pltpu.VMEM((cells, channels), BF16),
        (token, grad_norm, grad_one, grad_three, hidden, hidden_one, hidden_three, stat_two, weights_first, flat, stat_one, slope, *stats),
        (padded,),
        conv_flops,
        name="fourth",
    )
    grad_weight, grad_bias = call(
        weight_kernel,
        (shape((channels, 2 * channels), F32), shape((1, 2 * channels), F32)),
        tuple(pair_list),
        name="weight",
    )
    return (
        branch.reshape(images.shape),
        input_grad.reshape(images.shape),
        grad_weight[:width],
        grad_bias[0],
    )


def solution(mesh):
    return jax.shard_map(
        body,
        mesh=mesh,
        in_specs=(
            P(("groups", "image"), "tile", None, None),
            P(("groups", "image"), "tile", None, None),
            P(("groups", "image")),
            P(("groups", "image")),
            P(),
            P(),
            P(),
            P(),
            P(None, "tile"),
            P("tile"),
            P(None, "tile"),
            P("tile", None),
            P(),
        ),
        out_specs=(
            P(("groups", "image"), "tile", None, None),
            P(("groups", "image"), "tile", None, None),
            P(("groups", "tile"), None),
            P("groups"),
        ),
        check_vma=False,
    )
```

```python
import functools
import math

import jax
import jax.numpy as jnp
from jax import lax
from jax.experimental import pallas as pl
from jax.experimental.pallas import tpu as pltpu
from jax.sharding import PartitionSpec as P

GN_GROUPS = 32
EPSILON = 1e-05
VMEM_LIMIT = 12 * 1024 * 1024
F32, BF16 = jnp.float32, jnp.bfloat16

STAT_ROWS = 16


def split(values):
    high = values.astype(BF16).astype(F32)
    rest = values - high
    middle = rest.astype(BF16).astype(F32)
    return high, middle, (rest - middle).astype(BF16).astype(F32)


def terms(values):
    high, middle, low = split(values)
    return jnp.concatenate([high + pltpu.roll(middle, 4, 0), low], axis=0).astype(BF16)


def joined(block):
    wide = block.astype(F32)
    total = wide[0:8] + (pltpu.roll(wide[0:8], 4, 0) + wide[8:16])
    return jnp.where(lax.broadcasted_iota(jnp.int32, total.shape, 0) < 4, total, 0.0)


def rows8(*rows):
    width = rows[0].shape[1]
    index = lax.broadcasted_iota(jnp.int32, (8, width), 0)
    out = jnp.zeros((8, width), F32)
    for place, row in enumerate(rows):
        out = jnp.where(index == place, jnp.broadcast_to(row, (8, width)), out)
    return out


def group_matrix(channels):
    shift = (channels // GN_GROUPS).bit_length() - 1
    row = lax.shift_right_logical(lax.broadcasted_iota(jnp.int32, (channels, channels), 0), shift)
    col = lax.shift_right_logical(lax.broadcasted_iota(jnp.int32, (channels, channels), 1), shift)
    return (row == col).astype(F32).astype(BF16)


def group_sums(rows, groups):
    return joined(jnp.dot(terms(rows), groups, preferred_element_type=F32))


def tree_sum(parts):
    parts = list(parts)
    while len(parts) > 1:
        parts = [
            parts[i] + parts[i + 1] if i + 1 < len(parts) else parts[i]
            for i in range(0, len(parts), 2)
        ]
    return parts[0]


def local_moments(values, groups, count):
    mean = group_sums(rows8(jnp.sum(values, axis=0, keepdims=True)), groups)[0:1] / count
    centred = values - mean
    spread = group_sums(rows8(jnp.sum(centred * centred, axis=0, keepdims=True)), groups)[0:1]
    return mean, spread


def joint_moments(stats, count):
    tiles = len(stats)
    mean = tree_sum([s[0:1] for s in stats]) / tiles
    spread = tree_sum([s[1:2] + count * (s[0:1] - mean) * (s[0:1] - mean) for s in stats])
    return mean, lax.rsqrt(spread / (count * tiles) + EPSILON)


def sigmoid(values):
    return 1.0 / (1.0 + jnp.exp(-values))


def column_index(cells, cols, channels):
    index = lax.broadcasted_iota(jnp.int32, (cells, channels), 0)
    return lax.bitwise_and(index, cols - 1)


def conv(padded_ref, kernel_ref, cells, cols, flipped):
    parts = []
    for j in range(3):
        total = None
        for i in range(3):
            start = (2 - i if flipped else i) * cols
            product = lax.dot_general(
                padded_ref[start : start + cells],
                kernel_ref[3 * i + j],
                (((1,), (1 if flipped else 0,)), ((), ())),
                preferred_element_type=F32,
            )
            total = product if total is None else total + product
        parts.append(total)
    if flipped:
        parts = parts[::-1]
    return parts[1] + (shifted(parts[0], cols, 1) + shifted(parts[2], cols, -1))


def scattered(values, kernel_ref, cols):
    rows = values.shape[0] // cols
    parts = []
    for j in range(3):
        products = [
            lax.dot_general(
                values, kernel_ref[3 * i + j], (((1,), (1,)), ((), ())), preferred_element_type=F32
            )
            for i in range(3)
        ]
        lines = []
        for line in range(rows + 2):
            terms_of = [
                products[i][(line - i) * cols : (line - i + 1) * cols] for i in range(3) if 0 <= line - i < rows
            ]
            lines.append(tree_sum(terms_of))
        parts.append(jnp.concatenate(lines, axis=0))
    return parts[1] + (shifted(parts[2], cols, 1) + shifted(parts[0], cols, -1))


def shifted(values, cols, step):
    cells = values.shape[0]
    column = column_index(cells, cols, values.shape[1])
    if step == 1:
        return jnp.where(column == 0, 0.0, pltpu.roll(values, 1, 0))
    return jnp.where(column == cols - 1, 0.0, pltpu.roll(values, cells - 1, 0))


def stat_list(refs, start, tiles):
    if len(refs) == 1:
        size = refs[0].shape[0] // tiles
        return [joined(refs[0][size * t : size * t + STAT_ROWS]) for t in range(tiles)]
    return [joined(ref[s : s + STAT_ROWS]) for ref, s in zip(refs, start, strict=True)]


def standing(tiles):
    tile = lax.axis_index("tile")
    return tile, lax.bitwise_and(tile, 1) if tiles == 4 else 0 * tile


def edges(place, one, three):
    odd = place[1] == 1
    return jnp.where(odd, one, three), jnp.where(odd, three, one)


def starts(place, cells, cols):
    odd = place[1]
    first = pl.multiple_of((1 - odd) * (cells - cols), cols)
    third = pl.multiple_of(odd * (cells - cols), cols)
    return first, third


def first_kernel(dims, *refs):
    cells, cols, channels, tiles = dims
    count = (len(refs) - 4) // 2
    sources, copies_to = refs[:count], refs[count : 2 * count]
    one, two, three, sems = refs[2 * count :]
    copies = [
        pltpu.make_async_copy(source, target, sems.at[k])
        for k, (source, target) in enumerate(zip(sources, copies_to, strict=True))
    ]
    for copy in copies:
        copy.start()
    images, cotangent = copies_to[:2]
    place = standing(tiles)
    start_one, start_three = starts(place, cells, cols)
    groups = group_matrix(channels)
    copies[0].wait()
    mean, spread = local_moments(
        images[...].astype(F32), groups, cells * (channels // GN_GROUPS)
    )
    one[0:cols] = images[pl.ds(start_one, cols)]
    three[0:cols] = images[pl.ds(start_three, cols)]
    copies[1].wait()
    one[cols : 2 * cols] = cotangent[pl.ds(start_one, cols)]
    three[cols : 2 * cols] = cotangent[pl.ds(start_three, cols)]
    block = terms(rows8(mean, spread))
    one[2 * cols :] = block
    two[...] = block
    three[2 * cols :] = block
    for copy in copies[2:]:
        copy.wait()


def embedding(step, label, table, time_weight, time_bias, adaptive_weight):
    channels = adaptive_weight.shape[1] // 2
    half = time_weight.shape[0] // 2

    def times(vector, weights):
        return joined(jnp.dot(terms(rows8(vector)), weights, preferred_element_type=F32))[0:1]

    place = lax.broadcasted_iota(jnp.int32, (8, half), 1).astype(F32)
    angles = step.astype(F32) * jnp.exp(-math.log(10000.0) * place / half)
    sinusoid = jnp.concatenate([jnp.cos(angles), jnp.sin(angles)], axis=1)[0:1]
    classes = lax.broadcasted_iota(jnp.int32, (16, table.shape[0]), 1)
    onehot = (classes == label).astype(F32).astype(BF16)
    row = jnp.dot(onehot, table[...], preferred_element_type=F32)[0:1]
    hidden = times(sinusoid, time_weight[...]) + time_bias[...]
    embedded = hidden * sigmoid(hidden) + row
    activated = embedded * sigmoid(embedded)
    partial = times(activated, adaptive_weight[...])
    return rows8(partial[:, :channels], partial[:, channels:], activated)


def second_kernel(dims, n_stats, images, one, three, weights, gain, bias, embed, *rest):
    cells, cols, channels, tiles = dims
    place = standing(tiles)
    stat_refs, (hidden, stat, out_one, out_two, out_three, padded) = rest[:n_stats], rest[n_stats:]
    count = cells * (channels // GN_GROUPS)
    mean, inverse = joint_moments(
        stat_list(stat_refs, (0, 2 * cols, 0, 2 * cols), tiles), count
    )
    stat[...] = rows8(mean, inverse)
    above, below = edges(place, one[0:cols], three[0:cols])

    def active(block):
        pre = (block.astype(F32) - mean) * inverse * gain[...] + bias[...]
        return pre * sigmoid(pre)

    padded[0:cols] = jnp.where(place[0] > 0, active(above), 0.0).astype(BF16)
    padded[cols : cols + cells] = active(images[...]).astype(BF16)
    padded[cols + cells :] = jnp.where(place[0] < tiles - 1, active(below), 0.0).astype(BF16)
    rounded = conv(padded, weights, cells, cols, False).astype(BF16)
    hidden[...] = rounded
    mean_two, spread_two = local_moments(rounded.astype(F32), group_matrix(channels), count)
    block = terms(rows8(mean_two, spread_two, embed[0:1], embed[1:2]))
    start_one, start_three = starts(place, cells, cols)
    out_one[0:cols] = hidden[pl.ds(start_one, cols)]
    out_three[0:cols] = hidden[pl.ds(start_three, cols)]
    out_one[cols:] = block
    out_two[...] = block
    out_three[cols:] = block


def identity(size):
    row = lax.broadcasted_iota(jnp.int32, (size, size), 0)
    return (1.0 * (row == lax.broadcasted_iota(jnp.int32, (size, size), 1))).astype(BF16)


def turn_kernel(step, label, table, time_weight, time_bias, mix, source, bias_source, weights, bias, embed, grouped, sems):
    copies = [
        pltpu.make_async_copy(source, weights, sems.at[0]),
        pltpu.make_async_copy(bias_source, bias, sems.at[1]),
    ]
    for copy in copies:
        copy.start()
    embed[...] = embedding(step[0], label[0], table, time_weight, time_bias, mix)
    columns = tiled_columns(weights.shape[1])
    for copy in copies:
        copy.wait()
    for k in range(source.shape[0]):
        grouped[k] = jnp.dot(weights[k], columns, preferred_element_type=F32)


def tiled_columns(channels):
    size = (channels, 4 * GN_GROUPS)
    shift = (channels // GN_GROUPS).bit_length() - 1
    group = lax.shift_right_logical(lax.broadcasted_iota(jnp.int32, size, 0), shift)
    column = lax.bitwise_and(lax.broadcasted_iota(jnp.int32, size, 1), GN_GROUPS - 1)
    return (1.0 * (group == column)).astype(BF16)


def group_columns(channels, offset, length, axis):
    size = (channels, length) if axis else (length, channels)
    shift = (channels // GN_GROUPS).bit_length() - 1
    channel = lax.broadcasted_iota(jnp.int32, size, 1 - axis)
    short = lax.broadcasted_iota(jnp.int32, size, axis)
    hit = lax.shift_right_logical(channel, shift) + offset == short
    return (1.0 * hit).astype(BF16)


def grad_kernel(dims, cotangent, one, three, weights, out, padded):
    cells, cols, channels, tiles = dims
    place = standing(tiles)
    above, below = edges(place, one[cols : 2 * cols], three[cols : 2 * cols])
    padded[0:cols] = jnp.where(place[0] > 0, above, jnp.zeros_like(above))
    padded[cols : cols + cells] = cotangent[...]
    padded[cols + cells :] = jnp.where(place[0] < tiles - 1, below, jnp.zeros_like(below))
    out[...] = conv(padded, weights, cells, cols, True)


def halves(values):
    high = values.astype(BF16)
    return high, (values - high.astype(F32)).astype(BF16)


def cross_kernel(
    dims, images, one, three, stat_one, gain, bias, hidden, weights, grouped, slope, factors, matrix, left, products
):
    cells, cols, channels, tiles = dims
    place = standing(tiles)
    above, below = edges(place, one[0:cols], three[0:cols])

    def pieces(block):
        normed = (block.astype(F32) - stat_one[0:1]) * stat_one[1:2]
        pre = normed * gain[...] + bias[...]
        gate = sigmoid(pre)
        grade = gate * (1.0 + pre * (1.0 - gate)) * gain[...]
        return grade, grade * normed

    own = pieces(images[...])
    slope[...] = own[0]
    for which, (top, bottom) in enumerate(zip(pieces(above), pieces(below), strict=True)):
        factors[which, 0:cols] = jnp.where(place[0] > 0, top, 0.0).astype(BF16)
        factors[which, cols : cols + cells] = own[which].astype(BF16)
        factors[which, cols + cells :] = jnp.where(place[0] < tiles - 1, bottom, 0.0).astype(BF16)
    unit = identity(channels)
    for which in range(2):
        for i in range(3):
            place_at = (3 * which + i) * channels
            left[place_at : place_at + channels] = lax.dot_general(
                unit,
                factors[which, i * cols : i * cols + cells],
                (((1,), (1,)), ((), ())),
                preferred_element_type=F32,
            ).astype(BF16)
    wide = hidden[...].astype(F32)
    lines = (shifted(wide, cols, -1).astype(BF16), hidden[...], shifted(wide, cols, 1).astype(BF16))
    for j, line in enumerate(lines):
        products[j] = jnp.dot(left[...], line, preferred_element_type=F32)
    column = lax.bitwise_and(lax.broadcasted_iota(jnp.int32, (cells, 128), 0), cols - 1)
    which_column = lax.broadcasted_iota(jnp.int32, (cells, 128), 1)
    inside = jnp.where(
        which_column == 0, 1.0 * (column < cols - 1), jnp.where(which_column == 2, 1.0 * (column > 0), 1.0)
    )
    plain_sums = jnp.dot(left[...], inside.astype(BF16), preferred_element_type=F32)
    step = channels // 8
    totals = ([], [])
    for start in range(0, channels, step):
        parts = ([], [])
        for k in range(9):
            matrix_rows = weights[k, start : start + step].astype(F32)
            for which in range(2):
                begin = (3 * which + k // 3) * channels + start
                parts[which].append(products[k % 3, begin : begin + step] * matrix_rows)
        for which in range(2):
            totals[which].append(tree_sum(parts[which]))
    block = lax.shift_right_logical(
        lax.broadcasted_iota(jnp.int32, (channels, 4 * GN_GROUPS), 1), GN_GROUPS.bit_length() - 1
    )
    spread = jnp.zeros((channels, 4 * GN_GROUPS), F32)
    for which in range(2):
        for part in halves(jnp.concatenate(totals[which], axis=0)):
            spread += jnp.dot(
                part, group_columns(channels, which * GN_GROUPS, 4 * GN_GROUPS, 1), preferred_element_type=F32
            )
        plain = tree_sum(
            [
                grouped[k]
                * plain_sums[(3 * which + k // 3) * channels : (3 * which + k // 3 + 1) * channels, k % 3 : k % 3 + 1]
                for k in range(9)
            ]
        )
        spread += jnp.where(block == 2 + which, plain, 0.0)
    summed = jnp.sum(spread.reshape(GN_GROUPS, channels // GN_GROUPS, 4 * GN_GROUPS), axis=1)
    matrix[...] = jnp.concatenate(halves(summed), axis=1)


def third_kernel(
    dims, n_stats, hidden, one, three, grad_active, adaptive_bias, weights, factors, matrix, *rest
):
    cells, cols, channels, tiles = dims
    place = standing(tiles)
    stat_refs, (active, grad_norm, stat, out_one, out_two, out_three) = rest[:n_stats], rest[n_stats:]
    count = cells * (channels // GN_GROUPS)
    stats = stat_list(stat_refs, (0, cols, 0, cols), tiles)
    mean, inverse = joint_moments(stats, count)
    modulation = tree_sum(stats)
    factor = 1.0 + (modulation[2:3] + adaptive_bias[:, :channels])
    shift = modulation[3:4] + adaptive_bias[:, channels:]
    stat[...] = rows8(mean, inverse, factor)
    above, below = edges(place, one[0:cols], three[0:cols])

    def pieces(block):
        normed = (block.astype(F32) - mean) * inverse
        pre = normed * factor + shift
        return normed, pre, sigmoid(pre)

    normed, pre, gate = pieces(hidden[...])
    active[cols : cols + cells] = (pre * gate).astype(BF16)
    grad_pre = grad_active[...] * (gate * (1.0 + pre * (1.0 - gate)))
    grad = grad_pre * factor
    grad_norm[...] = grad
    base = scattered((grad * inverse).astype(BF16), weights, cols)
    _, pre, gate = pieces(above)
    active[0:cols] = jnp.where(place[0] > 0, pre * gate, 0.0).astype(BF16)
    _, pre, gate = pieces(below)
    active[cols + cells :] = jnp.where(place[0] < tiles - 1, pre * gate, 0.0).astype(BF16)
    block = terms(
        rows8(
            jnp.sum(grad_pre * normed, axis=0, keepdims=True),
            jnp.sum(grad_pre, axis=0, keepdims=True),
            jnp.sum(base * factors[0].astype(F32), axis=0, keepdims=True),
            jnp.sum(base * factors[1].astype(F32), axis=0, keepdims=True),
        )
    )
    start_one, start_three = starts(place, cells, cols)
    out_one[0:cols] = grad_norm[pl.ds(start_one, cols)].astype(BF16)
    out_three[0:cols] = grad_norm[pl.ds(start_three, cols)].astype(BF16)
    for out, start in ((out_one, cols), (out_two, 0), (out_three, cols)):
        out[start : start + STAT_ROWS] = block
        out[start + STAT_ROWS :] = matrix[...]


def pairs_kernel(dims, n_stats, embed, *rest):
    cells, cols, channels, tiles = dims
    sums = tree_sum(stat_list(rest[:n_stats], (0, cols, 0, cols), tiles))
    rest[n_stats][...] = rows8(sums[0:1], sums[1:2], embed[2:3])


def branch_kernel(dims, active, weights, out, token):
    cells, cols, channels, tiles = dims
    out[...] = conv(active, weights, cells, cols, False).astype(BF16)
    token[...] = jnp.zeros_like(token)


def fourth_kernel(
    dims, n_stats, token, grad_norm, grad_one, grad_three, hidden, one, three, stat_two, weights, images, stat_one, slope, *rest
):
    cells, cols, channels, tiles = dims
    place = standing(tiles)
    stat_refs, (out, padded) = rest[:n_stats], rest[n_stats:]
    total = cells * (channels // GN_GROUPS) * tiles
    if len(stat_refs) == 1:
        size = stat_refs[0].shape[0] // tiles
        blocks = [stat_refs[0][size * t + STAT_ROWS : size * (t + 1)] for t in range(tiles)]
    else:
        blocks = [ref[ref.shape[0] - GN_GROUPS :] for ref in stat_refs]
    width = 4 * GN_GROUPS
    matrix = tree_sum([b[:, :width].astype(F32) + b[:, width:].astype(F32) for b in blocks])
    sums = tree_sum(stat_list(stat_refs, (0, cols, 0, cols), tiles))
    mean, inverse, factor = stat_two[0:1], stat_two[1:2], stat_two[2:3]
    row = lax.broadcasted_iota(jnp.int32, (8, channels), 0)
    reduced = group_sums(jnp.where(row < 2, sums * factor, sums), group_matrix(channels))
    paired, plain = reduced[0:1] / total, reduced[1:2] / total
    above, below = edges(place, one[0:cols], three[0:cols])
    grad_above, grad_below = edges(place, grad_one[0:cols], grad_three[0:cols])

    def grad_hidden(grad, block):
        normed = (block.astype(F32) - mean) * inverse
        return inverse * (grad.astype(F32) - plain - normed * paired)

    padded[0:cols] = jnp.where(place[0] > 0, grad_hidden(grad_above, above), 0.0).astype(BF16)
    padded[cols : cols + cells] = grad_hidden(grad_norm[...], hidden[...]).astype(BF16)
    padded[cols + cells :] = jnp.where(
        place[0] < tiles - 1, grad_hidden(grad_below, below), 0.0
    ).astype(BF16)
    grad = conv(padded, weights, cells, cols, True) * slope[...]
    beta = paired * inverse * inverse
    alpha = plain * inverse - beta * mean
    per = channels // GN_GROUPS
    picked = joined(
        jnp.dot(terms(rows8(alpha / per, beta / per)), tiled_columns(channels), preferred_element_type=F32)
    )
    block = lax.shift_right_logical(
        lax.broadcasted_iota(jnp.int32, (1, width), 1), GN_GROUPS.bit_length() - 1
    )
    vectors = [
        jnp.where(block == which, picked[1:2], jnp.where(block == 2 + which, picked[0:1], 0.0))
        for which in range(2)
    ]
    found = lax.dot_general(
        rows8(*vectors),
        matrix,
        (((1,), (1,)), ((), ())),
        precision=lax.Precision.HIGHEST,
        preferred_element_type=F32,
    )
    back = joined(
        jnp.dot(terms(found), group_columns(channels, 0, GN_GROUPS, 0), preferred_element_type=F32)
    )
    means = [(reduced[2 + which : 3 + which] - back[which : which + 1]) / total for which in range(2)]
    normed = (images[...].astype(F32) - stat_one[0:1]) * stat_one[1:2]
    out[...] = (stat_one[1:2] * (grad - means[0] - normed * means[1])).astype(BF16)


def weight_kernel(*rest):
    pair_refs, (weight, bias) = rest[:-2], rest[-2:]
    if len(pair_refs) == 1:
        blocks = [pair_refs[0][8 * n : 8 * n + 8] for n in range(pair_refs[0].shape[0] // 8)]
        places = list(range(len(blocks)))
    else:
        blocks = [ref[...] for ref in pair_refs]
        places = [lax.bitwise_xor(lax.axis_index("image"), k) for k in range(len(blocks))]
    count = -(-len(blocks) // 8) * 8
    channels = blocks[0].shape[1]
    row = lax.broadcasted_iota(jnp.int32, (count, channels), 0)

    def ordered(which):
        out = jnp.zeros((count, channels), F32)
        for block, place in zip(blocks, places, strict=True):
            out = jnp.where(row == place, jnp.broadcast_to(block[which : which + 1], out.shape), out)
        return out

    activated = split(ordered(2))
    left = jnp.concatenate([activated[k] for k in (0, 0, 1, 0, 2, 1)], axis=0).astype(BF16)
    for start, which in ((0, 0), (channels, 1)):
        part = ordered(which)
        pieces = split(part)
        right = jnp.concatenate([pieces[k] for k in (0, 1, 0, 2, 0, 1)], axis=0).astype(BF16)
        weight[:, start : start + channels] = lax.dot_general(
            left, right, (((0,), (0,)), ((), ())), preferred_element_type=F32
        )
        bias[:, start : start + channels] = jnp.sum(part, axis=0, keepdims=True)


def call(kernel, out_shapes, operands, scratch=(), flops=1000, name=None, spaces=None):
    size = sum(o.size * o.dtype.itemsize for o in operands)
    return pl.pallas_call(
        kernel,
        out_shape=out_shapes,
        in_specs=[
            pl.BlockSpec(memory_space=(spaces or {}).get(k, pltpu.VMEM)) for k in range(len(operands))
        ],
        out_specs=jax.tree.map(lambda _: pl.BlockSpec(memory_space=pltpu.VMEM), out_shapes),
        scratch_shapes=list(scratch),
        compiler_params=pltpu.CompilerParams(vmem_limit_bytes=VMEM_LIMIT),
        cost_estimate=pl.CostEstimate(flops=flops, bytes_accessed=size, transcendentals=0),
        name=name,
    )(*operands)


def swap(values, axis, size, distance):
    return lax.ppermute(values, axis, [(i, i ^ distance) for i in range(size)])


def exchange(one, two, three):
    tiles = lax.axis_size("tile")
    if tiles == 4:
        got = [swap(part, "tile", tiles, k + 1) for k, part in enumerate((one, two, three))]
        return got[0], got[2], [two, *got]
    ahead = [(i, (i + 1) % tiles) for i in range(tiles)]
    behind = [(target, source) for source, target in ahead]
    below, above = lax.ppermute(three, "tile", behind), lax.ppermute(one, "tile", ahead)
    return below, above, [lax.all_gather(two, "tile", axis=0, tiled=True)]


def body(
    images,
    cotangent,
    timesteps,
    class_ids,
    norm_gain,
    norm_bias,
    conv_first,
    conv_second,
    time_weight,
    time_bias,
    class_table,
    adaptive_weight,
    adaptive_bias,
):
    _, rows, cols, channels = images.shape
    tiles, fleet = lax.axis_size("tile"), lax.axis_size("image")
    cells = rows * cols
    dims = (cells, cols, channels, tiles)
    shape = jax.ShapeDtypeStruct
    conv_flops = 18 * cells * channels * channels
    padded = pltpu.VMEM((cells + 2 * cols, channels), BF16)
    small = shape((STAT_ROWS, channels), BF16)
    halo = shape((cols + STAT_ROWS, channels), BF16)
    halos = shape((2 * cols + STAT_ROWS, channels), BF16)
    block = shape((8, channels), F32)
    wide = shape((cells, channels), F32)
    narrow = shape((cells, channels), BF16)

    width = adaptive_weight.shape[0]
    spare = channels - width
    time_bias, mix = time_bias[None], adaptive_weight
    if spare:
        time_weight, time_bias, class_table = (
            jnp.pad(part, ((0, 0), (0, spare))) for part in (time_weight, time_bias, class_table)
        )
        mix = jnp.pad(mix, ((0, spare), (0, 0)))
    pin = lambda part: pltpu.with_memory_space_constraint(part, pltpu.HBM)
    like = lambda parts: tuple(shape(part.shape, part.dtype) for part in parts)
    loads = (
        images.reshape(cells, channels),
        cotangent.reshape(cells, channels),
        norm_gain[None],
        norm_bias[None],
        class_table,
        time_weight,
        time_bias,
        mix,
    )
    flat, flat_cot, gain, bias, class_table, time_weight, time_bias, mix, one, two, three = call(
        functools.partial(first_kernel, dims),
        (*like(loads), halos, small, halos),
        tuple(pin(part) for part in loads),
        (pltpu.SemaphoreType.DMA((len(loads),)),),
        name="first",
        spaces={k: pl.ANY for k in range(len(loads))},
    )
    image_one, image_three, stats = exchange(one, two, three)
    taps = conv_first.reshape(9, channels, channels)
    weights_second = conv_second.reshape(9, channels, channels)
    weights_first, adaptive_bias, embed, grouped = call(
        turn_kernel,
        (
            shape(taps.shape, BF16),
            shape((1, 2 * channels), F32),
            block,
            shape((9, channels, 4 * GN_GROUPS), F32),
        ),
        (timesteps, class_ids, class_table, time_weight, time_bias, mix, pin(taps), pin(adaptive_bias[None])),
        (pltpu.SemaphoreType.DMA((2,)),),
        flops=conv_flops,
        name="turn",
        spaces={0: pltpu.SMEM, 1: pltpu.SMEM, 6: pl.ANY, 7: pl.ANY},
    )

    hidden, stat_one, one, two, three = call(
        functools.partial(second_kernel, dims, len(stats)),
        (narrow, block, halo, small, halo),
        (flat, image_one, image_three, weights_first, gain, bias, embed, *stats),
        (padded,),
        conv_flops,
        name="second",
    )
    hidden_one, hidden_three, stats = exchange(one, two, three)
    grad_active = call(
        functools.partial(grad_kernel, dims),
        wide,
        (flat_cot, image_one, image_three, weights_second),
        (padded,),
        conv_flops,
        name="grad",
    )
    slope, factors, matrix = call(
        functools.partial(cross_kernel, dims),
        (wide, shape((2, cells + 2 * cols, channels), BF16), shape((GN_GROUPS, 8 * GN_GROUPS), BF16)),
        (flat, image_one, image_three, stat_one, gain, bias, hidden, weights_first, grouped),
        (
            pltpu.VMEM((6 * channels, cells), BF16),
            pltpu.VMEM((3, 6 * channels, channels), F32),
        ),
        conv_flops,
        name="cross",
    )
    mail = shape((STAT_ROWS + GN_GROUPS, channels), BF16)
    mail_halo = shape((cols + STAT_ROWS + GN_GROUPS, channels), BF16)
    active, grad_norm, stat_two, one, two, three = call(
        functools.partial(third_kernel, dims, len(stats)),
        (shape((cells + 2 * cols, channels), BF16), wide, block, mail_halo, mail, mail_halo),
        (hidden, hidden_one, hidden_three, grad_active, adaptive_bias, weights_first, factors, matrix, *stats),
        flops=conv_flops,
        name="third",
    )
    grad_one, grad_three, stats = exchange(one, two, three)
    branch, token = call(
        functools.partial(branch_kernel, dims),
        (pltpu.VMEM((cells, channels), BF16), shape((8, 128), F32)),
        (active, weights_second),
        flops=conv_flops,
        name="branch",
    )
    pairs = call(
        functools.partial(pairs_kernel, dims, len(stats)), block, (embed, *stats), name="pairs"
    )
    if fleet == 4:
        pair_list = [pairs, *(swap(pairs, "image", fleet, k) for k in (1, 2, 3))]
    else:
        pair_list = [lax.all_gather(pairs, "image", axis=0, tiled=True)]
    input_grad = call(
        functools.partial(fourth_kernel, dims, len(stats)),
        pltpu.VMEM((cells, channels), BF16),
        (token, grad_norm, grad_one, grad_three, hidden, hidden_one, hidden_three, stat_two, weights_first, flat, stat_one, slope, *stats),
        (padded,),
        conv_flops,
        name="fourth",
    )
    grad_weight, grad_bias = call(
        weight_kernel,
        (shape((channels, 2 * channels), F32), shape((1, 2 * channels), F32)),
        tuple(pair_list),
        name="weight",
    )
    return (
        branch.reshape(images.shape),
        input_grad.reshape(images.shape),
        grad_weight[:width],
        grad_bias[0],
    )


def solution(mesh):
    return jax.shard_map(
        body,
        mesh=mesh,
        in_specs=(
            P(("groups", "image"), "tile", None, None),
            P(("groups", "image"), "tile", None, None),
            P(("groups", "image")),
            P(("groups", "image")),
            P(),
            P(),
            P(),
            P(),
            P(None, "tile"),
            P("tile"),
            P(None, "tile"),
            P("tile", None),
            P(),
        ),
        out_specs=(
            P(("groups", "image"), "tile", None, None),
            P(("groups", "image"), "tile", None, None),
            P(("groups", "tile"), None),
            P("groups"),
        ),
        check_vma=False,
    )
```
